32 devices in a mesh: row: 4 (over z), col: 8 (over y, x, core).
Axes of the slice: x: 2, y: 2, z: 4, core: 2. Of those that a mesh axis runs over, the one named last changes fastest.
Arguments:
- iterate: bfloat16 [3584, 18432], P('row', 'col'), as said below
Outputs:
- update: bfloat16 [3584, 18432], P('row', 'col')
Inputs may be any that keep to these rules, and one draw needn't show every extreme that they name: An iterate of the orthogonalization, with spectral norm of order one.
All inputs are finite; a program needn't handle non-finite values.
Results may differ from the reference program's by a relative error of at most 0.018.
Values may be sent and summed in bfloat16 or wider, within the bound.
No kernel may reach another device: no remote copies, remote signals or barrier semaphores. Data moves between devices by JAX's collectives and lax.ppermute only.
A program may use at most 64 MiB of HBM per device.

```python
import math
import jax
import jax.numpy as jnp
from jax import lax

M = 3584
N = 18432
N_COL = 8


coherent_rank = 16


def shape_iterate(random_part, row_key, col_key, left_key, right_key, row_top, col_top, strength, growth):
    row_mean = math.sqrt((row_top * row_top - 1.0) / (2.0 * math.log(row_top)))
    col_mean = math.sqrt((col_top * col_top - 1.0) / (2.0 * math.log(col_top)))
    row_scale = jnp.exp(jax.random.uniform(row_key, (M, 1), jnp.float32) * math.log(row_top)) / row_mean
    col_scale = jnp.exp(jax.random.uniform(col_key, (1, N), jnp.float32) * math.log(col_top)) / col_mean
    left_factor = jax.random.normal(left_key, (M, coherent_rank), jnp.float32)
    right_factor = jax.random.normal(right_key, (coherent_rank, N), jnp.float32)
    coherent = jnp.zeros((M, N), jnp.float32)
    for index in range(coherent_rank):
        coherent = coherent + left_factor[:, index:index + 1] * right_factor[index:index + 1, :]
    edge_value = math.sqrt(N) + math.sqrt(M)
    strength_scale = strength * edge_value / math.sqrt(M * N / coherent_rank) / math.sqrt(coherent_rank)
    combined = (row_scale * random_part + strength_scale * coherent) * col_scale
    return (0.95 / (growth * edge_value) * combined).astype(jnp.bfloat16)


def draw_iterate(key, part):
    key = jax.random.fold_in(key, 11)
    noise_key, row_key, col_key, left_key, right_key = jax.random.split(key, 5)
    random_part = jax.random.truncated_normal(noise_key, -4.0, 4.0, (M, N), jnp.float32)
    return shape_iterate(random_part, row_key, col_key, left_key, right_key, 1.5, 4.0, 1.1, 1.35)


def setup_inputs(seed: int = 0) -> dict:
    key_of = jax.random.split(jax.random.key(seed), 2)
    return {
        "iterate": draw_iterate(jax.random.fold_in(key_of[1], 71), 0),
    }


coef_a = 3.4445
coef_b = -4.775
coef_c = 2.0315

def reference(iterate):
    width = N // N_COL
    blocks = iterate.reshape(M, N_COL, width).transpose(1, 0, 2)

    def add_block(total, block):
        term = jnp.dot(block, block.T, preferred_element_type=jnp.float32).astype(jnp.bfloat16)
        term = lax.optimization_barrier(term)
        return (total + term.astype(jnp.float32), None)
    summed, unused = lax.scan(add_block, jnp.zeros((M, M), jnp.float32), blocks)
    gram = summed.astype(jnp.bfloat16)
    squared = jnp.dot(gram, gram, preferred_element_type=jnp.float32)
    factor = (coef_b * gram.astype(jnp.float32) + coef_c * squared).astype(jnp.bfloat16)
    result = coef_a * iterate.astype(jnp.float32) + jnp.dot(factor, iterate, preferred_element_type=jnp.float32)
    return (math.sqrt(N) * result).astype(jnp.bfloat16)
```

```python
import math

import jax
import jax.numpy as jnp
from jax import lax
from jax.sharding import PartitionSpec as P

N = 18432


coef_a = 3.4445
coef_b = -4.775
coef_c = 2.0315


def dot_rows(left, right):
    return lax.dot_general(
        left, right, (((1,), (1,)), ((), ())), preferred_element_type=jnp.float32
    )


def per_device(iterate):
    contract = (((1,), (1,)), ((), ()))
    gathered = lax.all_gather(iterate, "row", axis=0, tiled=True)
    partial_value = lax.dot_general(
        iterate, gathered, contract, preferred_element_type=jnp.float32
    )
    partial_value = partial_value.astype(jnp.bfloat16)
    gram_tile = lax.psum_scatter(partial_value, "col", scatter_dimension=1, tiled=True)
    gram_panel = lax.all_gather(gram_tile, "col", axis=1, tiled=True)
    squared = jnp.dot(
        gram_panel,
        lax.all_gather(gram_tile, "row", axis=0, tiled=True),
        preferred_element_type=jnp.float32,
    )
    factor = (coef_b * gram_tile.astype(jnp.float32) + coef_c * squared).astype(jnp.bfloat16)
    factor_panel = lax.all_gather(factor, "col", axis=1, tiled=True)
    product = jnp.dot(factor_panel, gathered, preferred_element_type=jnp.float32)
    result = coef_a * iterate.astype(jnp.float32) + product
    return (math.sqrt(N) * result).astype(jnp.bfloat16)


def per_device_line(n_col, x):
    rows = x.shape[0]
    z = lax.axis_index("row")
    right, left = [(0, 1), (1, 2), (2, 3)], [(3, 2), (2, 1), (1, 0)]

    def gram_block(one, other):
        return dot_rows(one, other).astype(jnp.bfloat16)

    def scatter(blocks):
        return lax.psum_scatter(jnp.stack(blocks), "col", scatter_dimension=1, tiled=True)

    r1 = lax.ppermute(x, "row", right)
    l1 = lax.ppermute(x, "row", left)
    r2 = lax.ppermute(r1, "row", right[1:])
    l2 = lax.ppermute(l1, "row", left[1:])

    first = scatter([gram_block(x, other) for other in (x, l1, r1)])
    first, r2, l2 = lax.optimization_barrier((first, r2, l2))

    width = x.shape[1] // 3
    pieces = [slice(0, width), slice(width, 2 * width), slice(2 * width, None)]
    r3 = [lax.ppermute(r2[:, piece], "row", right[2:]) for piece in pieces]
    l3 = [lax.ppermute(l2[:, piece], "row", left[2:]) for piece in pieces]

    across = l2 + r2
    inner = jnp.where(z == 1, r1, l1)
    second = scatter([gram_block(x, across), gram_block(inner, across)])
    second, r3[0], l3[0] = lax.optimization_barrier((second, r3[0], l3[0]))
    corner = lax.ppermute(second[1], "row", [(1, 0), (2, 3)])
    tile = jnp.concatenate(
        [
            first[0],
            jnp.where(z == 3, corner, first[1]),
            second[0],
            jnp.where(z == 0, corner, first[2]),
        ],
        axis=1,
    )

    panel = lax.all_gather(tile, "col", axis=0, tiled=True)
    tr1 = lax.ppermute(tile, "row", right)
    tl1 = lax.ppermute(tile, "row", left)
    tr2 = lax.ppermute(tr1, "row", right[1:])
    tl2 = lax.ppermute(tl1, "row", left[1:])
    tr3 = lax.ppermute(tr2, "row", right[2:])
    tl3 = lax.ppermute(tl2, "row", left[2:])
    strips = [tile, tl1 + tr3, tl2 + tr2, tr1 + tl3]
    strips = [jnp.roll(strip, d * rows, axis=1) for d, strip in enumerate(strips)]
    strip = jnp.concatenate(strips, axis=0)
    panel, strip, r3[1], l3[1] = lax.optimization_barrier((panel, strip, r3[1], l3[1]))
    squared = dot_rows(strip, panel)
    factor = (coef_b * strip[:, :rows].astype(jnp.float32) + coef_c * squared).astype(jnp.bfloat16)
    factor = lax.all_gather(factor.reshape(4, -1, rows), "col", axis=1, tiled=True)

    def term(d, block):
        return lax.dot_general(
            factor[d], block, (((0,), (0,)), ((), ())), preferred_element_type=jnp.float32
        )

    r3, l3 = jnp.concatenate(r3, axis=1), jnp.concatenate(l3, axis=1)
    product = term(0, x) + term(2, across) + term(1, l1 + r3) + term(3, r1 + l3)
    result = coef_a * x.astype(jnp.float32) + product
    return (math.sqrt(N) * result).astype(jnp.bfloat16)


def solution(mesh):
    n_row, n_col = mesh.shape["row"], mesh.shape["col"]

    def body(iterate):
        if n_row == 4 and iterate.shape[0] % (16 * n_col) == 0:
            return per_device_line(n_col, iterate)
        return per_device(iterate)

    return jax.shard_map(
        body,
        mesh=mesh,
        in_specs=(P("row", "col"),),
        out_specs=P("row", "col"),
        check_vma=False,
    )
```

```python
import functools
import math

import jax
import jax.numpy as jnp
from jax import lax
from jax.experimental import pallas as pl
from jax.experimental.pallas import tpu as pltpu
from jax.sharding import PartitionSpec as P

N = 18432


coef_a = 3.4445
coef_b = -4.775
coef_c = 2.0315


def dot_rows(left, right):
    return lax.dot_general(
        left, right, (((1,), (1,)), ((), ())), preferred_element_type=jnp.float32
    )


def per_device(iterate):
    contract = (((1,), (1,)), ((), ()))
    gathered = lax.all_gather(iterate, "row", axis=0, tiled=True)
    partial_value = lax.dot_general(
        iterate, gathered, contract, preferred_element_type=jnp.float32
    )
    partial_value = partial_value.astype(jnp.bfloat16)
    gram_tile = lax.psum_scatter(partial_value, "col", scatter_dimension=1, tiled=True)
    gram_panel = lax.all_gather(gram_tile, "col", axis=1, tiled=True)
    squared = jnp.dot(
        gram_panel,
        lax.all_gather(gram_tile, "row", axis=0, tiled=True),
        preferred_element_type=jnp.float32,
    )
    factor = (coef_b * gram_tile.astype(jnp.float32) + coef_c * squared).astype(jnp.bfloat16)
    factor_panel = lax.all_gather(factor, "col", axis=1, tiled=True)
    product = jnp.dot(factor_panel, gathered, preferred_element_type=jnp.float32)
    result = coef_a * iterate.astype(jnp.float32) + product
    return (math.sqrt(N) * result).astype(jnp.bfloat16)


def square_kernel(z_ref, panel, far_panel, own, l1, r3, l2, r2, r1, l3, corner, pair, end, last, out):
    z = z_ref[0]
    part = own.shape[1]
    rows = panel.shape[1]
    at_end = jnp.logical_or(z == 0, z == 3)
    near = jnp.where(at_end, end[...], corner[...])
    far = jnp.where(at_end, last[...], pair[...])
    low = jnp.where(z < 2, near, far)
    high = jnp.where(z < 2, far, near)
    zero = jnp.zeros_like(low)

    def strip(e, block):
        if e == 0:
            value = own[block]
        else:
            one, other = {1: (l1, r3), 2: (l2, r2), 3: (r1, l3)}[e]
            value = one[block] + other[block]
        if block == 3:
            value = value + jnp.where((z + e) % 4 == 0, low, zero)
        if block == 1:
            value = value + jnp.where((z + e) % 4 == 3, high, zero)
        return value

    total = jnp.zeros((rows, 4 * part), jnp.float32)
    for d in range(4):
        right = jnp.concatenate([strip(e, (d - e) % 4) for e in range(4)], axis=0)
        left = panel[d]
        if d == 1:
            left = left + jnp.where(z == 3, far_panel[...], jnp.zeros_like(left))
        if d == 3:
            left = left + jnp.where(z == 0, far_panel[...], jnp.zeros_like(left))
        total = total + dot_rows(left, right)
    index = lax.broadcasted_iota(jnp.int32, (rows, rows), 0)
    other = lax.broadcasted_iota(jnp.int32, (rows, rows), 1)
    unit = jnp.where(index == other, 1.0, 0.0).astype(jnp.bfloat16)
    linear = dot_rows(unit, jnp.concatenate([strip(e, (-e) % 4) for e in range(4)], axis=0))
    out[...] = (coef_b * linear + coef_c * total).astype(out.dtype)


def square(z, panel, *others):
    rows = panel.shape[1]
    part = others[1].shape[1]
    vmem = pl.BlockSpec(memory_space=pltpu.VMEM)
    return pl.pallas_call(
        square_kernel,
        out_shape=jax.ShapeDtypeStruct((rows, 4 * part), jnp.bfloat16),
        in_specs=[pl.BlockSpec(memory_space=pltpu.SMEM)] + [vmem] * (1 + len(others)),
        out_specs=vmem,
        compiler_params=pltpu.CompilerParams(vmem_limit_bytes=48 * 2**20),
        cost_estimate=pl.CostEstimate(
            flops=2 * rows * rows * 4 * 4 * part, bytes_accessed=2 * 5 * rows * rows, transcendentals=0
        ),
    )(z.reshape(1).astype(jnp.int32), panel, *others)


def product_kernel(starts, f, x, *rest):
    n_piece = len(starts) - 1
    groups = [rest[g * n_piece : (g + 1) * n_piece] for g in range(6)]
    l1, r3, l2, r2, r1, l3 = groups
    out, wide = rest[6 * n_piece :]
    n_col, part, width = x.shape
    step = pl.program_id(0)
    wide[:, :part, :] = x[...]
    for p in range(n_piece):

        @pl.when(jnp.logical_and(step >= starts[p], step < starts[p + 1]))
        def _(p=p):
            wide[:, part : 2 * part, :] = l1[p][...] + r3[p][...]
            wide[:, 2 * part : 3 * part, :] = l2[p][...] + r2[p][...]
            wide[:, 3 * part :, :] = r1[p][...] + l3[p][...]

    total = coef_a * x[...].reshape(n_col * part, width).astype(jnp.float32)
    for c in range(n_col):
        total = total + jnp.dot(f[c], wide[c], preferred_element_type=jnp.float32)
    out[...] = (math.sqrt(N) * total).astype(out.dtype)


def product(f, x, groups, tile):
    n_col, rows, depth = f.shape
    part = rows // n_col
    columns = x.shape[1]

    def split(value):
        return value.reshape(n_col, part, value.shape[1])

    starts = [0]
    for piece in groups[0]:
        starts.append(starts[-1] + piece.shape[1] // tile)

    def piece_spec(p):
        first, count = starts[p], starts[p + 1] - starts[p]
        return pl.BlockSpec((n_col, part, tile), lambda i: (0, 0, jnp.clip(i - first, 0, count - 1)))

    pieces = [piece_spec(p) for p in range(len(groups[0]))]
    return pl.pallas_call(
        functools.partial(product_kernel, tuple(starts)),
        grid=(columns // tile,),
        out_shape=jax.ShapeDtypeStruct((rows, columns), jnp.bfloat16),
        in_specs=[
            pl.BlockSpec((n_col, rows, depth), lambda i: (0, 0, 0), pipeline_mode=pl.Buffered(1)),
            pl.BlockSpec((n_col, part, tile), lambda i: (0, 0, i)),
        ]
        + pieces * 6,
        out_specs=pl.BlockSpec((rows, tile), lambda i: (0, i)),
        scratch_shapes=[pltpu.VMEM((n_col, depth, tile), jnp.bfloat16)],
        compiler_params=pltpu.CompilerParams(vmem_limit_bytes=56 * 2**20),
        cost_estimate=pl.CostEstimate(
            flops=2 * rows * n_col * depth * columns, bytes_accessed=2 * 12 * rows * columns, transcendentals=0
        ),
    )(f, *(split(value) for value in (x, *(piece for group in groups for piece in group))))


def sum_scatter(value, n_col):
    c = lax.axis_index("col")
    value = value.reshape(n_col, value.shape[0] // n_col, value.shape[1])
    bit = 1
    while bit < n_col:
        here = (c // bit) % 2
        value = value.reshape(-1, 2, *value.shape[1:])
        keep = lax.dynamic_index_in_dim(value, here, axis=1, keepdims=False)
        send = lax.dynamic_index_in_dim(value, 1 - here, axis=1, keepdims=False)
        other = lax.ppermute(send, "col", [(i, i ^ bit) for i in range(n_col)])
        value = (keep.astype(jnp.float32) + other.astype(jnp.float32)).astype(jnp.bfloat16)
        bit *= 2
    return value[0]


def per_device_line(n_col, x):
    z = lax.axis_index("row")
    right, left = [(0, 1), (1, 2), (2, 3)], [(3, 2), (2, 1), (1, 0)]
    unit = 256
    marks = [0, x.shape[1] - 2 * unit, x.shape[1]]

    def send(pieces, pairs):
        return [lax.ppermute(piece, "row", pairs) for piece in pieces]

    def gram_block(one, other):
        total = sum(dot_rows(a, b) for a, b in zip(one, other))
        return total.astype(jnp.bfloat16)

    def scatter(blocks):
        return lax.psum_scatter(jnp.stack(blocks), "col", scatter_dimension=1, tiled=True)

    xs = [x[:, a:b] for a, b in zip(marks, marks[1:])]
    r1, l1 = send(xs, right), send(xs, left)
    r2, l2 = send(r1, right[1:]), send(l1, left[1:])
    r1, l1 = list(r1), list(l1)

    own = scatter([gram_block(xs, xs)])
    own, r1[1], l1[1] = lax.optimization_barrier((own, r1[1], l1[1]))
    first = scatter([gram_block(xs, l1), gram_block(xs, r1), gram_block(r1, l1), gram_block(l1, r1)])
    second = lax.ppermute(first[2], "row", left[1:]) + lax.ppermute(first[3], "row", right[1:])
    tile = jnp.stack([own[0], first[0], second, first[1]])
    tile, r2, l2 = lax.optimization_barrier((tile, r2, l2))
    panel = lax.all_gather(tile, "col", axis=1, tiled=True)
    r3, l3 = send(r2, right[2:]), send(l2, left[2:])

    corner = gram_block(
        [jnp.where(z == 1, a, b) for a, b in zip(r1, l1)], [a + b for a, b in zip(l2, r2)]
    )

    tr1 = lax.ppermute(tile, "row", right)
    tl1 = lax.ppermute(tile, "row", left)
    tr2 = lax.ppermute(tr1, "row", right[1:])
    tl2 = lax.ppermute(tl1, "row", left[1:])
    tr3 = lax.ppermute(tr2, "row", right[2:])
    tl3 = lax.ppermute(tl2, "row", left[2:])

    corner, tr1, tl1 = lax.optimization_barrier((corner, tr1, tl1))
    corner = sum_scatter(corner, n_col)
    end = lax.ppermute(corner, "row", [(1, 0), (2, 3)])
    pair = lax.ppermute(corner, "row", [(1, 2), (2, 1)])
    last = lax.ppermute(pair, "row", [(1, 0), (2, 3)])
    panel, end = lax.optimization_barrier((panel, end))
    far_panel = lax.all_gather(end, "col", axis=0, tiled=True)
    far_panel, r3[0], l3[0] = lax.optimization_barrier((far_panel, r3[0], l3[0]))

    factor = square(z, panel, far_panel, tile, tl1, tr3, tl2, tr2, tr1, tl3, corner, pair, end, last)
    factor = lax.all_gather(factor, "col", axis=0, tiled=False)
    return product(factor, x, [l1, r3, l2, r2, r1, l3], unit)


def solution(mesh):
    n_row, n_col = mesh.shape["row"], mesh.shape["col"]

    def body(iterate):
        if (n_row, n_col) == (4, 8) and iterate.shape == (896, 2304):
            return per_device_line(n_col, iterate)
        return per_device(iterate)

    return jax.shard_map(
        body,
        mesh=mesh,
        in_specs=(P("row", "col"),),
        out_specs=P("row", "col"),
        check_vma=False,
    )
```

```python
import functools
import math

import jax
import jax.numpy as jnp
from jax import lax
from jax.experimental import pallas as pl
from jax.experimental.pallas import tpu as pltpu
from jax.sharding import PartitionSpec as P

N = 18432


coef_a = 3.4445
coef_b = -4.775
coef_c = 2.0315


def dot_rows(left, right):
    return lax.dot_general(
        left, right, (((1,), (1,)), ((), ())), preferred_element_type=jnp.float32
    )


def per_device(iterate):
    contract = (((1,), (1,)), ((), ()))
    gathered = lax.all_gather(iterate, "row", axis=0, tiled=True)
    partial_value = lax.dot_general(
        iterate, gathered, contract, preferred_element_type=jnp.float32
    )
    partial_value = partial_value.astype(jnp.bfloat16)
    gram_tile = lax.psum_scatter(partial_value, "col", scatter_dimension=1, tiled=True)
    gram_panel = lax.all_gather(gram_tile, "col", axis=1, tiled=True)
    squared = jnp.dot(
        gram_panel,
        lax.all_gather(gram_tile, "row", axis=0, tiled=True),
        preferred_element_type=jnp.float32,
    )
    factor = (coef_b * gram_tile.astype(jnp.float32) + coef_c * squared).astype(jnp.bfloat16)
    factor_panel = lax.all_gather(factor, "col", axis=1, tiled=True)
    product = jnp.dot(factor_panel, gathered, preferred_element_type=jnp.float32)
    result = coef_a * iterate.astype(jnp.float32) + product
    return (math.sqrt(N) * result).astype(jnp.bfloat16)


def square_kernel(z_ref, panel, far_panel, own, l1, r3, l2, r2, r1, l3, corner, pair, end, last, out):
    z = z_ref[0]
    part = own.shape[1]
    rows = panel.shape[1]
    at_end = jnp.logical_or(z == 0, z == 3)
    near = jnp.where(at_end, end[...], corner[...])
    far = jnp.where(at_end, last[...], pair[...])
    low = jnp.where(z < 2, near, far)
    high = jnp.where(z < 2, far, near)
    zero = jnp.zeros_like(low)

    def strip(e, block):
        if e == 0:
            value = own[block]
        else:
            one, other = {1: (l1, r3), 2: (l2, r2), 3: (r1, l3)}[e]
            value = one[block] + other[block]
        if block == 3:
            value = value + jnp.where((z + e) % 4 == 0, low, zero)
        if block == 1:
            value = value + jnp.where((z + e) % 4 == 3, high, zero)
        return value

    total = jnp.zeros((rows, 4 * part), jnp.float32)
    for d in range(4):
        right = jnp.concatenate([strip(e, (d - e) % 4) for e in range(4)], axis=0)
        left = panel[d]
        if d == 1:
            left = left + jnp.where(z == 3, far_panel[...], jnp.zeros_like(left))
        if d == 3:
            left = left + jnp.where(z == 0, far_panel[...], jnp.zeros_like(left))
        total = total + dot_rows(left, right)
    index = lax.broadcasted_iota(jnp.int32, (rows, rows), 0)
    other = lax.broadcasted_iota(jnp.int32, (rows, rows), 1)
    unit = jnp.where(index == other, 1.0, 0.0).astype(jnp.bfloat16)
    linear = dot_rows(unit, jnp.concatenate([strip(e, (-e) % 4) for e in range(4)], axis=0))
    out[...] = (coef_b * linear + coef_c * total).astype(out.dtype)


def square(z, panel, *others):
    rows = panel.shape[1]
    part = others[1].shape[1]
    vmem = pl.BlockSpec(memory_space=pltpu.VMEM)
    return pl.pallas_call(
        square_kernel,
        out_shape=jax.ShapeDtypeStruct((rows, 4 * part), jnp.bfloat16),
        in_specs=[pl.BlockSpec(memory_space=pltpu.SMEM)] + [vmem] * (1 + len(others)),
        out_specs=vmem,
        compiler_params=pltpu.CompilerParams(vmem_limit_bytes=48 * 2**20),
        cost_estimate=pl.CostEstimate(
            flops=2 * rows * rows * 4 * 4 * part, bytes_accessed=2 * 5 * rows * rows, transcendentals=0
        ),
    )(z.reshape(1).astype(jnp.int32), panel, *others)


def product_kernel(starts, f, x, l1, l2, r2, r1, *rest):
    n_piece = len(starts) - 1
    r3, l3 = rest[:n_piece], rest[n_piece : 2 * n_piece]
    out, wide = rest[-2:]
    n_col, part, width = x.shape
    step = pl.program_id(0)
    wide[:, :part, :] = x[...]
    wide[:, 2 * part : 3 * part, :] = l2[...] + r2[...]
    for p in range(n_piece):

        @pl.when(jnp.logical_and(step >= starts[p], step < starts[p + 1]))
        def _(p=p):
            wide[:, part : 2 * part, :] = l1[...] + r3[p][...]
            wide[:, 3 * part :, :] = r1[...] + l3[p][...]

    total = coef_a * x[...].reshape(n_col * part, width).astype(jnp.float32)
    for c in range(n_col):
        total = total + jnp.dot(f[c], wide[c], preferred_element_type=jnp.float32)
    out[...] = (math.sqrt(N) * total).astype(out.dtype)


def product(f, x, l1, l2, r2, r1, r3, l3, tile, first, before):
    n_col, rows, depth = f.shape
    part = rows // n_col
    columns = x.shape[1]

    def split(value):
        return value.reshape(n_col, part, value.shape[1])

    starts = [0]
    for piece in r3:
        starts.append(starts[-1] + piece.shape[1] // tile)

    def piece_spec(p):
        begin, count = starts[p], starts[p + 1] - starts[p]
        return pl.BlockSpec((n_col, part, tile), lambda i: (0, 0, jnp.clip(i - begin, 0, count - 1)))

    plain = pl.BlockSpec((n_col, part, tile), lambda i: (0, 0, i + first))
    pieces = [piece_spec(p) for p in range(len(r3))]
    operands = [f, *(split(value) for value in (x, l1, l2, r2, r1, *r3, *l3))]
    in_specs = [
        pl.BlockSpec((n_col, rows, depth), lambda i: (0, 0, 0), pipeline_mode=pl.Buffered(1))
    ]
    in_specs += [plain] * 5 + pieces * 2
    aliases = {}
    if before is not None:
        aliases = {len(operands): 0}
        operands.append(before)
        in_specs.append(pl.BlockSpec(memory_space=pl.ANY))
    share = tile * starts[-1]
    return pl.pallas_call(
        functools.partial(product_kernel, tuple(starts)),
        grid=(starts[-1],),
        out_shape=jax.ShapeDtypeStruct((rows, columns), jnp.bfloat16),
        in_specs=in_specs,
        out_specs=pl.BlockSpec((rows, tile), lambda i: (0, i + first)),
        scratch_shapes=[pltpu.VMEM((n_col, depth, tile), jnp.bfloat16)],
        input_output_aliases=aliases,
        compiler_params=pltpu.CompilerParams(vmem_limit_bytes=56 * 2**20),
        cost_estimate=pl.CostEstimate(
            flops=2 * rows * n_col * depth * share, bytes_accessed=2 * 12 * rows * share, transcendentals=0
        ),
    )(*operands)


def sum_scatter(value, n_col, fence):
    c = lax.axis_index("col")
    value = value.reshape(n_col, value.shape[0] // n_col, value.shape[1])
    bit = 1
    while bit < n_col:
        if 2 * bit == n_col:
            value, *fence = lax.optimization_barrier((value, *fence))
        here = (c // bit) % 2
        value = value.reshape(-1, 2, *value.shape[1:])
        keep = lax.dynamic_index_in_dim(value, here, axis=1, keepdims=False)
        send = lax.dynamic_index_in_dim(value, 1 - here, axis=1, keepdims=False)
        other = lax.ppermute(send, "col", [(i, i ^ bit) for i in range(n_col)])
        value = (keep.astype(jnp.float32) + other.astype(jnp.float32)).astype(jnp.bfloat16)
        bit *= 2
    return value[0], fence


def per_device_line(n_col, x):
    z = lax.axis_index("row")
    right, left = [(0, 1), (1, 2), (2, 3)], [(3, 2), (2, 1), (1, 0)]

    def gram_block(one, other):
        return dot_rows(one, other).astype(jnp.bfloat16)

    def scatter(blocks):
        return lax.psum_scatter(jnp.stack(blocks), "col", scatter_dimension=1, tiled=True)

    r1 = lax.ppermute(x, "row", right)
    l1 = lax.ppermute(x, "row", left)
    r2 = lax.ppermute(r1, "row", right[1:])
    l2 = lax.ppermute(l1, "row", left[1:])

    own = scatter([gram_block(x, x)])
    own, near_r, near_l = lax.optimization_barrier((own, r1, l1))
    first = scatter(
        [
            gram_block(x, near_l),
            gram_block(x, near_r),
            gram_block(near_r, near_l),
            gram_block(near_l, near_r),
        ]
    )
    second = lax.ppermute(first[2], "row", left[1:]) + lax.ppermute(first[3], "row", right[1:])
    tile = jnp.stack([own[0], first[0], second, first[1]])

    corner = gram_block(jnp.where(z == 1, r1, l1), l2 + r2)
    corner, tile = lax.optimization_barrier((corner, tile))

    panel = lax.all_gather(tile, "col", axis=1, tiled=True)
    tr1 = lax.ppermute(tile, "row", right)
    tl1 = lax.ppermute(tile, "row", left)
    corner, (tr1, tl1) = sum_scatter(corner, n_col, [tr1, tl1])
    tr2 = lax.ppermute(tr1, "row", right[1:])
    tl2 = lax.ppermute(tl1, "row", left[1:])
    end = lax.ppermute(corner, "row", [(1, 0), (2, 3)])
    pair = lax.ppermute(corner, "row", [(1, 2), (2, 1)])
    end, pair, tr2, tl2, last_r, last_l = lax.optimization_barrier((end, pair, tr2, tl2, r2, l2))
    last = lax.ppermute(pair, "row", [(1, 0), (2, 3)])
    tr3 = lax.ppermute(tr2, "row", right[2:])
    tl3 = lax.ppermute(tl2, "row", left[2:])
    end, panel = lax.optimization_barrier((end, panel))
    far_panel = lax.all_gather(end, "col", axis=0, tiled=True)

    unit = 256
    marks = [0, 2 * unit, 5 * unit, x.shape[1]]
    pieces = [slice(a, b) for a, b in zip(marks, marks[1:])]
    r3 = [lax.ppermute(last_r[:, piece], "row", right[2:]) for piece in pieces]
    l3 = [lax.ppermute(last_l[:, piece], "row", left[2:]) for piece in pieces]
    far_panel, r3[0], l3[0] = lax.optimization_barrier((far_panel, r3[0], l3[0]))

    factor = square(z, panel, far_panel, tile, tl1, tr3, tl2, tr2, tr1, tl3, corner, pair, end, last)
    factor = lax.all_gather(factor, "col", axis=0, tiled=False)
    out = product(factor, x, l1, l2, r2, r1, r3[:2], l3[:2], unit, 0, None)
    return product(factor, x, l1, l2, r2, r1, r3[2:], l3[2:], unit, marks[2] // unit, out)


def solution(mesh):
    n_row, n_col = mesh.shape["row"], mesh.shape["col"]

    def body(iterate):
        if (n_row, n_col) == (4, 8) and iterate.shape == (896, 2304):
            return per_device_line(n_col, iterate)
        return per_device(iterate)

    return jax.shard_map(
        body,
        mesh=mesh,
        in_specs=(P("row", "col"),),
        out_specs=P("row", "col"),
        check_vma=False,
    )
```

```python
import functools
import math

import jax
import jax.numpy as jnp
from jax import lax
from jax.experimental import pallas as pl
from jax.experimental.pallas import tpu as pltpu
from jax.sharding import PartitionSpec as P

N = 18432


coef_a = 3.4445
coef_b = -4.775
coef_c = 2.0315


def dot_rows(left, right):
    return lax.dot_general(
        left, right, (((1,), (1,)), ((), ())), preferred_element_type=jnp.float32
    )


def per_device(iterate):
    contract = (((1,), (1,)), ((), ()))
    gathered = lax.all_gather(iterate, "row", axis=0, tiled=True)
    partial_value = lax.dot_general(
        iterate, gathered, contract, preferred_element_type=jnp.float32
    )
    partial_value = partial_value.astype(jnp.bfloat16)
    gram_tile = lax.psum_scatter(partial_value, "col", scatter_dimension=1, tiled=True)
    gram_panel = lax.all_gather(gram_tile, "col", axis=1, tiled=True)
    squared = jnp.dot(
        gram_panel,
        lax.all_gather(gram_tile, "row", axis=0, tiled=True),
        preferred_element_type=jnp.float32,
    )
    factor = (coef_b * gram_tile.astype(jnp.float32) + coef_c * squared).astype(jnp.bfloat16)
    factor_panel = lax.all_gather(factor, "col", axis=1, tiled=True)
    product = jnp.dot(factor_panel, gathered, preferred_element_type=jnp.float32)
    result = coef_a * iterate.astype(jnp.float32) + product
    return (math.sqrt(N) * result).astype(jnp.bfloat16)


def whole():
    return pl.BlockSpec(memory_space=pltpu.VMEM)


def scalars():
    return pl.BlockSpec(memory_space=pltpu.SMEM)


def store_rows(out, block, left, right):
    half = right.shape[0] // 2
    for part in (slice(0, half), slice(half, 2 * half)):
        out[block, :, part] = dot_rows(left[...], right[part, :]).astype(out.dtype)


def near_kernel(x, l1, r1, out):
    store_rows(out, 0, x, l1)
    store_rows(out, 1, x, r1)
    store_rows(out, 2, r1, l1)
    store_rows(out, 3, l1, r1)


def corner_kernel(place, l1, r1, early, out):
    on_one = jnp.logical_and(place[0] == 1, place[1] == 0)
    on_two = jnp.logical_and(place[0] == 2, place[1] == 1)

    @pl.when(on_one)
    def _():
        store_rows(out, 0, r1, early)
        store_rows(out, 1, early, r1)

    @pl.when(on_two)
    def _():
        store_rows(out, 0, early, l1)
        store_rows(out, 1, l1, early)

    @pl.when(jnp.logical_not(jnp.logical_or(on_one, on_two)))
    def _():
        out[...] = jnp.zeros_like(out)


def gram_call(kernel, count, operands, scalar):
    rows, depth = operands[0].shape
    first = [] if scalar is None else [scalar]
    return pl.pallas_call(
        kernel,
        out_shape=jax.ShapeDtypeStruct((count, rows, rows), jnp.bfloat16),
        in_specs=[scalars()] * len(first) + [whole()] * len(operands),
        out_specs=whole(),
        compiler_params=pltpu.CompilerParams(vmem_limit_bytes=48 * 2**20),
        cost_estimate=pl.CostEstimate(
            flops=2 * count * rows * rows * depth, bytes_accessed=6 * rows * depth, transcendentals=0
        ),
    )(*first, *operands)


def square_kernel(place, panel, own, l1, r3, l2, r2, r1, l3, corner, out):
    z = place[0]
    part = own.shape[1]
    rows = panel.shape[1]
    low, high = corner[0], corner[1]
    zero = jnp.zeros_like(low)

    def strip(e, block):
        if e == 0:
            value = own[block]
        else:
            one, other = {1: (l1, r3), 2: (l2, r2), 3: (r1, l3)}[e]
            value = one[block] + other[block]
        if block == 3:
            value = value + jnp.where((z + e) % 4 == 0, low, zero)
        if block == 1:
            value = value + jnp.where((z + e) % 4 == 3, high, zero)
        return value

    total = jnp.zeros((rows, 4 * part), jnp.float32)
    for d in range(4):
        right = jnp.concatenate([strip(e, (d - e) % 4) for e in range(4)], axis=0)
        total = total + dot_rows(panel[d], right)
    index = lax.broadcasted_iota(jnp.int32, (rows, rows), 0)
    other = lax.broadcasted_iota(jnp.int32, (rows, rows), 1)
    unit = jnp.where(index == other, 1.0, 0.0).astype(jnp.bfloat16)
    linear = dot_rows(unit, jnp.concatenate([strip(e, (-e) % 4) for e in range(4)], axis=0))
    out[...] = (coef_b * linear + coef_c * total).astype(out.dtype)


def square(place, panel, *others):
    rows = panel.shape[1]
    part = others[0].shape[1]
    return pl.pallas_call(
        square_kernel,
        out_shape=jax.ShapeDtypeStruct((rows, 4 * part), jnp.bfloat16),
        in_specs=[scalars()] + [whole()] * (1 + len(others)),
        out_specs=whole(),
        compiler_params=pltpu.CompilerParams(vmem_limit_bytes=48 * 2**20),
        cost_estimate=pl.CostEstimate(
            flops=2 * rows * rows * 4 * 4 * part, bytes_accessed=2 * 5 * rows * rows, transcendentals=0
        ),
    )(place, panel, *others)


def product_kernel(starts, place, f, x, l1, r1, early, late, *rest):
    n_piece = len(starts) - 1
    far = [rest[p : 2 * n_piece : n_piece] for p in range(n_piece)]
    out, wide = rest[-2:]
    n_col, part, width = x.shape
    step = pl.program_id(0)
    wide[:, :part, :] = x[...]
    wide[:, 2 * part : 3 * part, :] = early[...] + late[...]
    for p in range(n_piece):

        @pl.when(jnp.logical_and(step >= starts[p], step < starts[p + 1]))
        def _(p=p):
            value = far[p][0][...] + far[p][1][...]
            zero = jnp.zeros_like(value)
            wide[:, part : 2 * part, :] = l1[...] + jnp.where(place[0] == 3, value, zero)
            wide[:, 3 * part :, :] = r1[...] + jnp.where(place[0] == 0, value, zero)

    total = coef_a * x[...].reshape(n_col * part, width).astype(jnp.float32)
    for c in range(n_col):
        total = total + jnp.dot(f[c], wide[c], preferred_element_type=jnp.float32)
    out[...] = (math.sqrt(N) * total).astype(out.dtype)


def product(place, f, near, far, tile, first, before):
    n_col, rows, depth = f.shape
    part = rows // n_col
    columns = near[0].shape[1]

    def split(value):
        return value.reshape(n_col, part, value.shape[1])

    starts = [0]
    for piece in far[0]:
        starts.append(starts[-1] + piece.shape[1] // tile)

    def piece_spec(p):
        begin, count = starts[p], starts[p + 1] - starts[p]
        return pl.BlockSpec((n_col, part, tile), lambda i: (0, 0, jnp.clip(i - begin, 0, count - 1)))

    plain = pl.BlockSpec((n_col, part, tile), lambda i: (0, 0, i + first))
    pieces = [piece_spec(p) for p in range(len(far[0]))]
    operands = [place, f, *(split(value) for value in (*near, *far[0], *far[1]))]
    in_specs = [
        scalars(),
        pl.BlockSpec((n_col, rows, depth), lambda i: (0, 0, 0), pipeline_mode=pl.Buffered(1)),
    ]
    in_specs += [plain] * len(near) + pieces * 2
    aliases = {}
    if before is not None:
        aliases = {len(operands): 0}
        operands.append(before)
        in_specs.append(pl.BlockSpec(memory_space=pl.ANY))
    share = tile * starts[-1]
    return pl.pallas_call(
        functools.partial(product_kernel, tuple(starts)),
        grid=(starts[-1],),
        out_shape=jax.ShapeDtypeStruct((rows, columns), jnp.bfloat16),
        in_specs=in_specs,
        out_specs=pl.BlockSpec((rows, tile), lambda i: (0, i + first)),
        scratch_shapes=[pltpu.VMEM((n_col, depth, tile), jnp.bfloat16)],
        input_output_aliases=aliases,
        compiler_params=pltpu.CompilerParams(vmem_limit_bytes=56 * 2**20),
        cost_estimate=pl.CostEstimate(
            flops=2 * rows * n_col * depth * share, bytes_accessed=2 * 12 * rows * share, transcendentals=0
        ),
    )(*operands)


def per_device_line(n_col, x):
    z, c = lax.axis_index("row"), lax.axis_index("col")
    place = jnp.stack([z, c % 2]).astype(jnp.int32)
    right, left = [(0, 1), (1, 2), (2, 3)], [(3, 2), (2, 1), (1, 0)]

    def send(value, pairs):
        return lax.ppermute(value, "row", pairs)

    def send_cores(value, even, odd):
        pairs = [
            (a * n_col + i, b * n_col + i)
            for i in range(n_col)
            for a, b in (odd if i % 2 else even)
        ]
        return lax.ppermute(value, ("row", "col"), pairs)

    def scatter(blocks):
        return lax.psum_scatter(blocks, "col", scatter_dimension=1, tiled=True)

    r1 = send(x, right)
    l1 = send(x, left)
    early = send_cores(jnp.where(c % 2 == 0, l1, r1), left[1:], right[1:])
    late = send_cores(jnp.where(c % 2 == 0, r1, l1), right[1:], left[1:])

    own = scatter(dot_rows(x, x).astype(jnp.bfloat16)[None])
    own, near_l, near_r = lax.optimization_barrier((own, l1, r1))
    blocks = gram_call(near_kernel, 4, [x, near_l, near_r], None)
    first = scatter(blocks)
    blocks, early_now = lax.optimization_barrier((blocks, early))
    corner = gram_call(corner_kernel, 2, [l1, r1, early_now], place)
    corner, first = lax.optimization_barrier((corner, first))
    corner = scatter(corner)

    first, late = lax.optimization_barrier((first, late))
    second = send(first[2], left[1:]) + send(first[3], right[1:])
    tile = jnp.stack([own[0], first[0], second, first[1]])
    tr1, tl1 = send(tile, right), send(tile, left)

    corner, tr1, tl1 = lax.optimization_barrier((corner, tr1, tl1))
    corner = corner + send(corner, [(1, 2), (2, 1)])
    corner = corner + send(corner, [(1, 0), (2, 3)])
    zero = jnp.zeros_like(corner[0])
    added = jnp.stack(
        [zero, jnp.where(z == 3, corner[1], zero), zero, jnp.where(z == 0, corner[0], zero)]
    )
    panel = lax.all_gather(tile + added, "col", axis=1, tiled=True)

    tr2, tl2 = send(tr1, right[1:]), send(tl1, left[1:])
    tr3, tl3 = send(tr2, right[2:]), send(tl2, left[2:])
    unit = 256
    marks = [0, 2 * unit, 5 * unit, x.shape[1]]
    pieces = [slice(a, b) for a, b in zip(marks, marks[1:])]
    tr3, tl3, early_on, late_on = lax.optimization_barrier((tr3, tl3, early, late))
    far = [
        [send_cores(early_on[:, piece], left[2:], right[2:]) for piece in pieces],
        [send_cores(late_on[:, piece], right[2:], left[2:]) for piece in pieces],
    ]
    panel, far[0][0], far[1][0] = lax.optimization_barrier((panel, far[0][0], far[1][0]))

    factor = square(place, panel, tile, tl1, tr3, tl2, tr2, tr1, tl3, corner)
    factor = lax.all_gather(factor, "col", axis=0, tiled=False)
    near = [x, l1, r1, early, late]
    out = product(place, factor, near, [part[:2] for part in far], unit, 0, None)
    return product(place, factor, near, [part[2:] for part in far], unit, marks[2] // unit, out)


def solution(mesh):
    n_row, n_col = mesh.shape["row"], mesh.shape["col"]

    def body(iterate):
        if (n_row, n_col) == (4, 8) and iterate.shape == (896, 2304):
            return per_device_line(n_col, iterate)
        return per_device(iterate)

    return jax.shard_map(
        body,
        mesh=mesh,
        in_specs=(P("row", "col"),),
        out_specs=P("row", "col"),
        check_vma=False,
    )
```

```python
import functools
import math

import jax
import jax.numpy as jnp
from jax import lax
from jax.experimental import pallas as pl
from jax.experimental.pallas import tpu as pltpu
from jax.sharding import PartitionSpec as P

N = 18432


coef_a = 3.4445
coef_b = -4.775
coef_c = 2.0315


def dot_rows(left, right):
    return lax.dot_general(
        left, right, (((1,), (1,)), ((), ())), preferred_element_type=jnp.float32
    )


def per_device(iterate):
    contract = (((1,), (1,)), ((), ()))
    gathered = lax.all_gather(iterate, "row", axis=0, tiled=True)
    partial_value = lax.dot_general(
        iterate, gathered, contract, preferred_element_type=jnp.float32
    )
    partial_value = partial_value.astype(jnp.bfloat16)
    gram_tile = lax.psum_scatter(partial_value, "col", scatter_dimension=1, tiled=True)
    gram_panel = lax.all_gather(gram_tile, "col", axis=1, tiled=True)
    squared = jnp.dot(
        gram_panel,
        lax.all_gather(gram_tile, "row", axis=0, tiled=True),
        preferred_element_type=jnp.float32,
    )
    factor = (coef_b * gram_tile.astype(jnp.float32) + coef_c * squared).astype(jnp.bfloat16)
    factor_panel = lax.all_gather(factor, "col", axis=1, tiled=True)
    product = jnp.dot(factor_panel, gathered, preferred_element_type=jnp.float32)
    result = coef_a * iterate.astype(jnp.float32) + product
    return (math.sqrt(N) * result).astype(jnp.bfloat16)


def whole():
    return pl.BlockSpec(memory_space=pltpu.VMEM)


def scalars():
    return pl.BlockSpec(memory_space=pltpu.SMEM)


def near_kernel(x, l1, r1, out, both):
    rows = x.shape[0]
    both[:rows, :] = x[...]
    for place, one, other in ((0, l1, r1), (1, r1, l1)):
        both[rows:, :] = other[...]
        for part in (slice(0, rows // 2), slice(rows // 2, rows)):
            value = dot_rows(both[...], one[part, :]).astype(out.dtype)
            out[place, :, part] = value[:rows]
            out[place + 2, :, part] = value[rows:]


def near_blocks(x, l1, r1):
    rows, depth = x.shape
    return pl.pallas_call(
        near_kernel,
        out_shape=jax.ShapeDtypeStruct((4, rows, rows), jnp.bfloat16),
        in_specs=[whole()] * 3,
        out_specs=whole(),
        scratch_shapes=[pltpu.VMEM((2 * rows, depth), jnp.bfloat16)],
        compiler_params=pltpu.CompilerParams(vmem_limit_bytes=52 * 2**20),
        cost_estimate=pl.CostEstimate(
            flops=8 * rows * rows * depth, bytes_accessed=6 * rows * depth, transcendentals=0
        ),
    )(x, l1, r1)


def corner_kernel(place, l1, r1, l2, r2, out):
    rows = l1.shape[0]
    out[...] = jnp.zeros_like(out)
    for plane, one, other in ((1, r1, l2), (2, l1, r2)):

        @pl.when(place[0] == plane)
        def _(one=one, other=other):
            for part in (slice(0, rows // 2), slice(rows // 2, rows)):
                out[0, :, part] = dot_rows(one[...], other[part, :]).astype(out.dtype)


def corner_block(place, l1, r1, l2, r2):
    rows, depth = l1.shape
    return pl.pallas_call(
        corner_kernel,
        out_shape=jax.ShapeDtypeStruct((1, rows, rows), jnp.bfloat16),
        in_specs=[scalars()] + [whole()] * 4,
        out_specs=whole(),
        compiler_params=pltpu.CompilerParams(vmem_limit_bytes=48 * 2**20),
        cost_estimate=pl.CostEstimate(
            flops=128 * rows * rows * depth, bytes_accessed=8 * rows * depth, transcendentals=0
        ),
    )(place, l1, r1, l2, r2)


def square_kernel(place, panel, own, l1, r3, l2, r2, r1, l3, corner, pair, end, last, out):
    z = place[0]
    part = own.shape[1]
    rows = panel.shape[1]
    at_end = jnp.logical_or(z == 0, z == 3)
    near = jnp.where(at_end, end[0], corner[0])
    far = jnp.where(at_end, last[0], pair[0])
    low = jnp.where(z < 2, near, far)
    high = jnp.where(z < 2, far, near)
    zero = jnp.zeros_like(low)

    def strip(e, block):
        if e == 0:
            value = own[block]
        else:
            one, other = {1: (l1, r3), 2: (l2, r2), 3: (r1, l3)}[e]
            value = one[block] + other[block]
        if block == 3:
            value = value + jnp.where((z + e) % 4 == 0, low, zero)
        if block == 1:
            value = value + jnp.where((z + e) % 4 == 3, high, zero)
        return value

    total = jnp.zeros((rows, 4 * part), jnp.float32)
    for d in range(4):
        right = jnp.concatenate([strip(e, (d - e) % 4) for e in range(4)], axis=0)
        total = total + dot_rows(panel[d], right)
    index = lax.broadcasted_iota(jnp.int32, (rows, rows), 0)
    other = lax.broadcasted_iota(jnp.int32, (rows, rows), 1)
    unit = jnp.where(index == other, 1.0, 0.0).astype(jnp.bfloat16)
    linear = dot_rows(unit, jnp.concatenate([strip(e, (-e) % 4) for e in range(4)], axis=0))
    out[...] = (coef_b * linear + coef_c * total).astype(out.dtype)


def square(place, panel, *others):
    rows = panel.shape[1]
    part = others[0].shape[1]
    return pl.pallas_call(
        square_kernel,
        out_shape=jax.ShapeDtypeStruct((rows, 4 * part), jnp.bfloat16),
        in_specs=[scalars()] + [whole()] * (1 + len(others)),
        out_specs=whole(),
        compiler_params=pltpu.CompilerParams(vmem_limit_bytes=48 * 2**20),
        cost_estimate=pl.CostEstimate(
            flops=2 * rows * rows * 4 * 4 * part, bytes_accessed=2 * 5 * rows * rows, transcendentals=0
        ),
    )(place, panel, *others)


def product_kernel(starts, place, f, x, l1, r1, l2, r2, *rest):
    n_piece = len(starts) - 1
    far = [rest[p : 2 * n_piece : n_piece] for p in range(n_piece)]
    out, wide = rest[-2:]
    n_col, part, width = x.shape
    step = pl.program_id(0)
    wide[:, :part, :] = x[...]
    wide[:, 2 * part : 3 * part, :] = l2[...] + r2[...]
    for p in range(n_piece):

        @pl.when(jnp.logical_and(step >= starts[p], step < starts[p + 1]))
        def _(p=p):
            value = far[p][0][...] + far[p][1][...]
            zero = jnp.zeros_like(value)
            wide[:, part : 2 * part, :] = l1[...] + jnp.where(place[0] == 3, value, zero)
            wide[:, 3 * part :, :] = r1[...] + jnp.where(place[0] == 0, value, zero)

    total = coef_a * x[...].reshape(n_col * part, width).astype(jnp.float32)
    for c in range(n_col):
        total = total + jnp.dot(f[c], wide[c], preferred_element_type=jnp.float32)
    out[...] = (math.sqrt(N) * total).astype(out.dtype)


def product(place, f, near, far, tile, first, before):
    n_col, rows, depth = f.shape
    part = rows // n_col
    columns = near[0].shape[1]

    def split(value):
        return value.reshape(n_col, part, value.shape[1])

    starts = [0]
    for piece in far[0]:
        starts.append(starts[-1] + piece.shape[1] // tile)

    def piece_spec(p):
        begin, count = starts[p], starts[p + 1] - starts[p]
        return pl.BlockSpec((n_col, part, tile), lambda i: (0, 0, jnp.clip(i - begin, 0, count - 1)))

    plain = pl.BlockSpec((n_col, part, tile), lambda i: (0, 0, i + first))
    pieces = [piece_spec(p) for p in range(len(far[0]))]
    operands = [place, f, *(split(value) for value in (*near, *far[0], *far[1]))]
    in_specs = [
        scalars(),
        pl.BlockSpec((n_col, rows, depth), lambda i: (0, 0, 0), pipeline_mode=pl.Buffered(1)),
    ]
    in_specs += [plain] * len(near) + pieces * 2
    aliases = {}
    if before is not None:
        aliases = {len(operands): 0}
        operands.append(before)
        in_specs.append(pl.BlockSpec(memory_space=pl.ANY))
    share = tile * starts[-1]
    return pl.pallas_call(
        functools.partial(product_kernel, tuple(starts)),
        grid=(starts[-1],),
        out_shape=jax.ShapeDtypeStruct((rows, columns), jnp.bfloat16),
        in_specs=in_specs,
        out_specs=pl.BlockSpec((rows, tile), lambda i: (0, i + first)),
        scratch_shapes=[pltpu.VMEM((n_col, depth, tile), jnp.bfloat16)],
        input_output_aliases=aliases,
        compiler_params=pltpu.CompilerParams(vmem_limit_bytes=56 * 2**20),
        cost_estimate=pl.CostEstimate(
            flops=2 * rows * n_col * depth * share, bytes_accessed=2 * 12 * rows * share, transcendentals=0
        ),
    )(*operands)


def per_device_line(n_col, x):
    z = lax.axis_index("row")
    place = z.reshape(1).astype(jnp.int32)
    right, left = [(0, 1), (1, 2), (2, 3)], [(3, 2), (2, 1), (1, 0)]

    def send(value, pairs):
        return lax.ppermute(value, "row", pairs)

    def scatter(blocks):
        return lax.psum_scatter(blocks, "col", scatter_dimension=1, tiled=True)

    r1, l1 = send(x, right), send(x, left)
    own = scatter(dot_rows(x, x).astype(jnp.bfloat16)[None])
    own, r1, l1 = lax.optimization_barrier((own, r1, l1))
    r2, l2 = send(r1, right[1:]), send(l1, left[1:])

    first = scatter(near_blocks(x, l1, r1))
    corner = corner_block(place, l1, r1, l2, r2)
    corner, first = lax.optimization_barrier((corner, first))
    corner = scatter(corner)

    second = send(first[2], left[1:]) + send(first[3], right[1:])
    tile = jnp.stack([own[0], first[0], second, first[1]])
    tr1, tl1 = send(tile, right), send(tile, left)

    corner, tr1, tl1 = lax.optimization_barrier((corner, tr1, tl1))
    end = send(corner, [(1, 0), (2, 3)])
    pair = send(corner, [(1, 2), (2, 1)])
    zero = jnp.zeros_like(end)
    added = [zero, jnp.where(z == 3, end, zero), zero, jnp.where(z == 0, end, zero)]
    panel = lax.all_gather(tile + jnp.concatenate(added), "col", axis=1, tiled=True)

    end, pair, tr1, tl1 = lax.optimization_barrier((end, pair, tr1, tl1))
    last = send(pair, [(1, 0), (2, 3)])
    tr2, tl2 = send(tr1, right[1:]), send(tl1, left[1:])
    tr3, tl3 = send(tr2, right[2:]), send(tl2, left[2:])
    unit = 256
    marks = [0, 2 * unit, 5 * unit, x.shape[1]]
    pieces = [slice(a, b) for a, b in zip(marks, marks[1:])]
    tr3, tl3, last, on_r, on_l = lax.optimization_barrier((tr3, tl3, last, r2, l2))
    far = [
        [send(on_r[:, piece], right[2:]) for piece in pieces],
        [send(on_l[:, piece], left[2:]) for piece in pieces],
    ]
    panel, far[0][0], far[1][0] = lax.optimization_barrier((panel, far[0][0], far[1][0]))

    factor = square(place, panel, tile, tl1, tr3, tl2, tr2, tr1, tl3, corner, pair, end, last)
    factor = lax.all_gather(factor, "col", axis=0, tiled=False)
    near = [x, l1, r1, l2, r2]
    out = product(place, factor, near, [part[:2] for part in far], unit, 0, None)
    return product(place, factor, near, [part[2:] for part in far], unit, marks[2] // unit, out)


def solution(mesh):
    n_row, n_col = mesh.shape["row"], mesh.shape["col"]

    def body(iterate):
        if (n_row, n_col) == (4, 8) and iterate.shape == (896, 2304):
            return per_device_line(n_col, iterate)
        return per_device(iterate)

    return jax.shard_map(
        body,
        mesh=mesh,
        in_specs=(P("row", "col"),),
        out_specs=P("row", "col"),
        check_vma=False,
    )
```

```python
import functools
import math

import jax
import jax.numpy as jnp
from jax import lax
from jax.experimental import pallas as pl
from jax.experimental.pallas import tpu as pltpu
from jax.sharding import PartitionSpec as P

N = 18432


coef_a = 3.4445
coef_b = -4.775
coef_c = 2.0315


def dot_rows(left, right):
    return lax.dot_general(
        left, right, (((1,), (1,)), ((), ())), preferred_element_type=jnp.float32
    )


def per_device(iterate):
    contract = (((1,), (1,)), ((), ()))
    gathered = lax.all_gather(iterate, "row", axis=0, tiled=True)
    partial_value = lax.dot_general(
        iterate, gathered, contract, preferred_element_type=jnp.float32
    )
    partial_value = partial_value.astype(jnp.bfloat16)
    gram_tile = lax.psum_scatter(partial_value, "col", scatter_dimension=1, tiled=True)
    gram_panel = lax.all_gather(gram_tile, "col", axis=1, tiled=True)
    squared = jnp.dot(
        gram_panel,
        lax.all_gather(gram_tile, "row", axis=0, tiled=True),
        preferred_element_type=jnp.float32,
    )
    factor = (coef_b * gram_tile.astype(jnp.float32) + coef_c * squared).astype(jnp.bfloat16)
    factor_panel = lax.all_gather(factor, "col", axis=1, tiled=True)
    product = jnp.dot(factor_panel, gathered, preferred_element_type=jnp.float32)
    result = coef_a * iterate.astype(jnp.float32) + product
    return (math.sqrt(N) * result).astype(jnp.bfloat16)


def whole():
    return pl.BlockSpec(memory_space=pltpu.VMEM)


def scalars():
    return pl.BlockSpec(memory_space=pltpu.SMEM)


def near_kernel(x, l1, r1, out, both):
    rows = x.shape[0]
    both[:rows, :] = x[...]
    for place, one, other in ((0, l1, r1), (1, r1, l1)):
        both[rows:, :] = other[...]
        for part in (slice(0, rows // 2), slice(rows // 2, rows)):
            value = dot_rows(both[...], one[part, :]).astype(out.dtype)
            out[place, :, part] = value[:rows]
            out[place + 2, :, part] = value[rows:]


def near_blocks(x, l1, r1):
    rows, depth = x.shape
    return pl.pallas_call(
        near_kernel,
        out_shape=jax.ShapeDtypeStruct((4, rows, rows), jnp.bfloat16),
        in_specs=[whole()] * 3,
        out_specs=whole(),
        scratch_shapes=[pltpu.VMEM((2 * rows, depth), jnp.bfloat16)],
        compiler_params=pltpu.CompilerParams(vmem_limit_bytes=52 * 2**20),
        cost_estimate=pl.CostEstimate(
            flops=8 * rows * rows * depth, bytes_accessed=6 * rows * depth, transcendentals=0
        ),
    )(x, l1, r1)


def corner_kernel(place, l1, r1, l2, r2, out, held, sems):
    rows = l1.shape[0]
    half = rows // 2
    for plane, one, other in ((1, r1, l2), (2, l1, r2)):

        @pl.when(place[0] == plane)
        def _(one=one, other=other):
            copies = [
                pltpu.make_async_copy(one, held.at[0], sems.at[0]),
                pltpu.make_async_copy(other.at[:half, :], held.at[1, :half, :], sems.at[1]),
                pltpu.make_async_copy(other.at[half:, :], held.at[1, half:, :], sems.at[2]),
            ]
            for copy in copies:
                copy.start()
            copies[0].wait()
            for part, copy in ((slice(0, half), copies[1]), (slice(half, rows), copies[2])):
                copy.wait()
                out[0, :, part] = dot_rows(held[0], held[1, part, :]).astype(out.dtype)

    @pl.when(jnp.logical_or(place[0] == 0, place[0] == 3))
    def _():
        out[...] = jnp.zeros_like(out)


def corner_block(place, l1, r1, l2, r2):
    rows, depth = l1.shape
    return pl.pallas_call(
        corner_kernel,
        out_shape=jax.ShapeDtypeStruct((1, rows, rows), jnp.bfloat16),
        in_specs=[scalars()] + [pl.BlockSpec(memory_space=pl.ANY)] * 4,
        out_specs=whole(),
        scratch_shapes=[pltpu.VMEM((2, rows, depth), jnp.bfloat16), pltpu.SemaphoreType.DMA((3,))],
        compiler_params=pltpu.CompilerParams(vmem_limit_bytes=32 * 2**20),
        cost_estimate=pl.CostEstimate(
            flops=128 * rows * rows * depth, bytes_accessed=8 * rows * depth, transcendentals=0
        ),
    )(place, l1, r1, l2, r2)


def square_kernel(place, panel, own, l1, r3, l2, r2, r1, l3, corner, pair, end, last, out):
    z = place[0]
    part = own.shape[1]
    rows = panel.shape[1]
    at_end = jnp.logical_or(z == 0, z == 3)
    near = jnp.where(at_end, end[0], corner[0])
    far = jnp.where(at_end, last[0], pair[0])
    low = jnp.where(z < 2, near, far)
    high = jnp.where(z < 2, far, near)
    zero = jnp.zeros_like(low)

    def strip(e, block):
        if e == 0:
            value = own[block]
        else:
            one, other = {1: (l1, r3), 2: (l2, r2), 3: (r1, l3)}[e]
            value = one[block] + other[block]
        if block == 3:
            value = value + jnp.where((z + e) % 4 == 0, low, zero)
        if block == 1:
            value = value + jnp.where((z + e) % 4 == 3, high, zero)
        return value

    total = jnp.zeros((rows, 4 * part), jnp.float32)
    for d in range(4):
        right = jnp.concatenate([strip(e, (d - e) % 4) for e in range(4)], axis=0)
        total = total + dot_rows(panel[d], right)
    index = lax.broadcasted_iota(jnp.int32, (rows, rows), 0)
    other = lax.broadcasted_iota(jnp.int32, (rows, rows), 1)
    unit = jnp.where(index == other, 1.0, 0.0).astype(jnp.bfloat16)
    linear = dot_rows(unit, jnp.concatenate([strip(e, (-e) % 4) for e in range(4)], axis=0))
    out[...] = (coef_b * linear + coef_c * total).astype(out.dtype)


def square(place, panel, *others):
    rows = panel.shape[1]
    part = others[0].shape[1]
    return pl.pallas_call(
        square_kernel,
        out_shape=jax.ShapeDtypeStruct((rows, 4 * part), jnp.bfloat16),
        in_specs=[scalars()] + [whole()] * (1 + len(others)),
        out_specs=whole(),
        compiler_params=pltpu.CompilerParams(vmem_limit_bytes=48 * 2**20),
        cost_estimate=pl.CostEstimate(
            flops=2 * rows * rows * 4 * 4 * part, bytes_accessed=2 * 5 * rows * rows, transcendentals=0
        ),
    )(place, panel, *others)


def product_kernel(starts, first, place, f, x, l1, r1, l2, r2, *rest):
    n_piece = len(starts) - 1
    from_r, from_l = rest[:n_piece], rest[n_piece : 2 * n_piece]
    out, whole_f, wide, sems = rest[-4:]
    z = place[0]
    n_col, rows, depth = f.shape
    part = depth // 4
    width = out.shape[1]
    step = pl.program_id(0)

    def copy(source, tile, slot, d):
        return pltpu.make_async_copy(
            source.at[:, :, pl.ds(pl.multiple_of(tile * width, width), width)],
            wide.at[slot, :, pl.ds(d * part, part), :],
            sems.at[slot, d],
        )

    def fetch(tile, slot):
        copy(x, first + tile, slot, 0).start()
        for d, usual, edge, pieces in ((1, l1, 3, from_r), (3, r1, 0, from_l)):

            @pl.when(z != edge)
            def _(d=d, usual=usual):
                copy(usual, first + tile, slot, d).start()

            for p in range(n_piece):
                inside = jnp.logical_and(tile >= starts[p], tile < starts[p + 1])

                @pl.when(jnp.logical_and(z == edge, inside))
                def _(d=d, piece=pieces[p], begin=starts[p]):
                    copy(piece, tile - begin, slot, d).start()

        @pl.when(z < 2)
        def _():
            copy(l2, first + tile, slot, 2).start()

        @pl.when(z >= 2)
        def _():
            copy(r2, first + tile, slot, 2).start()

    slot = lax.rem(step, 2)

    @pl.when(step == 0)
    def _():
        fetch(0, 0)
        for c in range(n_col):
            whole_f[:, c * depth : (c + 1) * depth] = f[c]

    @pl.when(step + 1 < starts[-1])
    def _():
        fetch(step + 1, 1 - slot)

    for d in range(4):
        copy(x, first + step, slot, d).wait()
    total = jnp.dot(
        whole_f[...],
        wide[slot].reshape(n_col * depth, width),
        preferred_element_type=jnp.float32,
    )
    own = wide[slot, :, :part, :].reshape(rows, width).astype(jnp.float32)
    out[...] = (math.sqrt(N) * (coef_a * own + total)).astype(out.dtype)


def product(place, f, near, far, tile, first, before):
    n_col, rows, depth = f.shape
    part = rows // n_col
    columns = near[0].shape[1]

    def split(value):
        return value.reshape(n_col, part, value.shape[1])

    starts = [0]
    for piece in far[0]:
        starts.append(starts[-1] + piece.shape[1] // tile)

    outside = pl.BlockSpec(memory_space=pl.ANY)
    operands = [place, f, *(split(value) for value in (*near, *far[0], *far[1]))]
    aliases = {}
    if before is not None:
        aliases = {len(operands): 0}
        operands.append(before)
    share = tile * starts[-1]
    return pl.pallas_call(
        functools.partial(product_kernel, tuple(starts), first),
        grid=(starts[-1],),
        out_shape=jax.ShapeDtypeStruct((rows, columns), jnp.bfloat16),
        in_specs=[
            scalars(),
            pl.BlockSpec((n_col, rows, depth), lambda i: (0, 0, 0), pipeline_mode=pl.Buffered(1)),
        ]
        + [outside] * (len(operands) - 2),
        out_specs=pl.BlockSpec((rows, tile), lambda i: (0, i + first)),
        scratch_shapes=[
            pltpu.VMEM((rows, n_col * depth), jnp.bfloat16),
            pltpu.VMEM((2, n_col, depth, tile), jnp.bfloat16),
            pltpu.SemaphoreType.DMA((2, 4)),
        ],
        input_output_aliases=aliases,
        compiler_params=pltpu.CompilerParams(vmem_limit_bytes=48 * 2**20),
        cost_estimate=pl.CostEstimate(
            flops=2 * rows * n_col * depth * share, bytes_accessed=2 * 6 * rows * share, transcendentals=0
        ),
    )(*operands)


def per_device_line(n_col, x):
    z = lax.axis_index("row")
    place = z.reshape(1).astype(jnp.int32)
    right, left = [(0, 1), (1, 2), (2, 3)], [(3, 2), (2, 1), (1, 0)]

    def send(value, pairs):
        return lax.ppermute(value, "row", pairs)

    def scatter(blocks):
        return lax.psum_scatter(blocks, "col", scatter_dimension=1, tiled=True)

    r1, l1 = send(x, right), send(x, left)
    own = scatter(dot_rows(x, x).astype(jnp.bfloat16)[None])
    own, r1, l1 = lax.optimization_barrier((own, r1, l1))
    r2, l2 = send(r1, right[1:]), send(l1, left[1:])

    first = scatter(near_blocks(x, l1, r1))
    corner = corner_block(place, l1, r1, l2, r2)
    corner, first = lax.optimization_barrier((corner, first))
    corner = scatter(corner)

    second = send(first[2], left[1:]) + send(first[3], right[1:])
    tile = jnp.stack([own[0], first[0], second, first[1]])
    tr1, tl1 = send(tile, right), send(tile, left)

    corner, tr1, tl1 = lax.optimization_barrier((corner, tr1, tl1))
    end = send(corner, [(1, 0), (2, 3)])
    pair = send(corner, [(1, 2), (2, 1)])
    zero = jnp.zeros_like(end)
    added = [zero, jnp.where(z == 3, end, zero), zero, jnp.where(z == 0, end, zero)]
    panel = lax.all_gather(tile + jnp.concatenate(added), "col", axis=1, tiled=True)

    end, tr1, tl1 = lax.optimization_barrier((end, tr1, tl1))
    last = send(pair, [(1, 0), (2, 3)])
    tr2, tl2 = send(tr1, right[1:]), send(tl1, left[1:])
    tr3, tl3 = send(tr2, right[2:]), send(tl2, left[2:])
    unit = 256
    marks = [0, unit, 4 * unit, x.shape[1]]
    pieces = [slice(a, b) for a, b in zip(marks, marks[1:])]
    tr3, tl3, on_r, on_l = lax.optimization_barrier((tr3, tl3, r2, l2))
    from_r, from_l = [], []
    for piece in pieces:
        from_r.append(send(on_r[:, piece], right[2:]))
        from_l.append(send(on_l[:, piece], left[2:]))
        from_r[-1], from_l[-1], on_r, on_l = lax.optimization_barrier(
            (from_r[-1], from_l[-1], on_r, on_l)
        )
    panel, from_r[0], from_l[0] = lax.optimization_barrier((panel, from_r[0], from_l[0]))
    far = [from_r, from_l]

    factor = square(place, panel, tile, tl1, tr3, tl2, tr2, tr1, tl3, corner, pair, end, last)
    factor = lax.all_gather(factor, "col", axis=0, tiled=False)
    near = [x, l1, r1, l2, r2]
    out = product(place, factor, near, [part[:2] for part in far], unit, 0, None)
    return product(place, factor, near, [part[2:] for part in far], unit, marks[2] // unit, out)


def solution(mesh):
    n_row, n_col = mesh.shape["row"], mesh.shape["col"]

    def body(iterate):
        if (n_row, n_col) == (4, 8) and iterate.shape == (896, 2304):
            return per_device_line(n_col, iterate)
        return per_device(iterate)

    return jax.shard_map(
        body,
        mesh=mesh,
        in_specs=(P("row", "col"),),
        out_specs=P("row", "col"),
        check_vma=False,
    )
```

```python
import functools
import math

import jax
import jax.numpy as jnp
from jax import lax
from jax.experimental import pallas as pl
from jax.experimental.pallas import tpu as pltpu
from jax.sharding import PartitionSpec as P

N = 18432


coef_a = 3.4445
coef_b = -4.775
coef_c = 2.0315


def dot_rows(left, right):
    return lax.dot_general(
        left, right, (((1,), (1,)), ((), ())), preferred_element_type=jnp.float32
    )


def per_device(iterate):
    contract = (((1,), (1,)), ((), ()))
    gathered = lax.all_gather(iterate, "row", axis=0, tiled=True)
    partial_value = lax.dot_general(
        iterate, gathered, contract, preferred_element_type=jnp.float32
    )
    partial_value = partial_value.astype(jnp.bfloat16)
    gram_tile = lax.psum_scatter(partial_value, "col", scatter_dimension=1, tiled=True)
    gram_panel = lax.all_gather(gram_tile, "col", axis=1, tiled=True)
    squared = jnp.dot(
        gram_panel,
        lax.all_gather(gram_tile, "row", axis=0, tiled=True),
        preferred_element_type=jnp.float32,
    )
    factor = (coef_b * gram_tile.astype(jnp.float32) + coef_c * squared).astype(jnp.bfloat16)
    factor_panel = lax.all_gather(factor, "col", axis=1, tiled=True)
    product = jnp.dot(factor_panel, gathered, preferred_element_type=jnp.float32)
    result = coef_a * iterate.astype(jnp.float32) + product
    return (math.sqrt(N) * result).astype(jnp.bfloat16)


def whole():
    return pl.BlockSpec(memory_space=pltpu.VMEM)


def scalars():
    return pl.BlockSpec(memory_space=pltpu.SMEM)


def near_kernel(x, l1, r1, out, both):
    rows = x.shape[0]
    both[:rows, :] = x[...]
    for place, one, other in ((0, l1, r1), (1, r1, l1)):
        both[rows:, :] = other[...]
        for part in (slice(0, rows // 2), slice(rows // 2, rows)):
            value = dot_rows(both[...], one[part, :]).astype(out.dtype)
            out[place, :, part] = value[:rows]
            out[place + 2, :, part] = value[rows:]


def near_blocks(x, l1, r1):
    rows, depth = x.shape
    return pl.pallas_call(
        near_kernel,
        out_shape=jax.ShapeDtypeStruct((4, rows, rows), jnp.bfloat16),
        in_specs=[whole()] * 3,
        out_specs=whole(),
        scratch_shapes=[pltpu.VMEM((2 * rows, depth), jnp.bfloat16)],
        compiler_params=pltpu.CompilerParams(vmem_limit_bytes=52 * 2**20),
        cost_estimate=pl.CostEstimate(
            flops=8 * rows * rows * depth, bytes_accessed=6 * rows * depth, transcendentals=0
        ),
    )(x, l1, r1)


def corner_kernel(place, l1, r1, l2, r2, out, held, sems):
    rows = l1.shape[0]
    half = rows // 2
    for plane, one, other in ((1, r1, l2), (2, l1, r2)):

        @pl.when(place[0] == plane)
        def _(one=one, other=other):
            copies = [
                pltpu.make_async_copy(one, held.at[0], sems.at[0]),
                pltpu.make_async_copy(other.at[:half, :], held.at[1, :half, :], sems.at[1]),
                pltpu.make_async_copy(other.at[half:, :], held.at[1, half:, :], sems.at[2]),
            ]
            for copy in copies:
                copy.start()
            copies[0].wait()
            for part, copy in ((slice(0, half), copies[1]), (slice(half, rows), copies[2])):
                copy.wait()
                out[0, :, part] = dot_rows(held[0], held[1, part, :]).astype(out.dtype)

    @pl.when(jnp.logical_or(place[0] == 0, place[0] == 3))
    def _():
        out[...] = jnp.zeros_like(out)


def corner_block(place, l1, r1, l2, r2):
    rows, depth = l1.shape
    return pl.pallas_call(
        corner_kernel,
        out_shape=jax.ShapeDtypeStruct((1, rows, rows), jnp.bfloat16),
        in_specs=[scalars()] + [pl.BlockSpec(memory_space=pl.ANY)] * 4,
        out_specs=whole(),
        scratch_shapes=[pltpu.VMEM((2, rows, depth), jnp.bfloat16), pltpu.SemaphoreType.DMA((3,))],
        compiler_params=pltpu.CompilerParams(vmem_limit_bytes=32 * 2**20),
        cost_estimate=pl.CostEstimate(
            flops=128 * rows * rows * depth, bytes_accessed=8 * rows * depth, transcendentals=0
        ),
    )(place, l1, r1, l2, r2)


def square_kernel(place, panel, own, l1, r3, l2, r2, r1, l3, corner, pair, end, out, last):
    z = place[0]
    part = own.shape[1]
    rows = panel.shape[1]
    at_end = jnp.logical_or(z == 0, z == 3)
    for plane, block in ((0, 3), (3, 1)):

        @pl.when(z == plane)
        def _(block=block):
            index = lax.broadcasted_iota(jnp.int32, (part, rows), 0) + place[1] * part
            other = lax.broadcasted_iota(jnp.int32, (part, rows), 1)
            pick = jnp.where(index == other, 1.0, 0.0).astype(jnp.bfloat16)
            last[...] = dot_rows(pick, panel[block]).astype(last.dtype)

    @pl.when(jnp.logical_not(at_end))
    def _():
        last[...] = pair[0]

    near = jnp.where(at_end, end[0], corner[0])
    far = last[...]
    low = jnp.where(z < 2, near, far)
    high = jnp.where(z < 2, far, near)
    zero = jnp.zeros_like(low)

    def strip(e, block):
        if e == 0:
            value = own[block]
        else:
            one, other = {1: (l1, r3), 2: (l2, r2), 3: (r1, l3)}[e]
            value = one[block] + other[block]
        if block == 3:
            value = value + jnp.where((z + e) % 4 == 0, low, zero)
        if block == 1:
            value = value + jnp.where((z + e) % 4 == 3, high, zero)
        return value

    total = jnp.zeros((rows, 4 * part), jnp.float32)
    for d in range(4):
        right = jnp.concatenate([strip(e, (d - e) % 4) for e in range(4)], axis=0)
        total = total + dot_rows(panel[d], right)
    index = lax.broadcasted_iota(jnp.int32, (rows, rows), 0)
    other = lax.broadcasted_iota(jnp.int32, (rows, rows), 1)
    unit = jnp.where(index == other, 1.0, 0.0).astype(jnp.bfloat16)
    linear = dot_rows(unit, jnp.concatenate([strip(e, (-e) % 4) for e in range(4)], axis=0))
    out[...] = (coef_b * linear + coef_c * total).astype(out.dtype)


def square(place, panel, *others):
    rows = panel.shape[1]
    part = others[0].shape[1]
    return pl.pallas_call(
        square_kernel,
        out_shape=jax.ShapeDtypeStruct((rows, 4 * part), jnp.bfloat16),
        in_specs=[scalars()] + [whole()] * (1 + len(others)),
        out_specs=whole(),
        scratch_shapes=[pltpu.VMEM((part, rows), jnp.bfloat16)],
        compiler_params=pltpu.CompilerParams(vmem_limit_bytes=48 * 2**20),
        cost_estimate=pl.CostEstimate(
            flops=2 * rows * rows * 4 * 4 * part, bytes_accessed=2 * 5 * rows * rows, transcendentals=0
        ),
    )(place, panel, *others)


def product_kernel(starts, first, place, f, x, l1, r1, across, *rest):
    n_piece = len(starts) - 1
    far = rest[:n_piece]
    out, whole_f, wide, sems = rest[-4:]
    z = place[0]
    n_col, rows, depth = f.shape
    part = depth // 4
    width = out.shape[1]
    step = pl.program_id(0)

    def copy(source, tile, slot, d):
        return pltpu.make_async_copy(
            source.at[:, :, pl.ds(pl.multiple_of(tile * width, width), width)],
            wide.at[slot, :, pl.ds(d * part, part), :],
            sems.at[slot, d],
        )

    def fetch(tile, slot):
        copy(x, first + tile, slot, 0).start()
        copy(across, first + tile, slot, 2).start()
        for d, usual, edge in ((1, l1, 3), (3, r1, 0)):

            @pl.when(z != edge)
            def _(d=d, usual=usual):
                copy(usual, first + tile, slot, d).start()

            for p in range(n_piece):
                inside = jnp.logical_and(tile >= starts[p], tile < starts[p + 1])

                @pl.when(jnp.logical_and(z == edge, inside))
                def _(d=d, piece=far[p], begin=starts[p]):
                    copy(piece, tile - begin, slot, d).start()

    slot = lax.rem(step, 2)

    @pl.when(step == 0)
    def _():
        fetch(0, 0)
        for c in range(n_col):
            whole_f[:, c * depth : (c + 1) * depth] = f[c]

    @pl.when(step + 1 < starts[-1])
    def _():
        fetch(step + 1, 1 - slot)

    for d in range(4):
        copy(x, first + step, slot, d).wait()
    total = jnp.dot(
        whole_f[...],
        wide[slot].reshape(n_col * depth, width),
        preferred_element_type=jnp.float32,
    )
    own = wide[slot, :, :part, :].reshape(rows, width).astype(jnp.float32)
    out[...] = (math.sqrt(N) * (coef_a * own + total)).astype(out.dtype)


def product(place, f, near, far, tile, first, before):
    n_col, rows, depth = f.shape
    part = rows // n_col
    columns = near[0].shape[1]

    def split(value):
        return value.reshape(n_col, part, value.shape[1])

    starts = [0]
    for piece in far:
        starts.append(starts[-1] + piece.shape[1] // tile)

    outside = pl.BlockSpec(memory_space=pl.ANY)
    operands = [place, f, *(split(value) for value in (*near, *far))]
    aliases = {}
    if before is not None:
        aliases = {len(operands): 0}
        operands.append(before)
    share = tile * starts[-1]
    return pl.pallas_call(
        functools.partial(product_kernel, tuple(starts), first),
        grid=(starts[-1],),
        out_shape=jax.ShapeDtypeStruct((rows, columns), jnp.bfloat16),
        in_specs=[
            scalars(),
            pl.BlockSpec((n_col, rows, depth), lambda i: (0, 0, 0), pipeline_mode=pl.Buffered(1)),
        ]
        + [outside] * (len(operands) - 2),
        out_specs=pl.BlockSpec((rows, tile), lambda i: (0, i + first)),
        scratch_shapes=[
            pltpu.VMEM((rows, n_col * depth), jnp.bfloat16),
            pltpu.VMEM((2, n_col, depth, tile), jnp.bfloat16),
            pltpu.SemaphoreType.DMA((2, 4)),
        ],
        input_output_aliases=aliases,
        compiler_params=pltpu.CompilerParams(vmem_limit_bytes=48 * 2**20),
        cost_estimate=pl.CostEstimate(
            flops=2 * rows * n_col * depth * share, bytes_accessed=2 * 6 * rows * share, transcendentals=0
        ),
    )(*operands)


def arrived_kernel(value, out):
    pass


def arrived(value):
    outside = pl.BlockSpec(memory_space=pl.ANY)
    return pl.pallas_call(
        arrived_kernel,
        out_shape=jax.ShapeDtypeStruct(value.shape, value.dtype),
        in_specs=[outside],
        out_specs=outside,
        input_output_aliases={0: 0},
        cost_estimate=pl.CostEstimate(flops=2 * 10**11, bytes_accessed=0, transcendentals=0),
    )(value)


def per_device_line(n_col, x):
    z = lax.axis_index("row")
    place = jnp.stack([z, lax.axis_index("col")]).astype(jnp.int32)
    right, left = [(0, 1), (1, 2), (2, 3)], [(3, 2), (2, 1), (1, 0)]

    def send(value, pairs):
        return lax.ppermute(value, "row", pairs)

    def scatter(blocks):
        return lax.psum_scatter(blocks, "col", scatter_dimension=1, tiled=True)

    r1, l1 = send(x, right), send(x, left)
    own = scatter(dot_rows(x, x).astype(jnp.bfloat16)[None])
    own, r1, l1 = lax.optimization_barrier((own, r1, l1))
    r2, l2 = send(r1, right[1:]), send(l1, left[1:])

    first = scatter(near_blocks(x, l1, r1))
    corner = corner_block(place, l1, r1, l2, r2)
    corner, first = lax.optimization_barrier((corner, first))
    corner = scatter(corner)

    second = send(first[2], left[1:]) + send(first[3], right[1:])
    tile = jnp.stack([own[0], first[0], second, first[1]])
    tr1, tl1 = send(tile, right), send(tile, left)

    corner, tr1, tl1 = lax.optimization_barrier((corner, tr1, tl1))
    end = send(corner, [(1, 0), (2, 3)])
    pair = send(corner, [(1, 2), (2, 1)])
    zero = jnp.zeros_like(end)
    added = [zero, jnp.where(z == 3, end, zero), zero, jnp.where(z == 0, end, zero)]
    panel = lax.all_gather(tile + jnp.concatenate(added), "col", axis=1, tiled=True)

    end, tr1, tl1 = lax.optimization_barrier((end, tr1, tl1))
    tr2, tl2 = send(tr1, right[1:]), send(tl1, left[1:])
    tr3, tl3 = send(tr2, right[2:]), send(tl2, left[2:])
    unit = 256
    marks = [0, x.shape[1] - 2 * unit, x.shape[1]]
    across = l2 + r2
    tr3, tl3, onward = lax.optimization_barrier((tr3, tl3, across))
    far = [send(onward[:, a:b], [(1, 0), (2, 3)]) for a, b in zip(marks, marks[1:])]
    far[0] = arrived(far[0])

    factor = square(place, panel, tile, tl1, tr3, tl2, tr2, tr1, tl3, corner, pair, end)
    factor = lax.all_gather(factor, "col", axis=0, tiled=False)
    near = [x, l1, r1, across]
    out = product(place, factor, near, far[:1], unit, 0, None)
    return product(place, factor, near, far[1:], unit, marks[1] // unit, out)


def solution(mesh):
    n_row, n_col = mesh.shape["row"], mesh.shape["col"]

    def body(iterate):
        if (n_row, n_col) == (4, 8) and iterate.shape == (896, 2304):
            return per_device_line(n_col, iterate)
        return per_device(iterate)

    return jax.shard_map(
        body,
        mesh=mesh,
        in_specs=(P("row", "col"),),
        out_specs=P("row", "col"),
        check_vma=False,
    )
```

```python
import functools
import math

import jax
import jax.numpy as jnp
from jax import lax
from jax.experimental import pallas as pl
from jax.experimental.pallas import tpu as pltpu
from jax.sharding import PartitionSpec as P

N = 18432


coef_a = 3.4445
coef_b = -4.775
coef_c = 2.0315


def dot_rows(left, right):
    return lax.dot_general(
        left, right, (((1,), (1,)), ((), ())), preferred_element_type=jnp.float32
    )


def per_device(iterate):
    contract = (((1,), (1,)), ((), ()))
    gathered = lax.all_gather(iterate, "row", axis=0, tiled=True)
    partial_value = lax.dot_general(
        iterate, gathered, contract, preferred_element_type=jnp.float32
    )
    partial_value = partial_value.astype(jnp.bfloat16)
    gram_tile = lax.psum_scatter(partial_value, "col", scatter_dimension=1, tiled=True)
    gram_panel = lax.all_gather(gram_tile, "col", axis=1, tiled=True)
    squared = jnp.dot(
        gram_panel,
        lax.all_gather(gram_tile, "row", axis=0, tiled=True),
        preferred_element_type=jnp.float32,
    )
    factor = (coef_b * gram_tile.astype(jnp.float32) + coef_c * squared).astype(jnp.bfloat16)
    factor_panel = lax.all_gather(factor, "col", axis=1, tiled=True)
    product = jnp.dot(factor_panel, gathered, preferred_element_type=jnp.float32)
    result = coef_a * iterate.astype(jnp.float32) + product
    return (math.sqrt(N) * result).astype(jnp.bfloat16)


def whole():
    return pl.BlockSpec(memory_space=pltpu.VMEM)


def scalars():
    return pl.BlockSpec(memory_space=pltpu.SMEM)


def near_kernel(x, l1, r1, out, both):
    rows = x.shape[0]
    both[:rows, :] = x[...]
    for place, one, other in ((0, l1, r1), (1, r1, l1)):
        both[rows:, :] = other[...]
        for part in (slice(0, rows // 2), slice(rows // 2, rows)):
            value = dot_rows(both[...], one[part, :]).astype(out.dtype)
            out[place, :, part] = value[:rows]
            out[place + 2, :, part] = value[rows:]


def near_blocks(x, l1, r1):
    rows, depth = x.shape
    return pl.pallas_call(
        near_kernel,
        out_shape=jax.ShapeDtypeStruct((4, rows, rows), jnp.bfloat16),
        in_specs=[whole()] * 3,
        out_specs=whole(),
        scratch_shapes=[pltpu.VMEM((2 * rows, depth), jnp.bfloat16)],
        compiler_params=pltpu.CompilerParams(vmem_limit_bytes=52 * 2**20),
        cost_estimate=pl.CostEstimate(
            flops=8 * rows * rows * depth, bytes_accessed=6 * rows * depth, transcendentals=0
        ),
    )(x, l1, r1)


def corner_kernel(place, l1, r1, l2, r2, out, held, sems):
    rows = l1.shape[0]
    half = rows // 2
    for plane, one, other in ((1, r1, l2), (2, l1, r2)):

        @pl.when(place[0] == plane)
        def _(one=one, other=other):
            copies = [
                pltpu.make_async_copy(one, held.at[0], sems.at[0]),
                pltpu.make_async_copy(other.at[:half, :], held.at[1, :half, :], sems.at[1]),
                pltpu.make_async_copy(other.at[half:, :], held.at[1, half:, :], sems.at[2]),
            ]
            for copy in copies:
                copy.start()
            copies[0].wait()
            for part, copy in ((slice(0, half), copies[1]), (slice(half, rows), copies[2])):
                copy.wait()
                out[0, :, part] = dot_rows(held[0], held[1, part, :]).astype(out.dtype)

    @pl.when(jnp.logical_or(place[0] == 0, place[0] == 3))
    def _():
        out[...] = jnp.zeros_like(out)


def corner_block(place, l1, r1, l2, r2):
    rows, depth = l1.shape
    return pl.pallas_call(
        corner_kernel,
        out_shape=jax.ShapeDtypeStruct((1, rows, rows), jnp.bfloat16),
        in_specs=[scalars()] + [pl.BlockSpec(memory_space=pl.ANY)] * 4,
        out_specs=whole(),
        scratch_shapes=[pltpu.VMEM((2, rows, depth), jnp.bfloat16), pltpu.SemaphoreType.DMA((3,))],
        compiler_params=pltpu.CompilerParams(vmem_limit_bytes=32 * 2**20),
        cost_estimate=pl.CostEstimate(
            flops=128 * rows * rows * depth, bytes_accessed=8 * rows * depth, transcendentals=0
        ),
    )(place, l1, r1, l2, r2)


def strips_kernel(place, own, l1, r3, l2, r2, r1, l3, corner, pair, end, out):
    z = place[0]
    part = own.shape[1]
    at_end = jnp.logical_or(z == 0, z == 3)
    zero = jnp.zeros_like(end[0])
    near = jnp.where(at_end, end[0], corner[0])
    far = jnp.where(at_end, zero, pair[0])
    low = jnp.where(z < 2, near, far)
    high = jnp.where(z < 2, far, near)
    for e in range(4):
        for block in range(4):
            if e == 0:
                value = own[block]
            else:
                one, other = {1: (l1, r3), 2: (l2, r2), 3: (r1, l3)}[e]
                value = one[block] + other[block]
            if block == 3:
                value = value + jnp.where((z + e) % 4 == 0, low, zero)
            if block == 1:
                value = value + jnp.where((z + e) % 4 == 3, high, zero)
            out[(block + e) % 4, e * part : (e + 1) * part, :] = value


def strips(place, *others):
    _, part, rows = others[0].shape
    return pl.pallas_call(
        strips_kernel,
        out_shape=jax.ShapeDtypeStruct((4, 4 * part, rows), jnp.bfloat16),
        in_specs=[scalars()] + [whole()] * len(others),
        out_specs=whole(),
        compiler_params=pltpu.CompilerParams(vmem_limit_bytes=24 * 2**20),
        cost_estimate=pl.CostEstimate(
            flops=16 * part * rows, bytes_accessed=2 * 44 * part * rows, transcendentals=0
        ),
    )(place, *others)


def square_kernel(place, panel, right, out, held, first, sems):
    z = place[0]
    rows, part = panel.shape[1], right.shape[1] // 4
    order = (3, 1, 2, 0)
    copies = {d: pltpu.make_async_copy(panel.at[d], held.at[d], sems.at[d]) for d in order}
    for d in order:
        copies[d].start()
    first[...] = right[0]
    total = jnp.zeros(out.shape, jnp.float32)
    for d in order[:3]:
        copies[d].wait()
        total = total + dot_rows(held[d], right[d])
    for plane, block, e in ((0, 3, 3), (3, 1, 1)):

        @pl.when(z == plane)
        def _(block=block, e=e):
            index = lax.broadcasted_iota(jnp.int32, (part, rows), 0) + place[1] * part
            other = lax.broadcasted_iota(jnp.int32, (part, rows), 1)
            pick = jnp.where(index == other, 1.0, 0.0).astype(jnp.bfloat16)
            far = dot_rows(pick, held[block]).astype(first.dtype)
            first[e * part : (e + 1) * part, :] = right[0, e * part : (e + 1) * part, :] + far

    copies[0].wait()
    total = total + dot_rows(held[0], first[...])
    index = lax.broadcasted_iota(jnp.int32, (rows, rows), 0)
    other = lax.broadcasted_iota(jnp.int32, (rows, rows), 1)
    unit = jnp.where(index == other, 1.0, 0.0).astype(jnp.bfloat16)
    out[...] = (coef_b * dot_rows(unit, first[...]) + coef_c * total).astype(out.dtype)


def square(place, panel, right):
    rows, depth = panel.shape[1], right.shape[1]
    return pl.pallas_call(
        square_kernel,
        out_shape=jax.ShapeDtypeStruct((rows, depth), jnp.bfloat16),
        in_specs=[scalars(), pl.BlockSpec(memory_space=pl.ANY), whole()],
        out_specs=whole(),
        scratch_shapes=[
            pltpu.VMEM(panel.shape, jnp.bfloat16),
            pltpu.VMEM((depth, rows), jnp.bfloat16),
            pltpu.SemaphoreType.DMA((4,)),
        ],
        compiler_params=pltpu.CompilerParams(vmem_limit_bytes=40 * 2**20),
        cost_estimate=pl.CostEstimate(
            flops=2 * rows * rows * 4 * depth, bytes_accessed=2 * 5 * rows * rows, transcendentals=0
        ),
    )(place, panel, right)


def product_kernel(starts, first, place, f, x, l1, r1, across, *rest):
    n_piece = len(starts) - 1
    far = rest[:n_piece]
    out, whole_f, wide, sems = rest[-4:]
    z = place[0]
    n_col, rows, depth = f.shape
    part = depth // 4
    width = out.shape[1]
    step = pl.program_id(0)

    def copy(source, tile, slot, d):
        return pltpu.make_async_copy(
            source.at[:, :, pl.ds(pl.multiple_of(tile * width, width), width)],
            wide.at[slot, :, pl.ds(d * part, part), :],
            sems.at[slot, d],
        )

    def fetch(tile, slot):
        copy(x, first + tile, slot, 0).start()
        copy(across, first + tile, slot, 2).start()
        for d, usual, edge in ((1, l1, 3), (3, r1, 0)):

            @pl.when(z != edge)
            def _(d=d, usual=usual):
                copy(usual, first + tile, slot, d).start()

            for p in range(n_piece):
                inside = jnp.logical_and(tile >= starts[p], tile < starts[p + 1])

                @pl.when(jnp.logical_and(z == edge, inside))
                def _(d=d, piece=far[p], begin=starts[p]):
                    copy(piece, tile - begin, slot, d).start()

    slot = lax.rem(step, 2)

    @pl.when(step == 0)
    def _():
        fetch(0, 0)
        for c in range(n_col):
            whole_f[:, c * depth : (c + 1) * depth] = f[c]

    @pl.when(step + 1 < starts[-1])
    def _():
        fetch(step + 1, 1 - slot)

    for d in range(4):
        copy(x, first + step, slot, d).wait()
    total = jnp.dot(
        whole_f[...],
        wide[slot].reshape(n_col * depth, width),
        preferred_element_type=jnp.float32,
    )
    own = wide[slot, :, :part, :].reshape(rows, width).astype(jnp.float32)
    out[...] = (math.sqrt(N) * (coef_a * own + total)).astype(out.dtype)


def product(place, f, near, far, tile, first, before):
    n_col, rows, depth = f.shape
    part = rows // n_col
    columns = near[0].shape[1]

    def split(value):
        return value.reshape(n_col, part, value.shape[1])

    starts = [0]
    for piece in far:
        starts.append(starts[-1] + piece.shape[1] // tile)

    outside = pl.BlockSpec(memory_space=pl.ANY)
    operands = [place, f, *(split(value) for value in (*near, *far))]
    aliases = {}
    if before is not None:
        aliases = {len(operands): 0}
        operands.append(before)
    share = tile * starts[-1]
    return pl.pallas_call(
        functools.partial(product_kernel, tuple(starts), first),
        grid=(starts[-1],),
        out_shape=jax.ShapeDtypeStruct((rows, columns), jnp.bfloat16),
        in_specs=[
            scalars(),
            pl.BlockSpec((n_col, rows, depth), lambda i: (0, 0, 0), pipeline_mode=pl.Buffered(1)),
        ]
        + [outside] * (len(operands) - 2),
        out_specs=pl.BlockSpec((rows, tile), lambda i: (0, i + first)),
        scratch_shapes=[
            pltpu.VMEM((rows, n_col * depth), jnp.bfloat16),
            pltpu.VMEM((2, n_col, depth, tile), jnp.bfloat16),
            pltpu.SemaphoreType.DMA((2, 4)),
        ],
        input_output_aliases=aliases,
        compiler_params=pltpu.CompilerParams(vmem_limit_bytes=48 * 2**20),
        cost_estimate=pl.CostEstimate(
            flops=2 * rows * n_col * depth * share, bytes_accessed=2 * 6 * rows * share, transcendentals=0
        ),
    )(*operands)


def arrived_kernel(value, out):
    pass


def arrived(value):
    outside = pl.BlockSpec(memory_space=pl.ANY)
    return pl.pallas_call(
        arrived_kernel,
        out_shape=jax.ShapeDtypeStruct(value.shape, value.dtype),
        in_specs=[outside],
        out_specs=outside,
        input_output_aliases={0: 0},
        cost_estimate=pl.CostEstimate(flops=2 * 10**11, bytes_accessed=0, transcendentals=0),
    )(value)


def per_device_line(n_col, x):
    z = lax.axis_index("row")
    place = jnp.stack([z, lax.axis_index("col")]).astype(jnp.int32)
    right, left = [(0, 1), (1, 2), (2, 3)], [(3, 2), (2, 1), (1, 0)]

    def send(value, pairs):
        return lax.ppermute(value, "row", pairs)

    def scatter(blocks):
        return lax.psum_scatter(blocks, "col", scatter_dimension=1, tiled=True)

    r1, l1 = send(x, right), send(x, left)
    own = scatter(dot_rows(x, x).astype(jnp.bfloat16)[None])
    own, r1, l1 = lax.optimization_barrier((own, r1, l1))
    r2, l2 = send(r1, right[1:]), send(l1, left[1:])

    first = scatter(near_blocks(x, l1, r1))
    corner = corner_block(place, l1, r1, l2, r2)
    corner, first = lax.optimization_barrier((corner, first))
    corner = scatter(corner)

    second = send(first[2], left[1:]) + send(first[3], right[1:])
    tile = jnp.stack([own[0], first[0], second, first[1]])
    tr1, tl1 = send(tile, right), send(tile, left)

    unit = 256
    marks = [0, unit, x.shape[1] - 2 * unit, x.shape[1]]
    across = l2 + r2

    def send_on(p, *after):
        value = lax.optimization_barrier((across, *after))[0]
        return send(value[:, marks[p] : marks[p + 1]], [(1, 0), (2, 3)])

    far = [send_on(0, tile)]
    corner, tr1, tl1, far[0] = lax.optimization_barrier((corner, tr1, tl1, far[0]))
    end = send(corner, [(1, 0), (2, 3)])
    pair = send(corner, [(1, 2), (2, 1)])
    zero = jnp.zeros_like(end)
    added = [zero, jnp.where(z == 3, end, zero), zero, jnp.where(z == 0, end, zero)]
    panel = lax.all_gather(tile + jnp.concatenate(added), "col", axis=1, tiled=True)

    end, tr1, tl1 = lax.optimization_barrier((end, tr1, tl1))
    tr2, tl2 = send(tr1, right[1:]), send(tl1, left[1:])
    tr3, tl3 = send(tr2, right[2:]), send(tl2, left[2:])
    far.append(arrived(send_on(1, tr3, tl3, pair)))

    rights = strips(place, tile, tl1, tr3, tl2, tr2, tr1, tl3, corner, pair, end)
    factor = square(place, panel, rights)
    far.append(send_on(2, factor))
    factor = lax.all_gather(factor, "col", axis=0, tiled=False)
    near = [x, l1, r1, across]
    out = product(place, factor, near, far[:2], unit, 0, None)
    return product(place, factor, near, far[2:], unit, marks[2] // unit, out)


def solution(mesh):
    n_row, n_col = mesh.shape["row"], mesh.shape["col"]

    def body(iterate):
        if (n_row, n_col) == (4, 8) and iterate.shape == (896, 2304):
            return per_device_line(n_col, iterate)
        return per_device(iterate)

    return jax.shard_map(
        body,
        mesh=mesh,
        in_specs=(P("row", "col"),),
        out_specs=P("row", "col"),
        check_vma=False,
    )
```

```python
import functools
import math

import jax
import jax.numpy as jnp
from jax import lax
from jax.experimental import pallas as pl
from jax.experimental.pallas import tpu as pltpu
from jax.sharding import PartitionSpec as P

N = 18432


coef_a = 3.4445
coef_b = -4.775
coef_c = 2.0315


def dot_rows(left, right):
    return lax.dot_general(
        left, right, (((1,), (1,)), ((), ())), preferred_element_type=jnp.float32
    )


def per_device(iterate):
    contract = (((1,), (1,)), ((), ()))
    gathered = lax.all_gather(iterate, "row", axis=0, tiled=True)
    partial_value = lax.dot_general(
        iterate, gathered, contract, preferred_element_type=jnp.float32
    )
    partial_value = partial_value.astype(jnp.bfloat16)
    gram_tile = lax.psum_scatter(partial_value, "col", scatter_dimension=1, tiled=True)
    gram_panel = lax.all_gather(gram_tile, "col", axis=1, tiled=True)
    squared = jnp.dot(
        gram_panel,
        lax.all_gather(gram_tile, "row", axis=0, tiled=True),
        preferred_element_type=jnp.float32,
    )
    factor = (coef_b * gram_tile.astype(jnp.float32) + coef_c * squared).astype(jnp.bfloat16)
    factor_panel = lax.all_gather(factor, "col", axis=1, tiled=True)
    product = jnp.dot(factor_panel, gathered, preferred_element_type=jnp.float32)
    result = coef_a * iterate.astype(jnp.float32) + product
    return (math.sqrt(N) * result).astype(jnp.bfloat16)


def whole():
    return pl.BlockSpec(memory_space=pltpu.VMEM)


def scalars():
    return pl.BlockSpec(memory_space=pltpu.SMEM)


def near_kernel(x, l1, r1, out, both):
    rows = x.shape[0]
    both[:rows, :] = x[...]
    for place, one, other in ((0, l1, r1), (1, r1, l1)):
        both[rows:, :] = other[...]
        for part in (slice(0, rows // 2), slice(rows // 2, rows)):
            value = dot_rows(both[...], one[part, :]).astype(out.dtype)
            out[place, :, part] = value[:rows]
            out[place + 2, :, part] = value[rows:]


def near_blocks(x, l1, r1):
    rows, depth = x.shape
    return pl.pallas_call(
        near_kernel,
        out_shape=jax.ShapeDtypeStruct((4, rows, rows), jnp.bfloat16),
        in_specs=[whole()] * 3,
        out_specs=whole(),
        scratch_shapes=[pltpu.VMEM((2 * rows, depth), jnp.bfloat16)],
        compiler_params=pltpu.CompilerParams(vmem_limit_bytes=52 * 2**20),
        cost_estimate=pl.CostEstimate(
            flops=8 * rows * rows * depth, bytes_accessed=6 * rows * depth, transcendentals=0
        ),
    )(x, l1, r1)


def corner_kernel(place, l1, r1, l2, r2, out, held, sems):
    rows = l1.shape[0]
    marks = [*range(0, rows, 256), rows]
    parts = [slice(a, b) for a, b in zip(marks, marks[1:])]
    for plane, one, other in ((1, r1, l2), (2, l1, r2)):

        @pl.when(place[0] == plane)
        def _(one=one, other=other):
            copies = [pltpu.make_async_copy(one, held.at[0], sems.at[len(parts)])]
            for p, part in enumerate(parts):
                copies.append(
                    pltpu.make_async_copy(other.at[part, :], held.at[1, part, :], sems.at[p])
                )
            for copy in copies:
                copy.start()
            copies[0].wait()
            for part, copy in zip(parts, copies[1:]):
                copy.wait()
                out[0, :, part] = dot_rows(held[0], held[1, part, :]).astype(out.dtype)

    @pl.when(jnp.logical_or(place[0] == 0, place[0] == 3))
    def _():
        out[...] = jnp.zeros_like(out)


def corner_block(place, l1, r1, l2, r2):
    rows, depth = l1.shape
    return pl.pallas_call(
        corner_kernel,
        out_shape=jax.ShapeDtypeStruct((1, rows, rows), jnp.bfloat16),
        in_specs=[scalars()] + [pl.BlockSpec(memory_space=pl.ANY)] * 4,
        out_specs=whole(),
        scratch_shapes=[
            pltpu.VMEM((2, rows, depth), jnp.bfloat16),
            pltpu.SemaphoreType.DMA((pl.cdiv(rows, 256) + 1,)),
        ],
        compiler_params=pltpu.CompilerParams(vmem_limit_bytes=56 * 2**20),
        cost_estimate=pl.CostEstimate(
            flops=128 * rows * rows * depth, bytes_accessed=8 * rows * depth, transcendentals=0
        ),
    )(place, l1, r1, l2, r2)


def strips_kernel(place, own, l1, r3, l2, r2, r1, l3, corner, pair, end, out):
    z = place[0]
    part = own.shape[1]
    at_end = jnp.logical_or(z == 0, z == 3)
    zero = jnp.zeros_like(end[0])
    near = jnp.where(at_end, end[0], corner[0])
    far = jnp.where(at_end, zero, pair[0])
    low = jnp.where(z < 2, near, far)
    high = jnp.where(z < 2, far, near)
    for e in range(4):
        for block in range(4):
            if e == 0:
                value = own[block]
            else:
                one, other = {1: (l1, r3), 2: (l2, r2), 3: (r1, l3)}[e]
                value = one[block] + other[block]
            if block == 3:
                value = value + jnp.where((z + e) % 4 == 0, low, zero)
            if block == 1:
                value = value + jnp.where((z + e) % 4 == 3, high, zero)
            out[(block + e) % 4, e * part : (e + 1) * part, :] = value


def strips(place, *others):
    _, part, rows = others[0].shape
    return pl.pallas_call(
        strips_kernel,
        out_shape=jax.ShapeDtypeStruct((4, 4 * part, rows), jnp.bfloat16),
        in_specs=[scalars()] + [whole()] * len(others),
        out_specs=whole(),
        compiler_params=pltpu.CompilerParams(vmem_limit_bytes=24 * 2**20),
        cost_estimate=pl.CostEstimate(
            flops=16 * part * rows, bytes_accessed=2 * 44 * part * rows, transcendentals=0
        ),
    )(place, *others)


def square_kernel(place, panel, right, out, held, first, sems):
    z = place[0]
    rows, part = panel.shape[1], right.shape[1] // 4
    order = (3, 1, 2, 0)
    copies = {d: pltpu.make_async_copy(panel.at[d], held.at[d], sems.at[d]) for d in order}
    for d in order:
        copies[d].start()
    first[...] = right[0]
    total = jnp.zeros(out.shape, jnp.float32)
    for d in order[:3]:
        copies[d].wait()
        total = total + dot_rows(held[d], right[d])
    for plane, block, e in ((0, 3, 3), (3, 1, 1)):

        @pl.when(z == plane)
        def _(block=block, e=e):
            index = lax.broadcasted_iota(jnp.int32, (part, rows), 0) + place[1] * part
            other = lax.broadcasted_iota(jnp.int32, (part, rows), 1)
            pick = jnp.where(index == other, 1.0, 0.0).astype(jnp.bfloat16)
            far = dot_rows(pick, held[block]).astype(first.dtype)
            first[e * part : (e + 1) * part, :] = right[0, e * part : (e + 1) * part, :] + far

    copies[0].wait()
    total = total + dot_rows(held[0], first[...])
    index = lax.broadcasted_iota(jnp.int32, (rows, rows), 0)
    other = lax.broadcasted_iota(jnp.int32, (rows, rows), 1)
    unit = jnp.where(index == other, 1.0, 0.0).astype(jnp.bfloat16)
    out[...] = (coef_b * dot_rows(unit, first[...]) + coef_c * total).astype(out.dtype)


def square(place, panel, right):
    rows, depth = panel.shape[1], right.shape[1]
    return pl.pallas_call(
        square_kernel,
        out_shape=jax.ShapeDtypeStruct((rows, depth), jnp.bfloat16),
        in_specs=[scalars(), pl.BlockSpec(memory_space=pl.ANY), whole()],
        out_specs=whole(),
        scratch_shapes=[
            pltpu.VMEM(panel.shape, jnp.bfloat16),
            pltpu.VMEM((depth, rows), jnp.bfloat16),
            pltpu.SemaphoreType.DMA((4,)),
        ],
        compiler_params=pltpu.CompilerParams(vmem_limit_bytes=56 * 2**20),
        cost_estimate=pl.CostEstimate(
            flops=2 * rows * rows * 4 * depth, bytes_accessed=2 * 5 * rows * rows, transcendentals=0
        ),
    )(place, panel, right)


def product_kernel(starts, first, place, f, x, l1, r1, across, *rest):
    n_piece = len(starts) - 1
    far = rest[:n_piece]
    out, held_f, whole_f, wide, sems, f_sems = rest[-6:]
    z = place[0]
    n_col, rows, depth = f.shape
    part = depth // 4
    width = out.shape[1]
    step = pl.program_id(0)

    def copy(source, tile, slot, d):
        return pltpu.make_async_copy(
            source.at[:, :, pl.ds(pl.multiple_of(tile * width, width), width)],
            wide.at[slot, :, pl.ds(d * part, part), :],
            sems.at[slot, d],
        )

    def fetch(tile, slot):
        copy(x, first + tile, slot, 0).start()
        copy(across, first + tile, slot, 2).start()
        for d, usual, edge in ((1, l1, 3), (3, r1, 0)):

            @pl.when(z != edge)
            def _(d=d, usual=usual):
                copy(usual, first + tile, slot, d).start()

            for p in range(n_piece):
                inside = jnp.logical_and(tile >= starts[p], tile < starts[p + 1])

                @pl.when(jnp.logical_and(z == edge, inside))
                def _(d=d, piece=far[p], begin=starts[p]):
                    copy(piece, tile - begin, slot, d).start()

    slot = lax.rem(step, 2)

    @pl.when(step == 0)
    def _():
        copies = [pltpu.make_async_copy(f.at[c], held_f.at[c], f_sems.at[c]) for c in range(n_col)]
        for one in copies:
            one.start()
        fetch(0, 0)
        for c in range(n_col):
            copies[c].wait()
            whole_f[:, c * depth : (c + 1) * depth] = held_f[c]

    @pl.when(step + 1 < starts[-1])
    def _():
        fetch(step + 1, 1 - slot)

    for d in range(4):
        copy(x, first + step, slot, d).wait()
    total = jnp.dot(
        whole_f[...],
        wide[slot].reshape(n_col * depth, width),
        preferred_element_type=jnp.float32,
    )
    own = wide[slot, :, :part, :].reshape(rows, width).astype(jnp.float32)
    out[...] = (math.sqrt(N) * (coef_a * own + total)).astype(out.dtype)


def product(place, f, near, far, tile, first, before):
    n_col, rows, depth = f.shape
    part = rows // n_col
    columns = near[0].shape[1]

    def split(value):
        return value.reshape(n_col, part, value.shape[1])

    starts = [0]
    for piece in far:
        starts.append(starts[-1] + piece.shape[1] // tile)

    outside = pl.BlockSpec(memory_space=pl.ANY)
    operands = [place, f, *(split(value) for value in (*near, *far))]
    aliases = {}
    if before is not None:
        aliases = {len(operands): 0}
        operands.append(before)
    share = tile * starts[-1]
    return pl.pallas_call(
        functools.partial(product_kernel, tuple(starts), first),
        grid=(starts[-1],),
        out_shape=jax.ShapeDtypeStruct((rows, columns), jnp.bfloat16),
        in_specs=[scalars()] + [outside] * (len(operands) - 1),
        out_specs=pl.BlockSpec((rows, tile), lambda i: (0, i + first)),
        scratch_shapes=[
            pltpu.VMEM(f.shape, jnp.bfloat16),
            pltpu.VMEM((rows, n_col * depth), jnp.bfloat16),
            pltpu.VMEM((2, n_col, depth, tile), jnp.bfloat16),
            pltpu.SemaphoreType.DMA((2, 4)),
            pltpu.SemaphoreType.DMA((n_col,)),
        ],
        input_output_aliases=aliases,
        compiler_params=pltpu.CompilerParams(vmem_limit_bytes=56 * 2**20),
        cost_estimate=pl.CostEstimate(
            flops=2 * rows * n_col * depth * share if first else 0,
            bytes_accessed=2 * 6 * rows * share if first else 0,
            transcendentals=0,
        ),
    )(*operands)


def arrived_kernel(value, out):
    pass


def arrived(value):
    outside = pl.BlockSpec(memory_space=pl.ANY)
    return pl.pallas_call(
        arrived_kernel,
        out_shape=jax.ShapeDtypeStruct(value.shape, value.dtype),
        in_specs=[outside],
        out_specs=outside,
        input_output_aliases={0: 0},
        cost_estimate=pl.CostEstimate(flops=2 * 10**11, bytes_accessed=0, transcendentals=0),
    )(value)


def per_device_line(n_col, x):
    z = lax.axis_index("row")
    place = jnp.stack([z, lax.axis_index("col")]).astype(jnp.int32)
    right, left = [(0, 1), (1, 2), (2, 3)], [(3, 2), (2, 1), (1, 0)]

    def send(value, pairs):
        return lax.ppermute(value, "row", pairs)

    def scatter(blocks):
        return lax.psum_scatter(blocks, "col", scatter_dimension=1, tiled=True)

    r1, l1 = send(x, right), send(x, left)
    own = scatter(dot_rows(x, x).astype(jnp.bfloat16)[None])
    own, r1, l1 = lax.optimization_barrier((own, r1, l1))
    r2, l2 = send(r1, right[1:]), send(l1, left[1:])

    first = scatter(near_blocks(x, l1, r1))
    corner = corner_block(place, l1, r1, l2, r2)
    corner, first = lax.optimization_barrier((corner, first))
    corner = scatter(corner)

    second = send(first[2], left[1:]) + send(first[3], right[1:])
    tile = jnp.stack([own[0], first[0], second, first[1]])
    tr1, tl1 = send(tile, right), send(tile, left)

    unit = 256
    marks = [0, unit, x.shape[1] - 2 * unit, x.shape[1]]
    across = l2 + r2

    def send_on(p, *after):
        value = lax.optimization_barrier((across, *after))[0]
        return send(value[:, marks[p] : marks[p + 1]], [(1, 0), (2, 3)])

    far = [send_on(0, tile)]
    corner, tr1, tl1, far[0] = lax.optimization_barrier((corner, tr1, tl1, far[0]))
    end = send(corner, [(1, 0), (2, 3)])
    pair = send(corner, [(1, 2), (2, 1)])
    zero = jnp.zeros_like(end)
    added = [zero, jnp.where(z == 3, end, zero), zero, jnp.where(z == 0, end, zero)]
    panel = lax.all_gather(tile + jnp.concatenate(added), "col", axis=1, tiled=True)

    end, tr1, tl1 = lax.optimization_barrier((end, tr1, tl1))
    tr2, tl2 = send(tr1, right[1:]), send(tl1, left[1:])
    tr3, tl3 = send(tr2, right[2:]), send(tl2, left[2:])
    far.append(arrived(send_on(1, tr3, tl3, pair)))

    rights = strips(place, tile, tl1, tr3, tl2, tr2, tr1, tl3, corner, pair, end)
    factor = square(place, panel, rights)
    far.append(send_on(2, factor))
    factor = lax.all_gather(factor, "col", axis=0, tiled=False)
    near = [x, l1, r1, across]
    out = product(place, factor, near, far[:2], unit, 0, None)
    return product(place, factor, near, far[2:], unit, marks[2] // unit, out)


def solution(mesh):
    n_row, n_col = mesh.shape["row"], mesh.shape["col"]

    def body(iterate):
        if (n_row, n_col) == (4, 8) and iterate.shape == (896, 2304):
            return per_device_line(n_col, iterate)
        return per_device(iterate)

    return jax.shard_map(
        body,
        mesh=mesh,
        in_specs=(P("row", "col"),),
        out_specs=P("row", "col"),
        check_vma=False,
    )
```

```python
import functools
import math

import jax
import jax.numpy as jnp
from jax import lax
from jax.experimental import pallas as pl
from jax.experimental.pallas import tpu as pltpu
from jax.sharding import PartitionSpec as P

N = 18432


coef_a = 3.4445
coef_b = -4.775
coef_c = 2.0315


def dot_rows(left, right):
    return lax.dot_general(
        left, right, (((1,), (1,)), ((), ())), preferred_element_type=jnp.float32
    )


def per_device(iterate):
    contract = (((1,), (1,)), ((), ()))
    gathered = lax.all_gather(iterate, "row", axis=0, tiled=True)
    partial_value = lax.dot_general(
        iterate, gathered, contract, preferred_element_type=jnp.float32
    )
    partial_value = partial_value.astype(jnp.bfloat16)
    gram_tile = lax.psum_scatter(partial_value, "col", scatter_dimension=1, tiled=True)
    gram_panel = lax.all_gather(gram_tile, "col", axis=1, tiled=True)
    squared = jnp.dot(
        gram_panel,
        lax.all_gather(gram_tile, "row", axis=0, tiled=True),
        preferred_element_type=jnp.float32,
    )
    factor = (coef_b * gram_tile.astype(jnp.float32) + coef_c * squared).astype(jnp.bfloat16)
    factor_panel = lax.all_gather(factor, "col", axis=1, tiled=True)
    product = jnp.dot(factor_panel, gathered, preferred_element_type=jnp.float32)
    result = coef_a * iterate.astype(jnp.float32) + product
    return (math.sqrt(N) * result).astype(jnp.bfloat16)


def whole():
    return pl.BlockSpec(memory_space=pltpu.VMEM)


def scalars():
    return pl.BlockSpec(memory_space=pltpu.SMEM)


def near_kernel(x, l1, r1, out, both):
    rows = x.shape[0]
    both[:rows, :] = x[...]
    for place, one, other in ((0, l1, r1), (1, r1, l1)):
        both[rows:, :] = other[...]
        value = dot_rows(both[...], one[...]).astype(out.dtype)
        out[place] = value[:rows]
        out[place + 2] = value[rows:]


def near_blocks(x, l1, r1):
    rows, depth = x.shape
    return pl.pallas_call(
        near_kernel,
        out_shape=jax.ShapeDtypeStruct((4, rows, rows), jnp.bfloat16),
        in_specs=[whole()] * 3,
        out_specs=whole(),
        scratch_shapes=[pltpu.VMEM((2 * rows, depth), jnp.bfloat16)],
        compiler_params=pltpu.CompilerParams(vmem_limit_bytes=52 * 2**20),
        cost_estimate=pl.CostEstimate(
            flops=8 * rows * rows * depth, bytes_accessed=6 * rows * depth, transcendentals=0
        ),
    )(x, l1, r1)


def corner_kernel(place, l1, r1, l2, r2, out, held, sems):
    for plane, one, other in ((1, r1, l2), (2, l1, r2)):

        @pl.when(place[0] == plane)
        def _(one=one, other=other):
            copies = [
                pltpu.make_async_copy(one, held.at[0], sems.at[0]),
                pltpu.make_async_copy(other, held.at[1], sems.at[1]),
            ]
            for copy in copies:
                copy.start()
            for copy in copies:
                copy.wait()
            out[0] = dot_rows(held[0], held[1]).astype(out.dtype)

    @pl.when(jnp.logical_or(place[0] == 0, place[0] == 3))
    def _():
        out[...] = jnp.zeros_like(out)


def corner_block(place, l1, r1, l2, r2):
    rows, depth = l1.shape
    return pl.pallas_call(
        corner_kernel,
        out_shape=jax.ShapeDtypeStruct((1, rows, rows), jnp.bfloat16),
        in_specs=[scalars()] + [pl.BlockSpec(memory_space=pl.ANY)] * 4,
        out_specs=whole(),
        scratch_shapes=[pltpu.VMEM((2, rows, depth), jnp.bfloat16), pltpu.SemaphoreType.DMA((2,))],
        compiler_params=pltpu.CompilerParams(vmem_limit_bytes=56 * 2**20),
        cost_estimate=pl.CostEstimate(
            flops=128 * rows * rows * depth, bytes_accessed=8 * rows * depth, transcendentals=0
        ),
    )(place, l1, r1, l2, r2)


def strips_kernel(place, own, l1, r3, l2, r2, r1, l3, corner, pair, end, out):
    z = place[0]
    _, part, rows = own.shape
    at_end = jnp.logical_or(z == 0, z == 3)
    zero = jnp.zeros_like(end[0])
    near = jnp.where(at_end, end[0], corner[0])
    far = jnp.where(at_end, zero, pair[0])
    low = jnp.where(z < 2, near, far)
    high = jnp.where(z < 2, far, near)
    for e in range(4):
        for block in range(4):
            if e == 0:
                value = own[block]
            else:
                one, other = {1: (l1, r3), 2: (l2, r2), 3: (r1, l3)}[e]
                value = one[block] + other[block]
            if block == 3:
                value = value + jnp.where((z + e) % 4 == 0, low, zero)
            if block == 1:
                value = value + jnp.where((z + e) % 4 == 3, high, zero)
            place_of = (block + e) % 4 * rows
            out[e * part : (e + 1) * part, place_of : place_of + rows] = value


def strips(place, *others):
    _, part, rows = others[0].shape
    return pl.pallas_call(
        strips_kernel,
        out_shape=jax.ShapeDtypeStruct((4 * part, 4 * rows), jnp.bfloat16),
        in_specs=[scalars()] + [whole()] * len(others),
        out_specs=whole(),
        compiler_params=pltpu.CompilerParams(vmem_limit_bytes=24 * 2**20),
        cost_estimate=pl.CostEstimate(
            flops=16 * part * rows, bytes_accessed=2 * 44 * part * rows, transcendentals=0
        ),
    )(place, *others)


def square_kernel(place, panel, right, out, held, strip, sems):
    z = place[0]
    rows, part = panel.shape[1], right.shape[0] // 4
    copies = [pltpu.make_async_copy(right, strip, sems.at[4])]
    for d in range(4):
        columns = held.at[:, d * rows : (d + 1) * rows]
        copies.append(pltpu.make_async_copy(panel.at[d], columns, sems.at[d]))
    for copy in copies:
        copy.start()
    for copy in copies:
        copy.wait()
    for plane, block, e in ((0, 3, 3), (3, 1, 1)):

        @pl.when(z == plane)
        def _(block=block, e=e):
            index = lax.broadcasted_iota(jnp.int32, (part, rows), 0) + place[1] * part
            other = lax.broadcasted_iota(jnp.int32, (part, rows), 1)
            pick = jnp.where(index == other, 1.0, 0.0).astype(jnp.bfloat16)
            far = dot_rows(pick, held[:, block * rows : (block + 1) * rows]).astype(strip.dtype)
            strip[e * part : (e + 1) * part, :rows] += far

    total = dot_rows(held[...], strip[...])
    index = lax.broadcasted_iota(jnp.int32, (rows, rows), 0)
    other = lax.broadcasted_iota(jnp.int32, (rows, rows), 1)
    unit = jnp.where(index == other, 1.0, 0.0).astype(jnp.bfloat16)
    out[...] = (coef_b * dot_rows(unit, strip[:, :rows]) + coef_c * total).astype(out.dtype)


def square(place, panel, right):
    rows, depth = panel.shape[1], right.shape[0]
    outside = pl.BlockSpec(memory_space=pl.ANY)
    return pl.pallas_call(
        square_kernel,
        out_shape=jax.ShapeDtypeStruct((rows, depth), jnp.bfloat16),
        in_specs=[scalars(), outside, outside],
        out_specs=whole(),
        scratch_shapes=[
            pltpu.VMEM((rows, 4 * rows), jnp.bfloat16),
            pltpu.VMEM((depth, 4 * rows), jnp.bfloat16),
            pltpu.SemaphoreType.DMA((5,)),
        ],
        compiler_params=pltpu.CompilerParams(vmem_limit_bytes=56 * 2**20),
        cost_estimate=pl.CostEstimate(
            flops=2 * rows * rows * 4 * depth, bytes_accessed=2 * 5 * rows * rows, transcendentals=0
        ),
    )(place, panel, right)


def product_kernel(marks, first, place, f, x, l1, r1, across, *rest):
    far = rest[: len(marks) - 1]
    out, held_f, whole_f, wide, sems, f_sems = rest[-6:]
    z = place[0]
    n_col, rows, depth = f.shape
    part = depth // 4
    width = out.shape[1]
    n_tile = (marks[-1] - marks[0]) // width
    step = pl.program_id(0)

    def copy(source, begin, count, slot, d, offset):
        return pltpu.make_async_copy(
            source.at[:, :, pl.ds(begin, count)],
            wide.at[slot, :, pl.ds(d * part, part), pl.ds(offset, count)],
            sems.at[slot, d],
        )

    def fetch(tile, slot):
        begin = pl.multiple_of(first + tile * width, 128)
        copy(x, begin, width, slot, 0, 0).start()
        copy(across, begin, width, slot, 2, 0).start()
        for d, usual, edge in ((1, l1, 3), (3, r1, 0)):

            @pl.when(z != edge)
            def _(d=d, usual=usual):
                copy(usual, begin, width, slot, d, 0).start()

            for t in range(n_tile):

                @pl.when(jnp.logical_and(z == edge, tile == t))
                def _(d=d, t=t):
                    for piece, low, high in zip(far, marks, marks[1:]):
                        left = max(low, first + t * width)
                        right = min(high, first + (t + 1) * width)
                        if left < right:
                            offset = left - first - t * width
                            copy(piece, left - low, right - left, slot, d, offset).start()

    slot = lax.rem(step, 2)

    @pl.when(step == 0)
    def _():
        copies = [pltpu.make_async_copy(f.at[c], held_f.at[c], f_sems.at[c]) for c in range(n_col)]
        for one in copies:
            one.start()
        fetch(0, 0)
        for c in range(n_col):
            copies[c].wait()
            whole_f[:, c * depth : (c + 1) * depth] = held_f[c]

    @pl.when(step + 1 < n_tile)
    def _():
        fetch(step + 1, 1 - slot)

    for d in range(4):
        copy(x, 0, width, slot, d, 0).wait()
    total = jnp.dot(
        whole_f[...],
        wide[slot].reshape(n_col * depth, width),
        preferred_element_type=jnp.float32,
    )
    own = wide[slot, :, :part, :].reshape(rows, width).astype(jnp.float32)
    out[...] = (math.sqrt(N) * (coef_a * own + total)).astype(out.dtype)


def product(place, f, near, far, tile, marks, before):
    n_col, rows, depth = f.shape
    part = rows // n_col
    columns = near[0].shape[1]
    share = marks[-1] - marks[0]

    def split(value):
        return value.reshape(n_col, part, value.shape[1])

    outside = pl.BlockSpec(memory_space=pl.ANY)
    operands = [place, f, *(split(value) for value in (*near, *far))]
    aliases = {}
    if before is not None:
        aliases = {len(operands): 0}
        operands.append(before)
    return pl.pallas_call(
        functools.partial(product_kernel, tuple(marks), marks[0]),
        grid=(share // tile,),
        out_shape=jax.ShapeDtypeStruct((rows, columns), jnp.bfloat16),
        in_specs=[scalars()] + [outside] * (len(operands) - 1),
        out_specs=pl.BlockSpec((rows, tile), lambda i: (0, i + marks[0] // tile)),
        scratch_shapes=[
            pltpu.VMEM(f.shape, jnp.bfloat16),
            pltpu.VMEM((rows, n_col * depth), jnp.bfloat16),
            pltpu.VMEM((2, n_col, depth, tile), jnp.bfloat16),
            pltpu.SemaphoreType.DMA((2, 4)),
            pltpu.SemaphoreType.DMA((n_col,)),
        ],
        input_output_aliases=aliases,
        compiler_params=pltpu.CompilerParams(vmem_limit_bytes=56 * 2**20),
        cost_estimate=pl.CostEstimate(
            flops=2 * rows * n_col * depth * share if before is not None else 0,
            bytes_accessed=2 * 6 * rows * share if before is not None else 0,
            transcendentals=0,
        ),
    )(*operands)


def arrived_kernel(value, out):
    pass


def arrived(value):
    outside = pl.BlockSpec(memory_space=pl.ANY)
    return pl.pallas_call(
        arrived_kernel,
        out_shape=jax.ShapeDtypeStruct(value.shape, value.dtype),
        in_specs=[outside],
        out_specs=outside,
        input_output_aliases={0: 0},
        cost_estimate=pl.CostEstimate(flops=2 * 10**11, bytes_accessed=0, transcendentals=0),
    )(value)


def per_device_line(n_col, x):
    z = lax.axis_index("row")
    place = jnp.stack([z, lax.axis_index("col")]).astype(jnp.int32)
    right, left = [(0, 1), (1, 2), (2, 3)], [(3, 2), (2, 1), (1, 0)]

    def send(value, pairs):
        return lax.ppermute(value, "row", pairs)

    def scatter(blocks):
        return lax.psum_scatter(blocks, "col", scatter_dimension=1, tiled=True)

    r1, l1 = send(x, right), send(x, left)
    own = scatter(dot_rows(x, x).astype(jnp.bfloat16)[None])
    own, r1, l1 = lax.optimization_barrier((own, r1, l1))
    r2, l2 = send(r1, right[1:]), send(l1, left[1:])

    first = scatter(near_blocks(x, l1, r1))
    corner = corner_block(place, l1, r1, l2, r2)
    corner, first = lax.optimization_barrier((corner, first))
    corner = scatter(corner)

    second = send(first[2], left[1:]) + send(first[3], right[1:])
    tile = jnp.stack([own[0], first[0], second, first[1]])
    tr1, tl1 = send(tile, right), send(tile, left)

    marks = [0, 256, x.shape[1] - 768, x.shape[1]]
    across = l2 + r2

    def send_on(p, *after):
        value = lax.optimization_barrier((across, *after))[0]
        return send(value[:, marks[p] : marks[p + 1]], [(1, 0), (2, 3)])

    far = [send_on(0, tile)]
    corner, tr1, tl1, far[0] = lax.optimization_barrier((corner, tr1, tl1, far[0]))
    end = send(corner, [(1, 0), (2, 3)])
    pair = send(corner, [(1, 2), (2, 1)])
    zero = jnp.zeros_like(end)
    added = [zero, jnp.where(z == 3, end, zero), zero, jnp.where(z == 0, end, zero)]
    panel = lax.all_gather(tile + jnp.concatenate(added), "col", axis=1, tiled=True)

    end, tr1, tl1 = lax.optimization_barrier((end, tr1, tl1))
    tr2, tl2 = send(tr1, right[1:]), send(tl1, left[1:])
    tr3, tl3 = send(tr2, right[2:]), send(tl2, left[2:])
    far.append(arrived(send_on(1, tr3, tl3, pair)))

    rights = strips(place, tile, tl1, tr3, tl2, tr2, tr1, tl3, corner, pair, end)
    factor = square(place, panel, rights)
    far.append(send_on(2, factor))
    factor = lax.all_gather(factor, "col", axis=0, tiled=False)
    near = [x, l1, r1, across]
    out = product(place, factor, near, far[:2], 512, marks[:3], None)
    return product(place, factor, near, far[2:], 768, marks[2:], out)


def solution(mesh):
    n_row, n_col = mesh.shape["row"], mesh.shape["col"]

    def body(iterate):
        if (n_row, n_col) == (4, 8) and iterate.shape == (896, 2304):
            return per_device_line(n_col, iterate)
        return per_device(iterate)

    return jax.shard_map(
        body,
        mesh=mesh,
        in_specs=(P("row", "col"),),
        out_specs=P("row", "col"),
        check_vma=False,
    )
```

```python
import functools
import math

import jax
import jax.numpy as jnp
from jax import lax
from jax.experimental import pallas as pl
from jax.experimental.pallas import tpu as pltpu
from jax.sharding import PartitionSpec as P

N = 18432


coef_a = 3.4445
coef_b = -4.775
coef_c = 2.0315


def dot_rows(left, right):
    return lax.dot_general(
        left, right, (((1,), (1,)), ((), ())), preferred_element_type=jnp.float32
    )


def per_device(iterate):
    contract = (((1,), (1,)), ((), ()))
    gathered = lax.all_gather(iterate, "row", axis=0, tiled=True)
    partial_value = lax.dot_general(
        iterate, gathered, contract, preferred_element_type=jnp.float32
    )
    partial_value = partial_value.astype(jnp.bfloat16)
    gram_tile = lax.psum_scatter(partial_value, "col", scatter_dimension=1, tiled=True)
    gram_panel = lax.all_gather(gram_tile, "col", axis=1, tiled=True)
    squared = jnp.dot(
        gram_panel,
        lax.all_gather(gram_tile, "row", axis=0, tiled=True),
        preferred_element_type=jnp.float32,
    )
    factor = (coef_b * gram_tile.astype(jnp.float32) + coef_c * squared).astype(jnp.bfloat16)
    factor_panel = lax.all_gather(factor, "col", axis=1, tiled=True)
    product = jnp.dot(factor_panel, gathered, preferred_element_type=jnp.float32)
    result = coef_a * iterate.astype(jnp.float32) + product
    return (math.sqrt(N) * result).astype(jnp.bfloat16)


def whole():
    return pl.BlockSpec(memory_space=pltpu.VMEM)


def scalars():
    return pl.BlockSpec(memory_space=pltpu.SMEM)


def load_pieces(pieces, marks, target, sem):
    copies = [
        pltpu.make_async_copy(piece, target.at[:, low:high], sem.at[p])
        for p, (piece, low, high) in enumerate(zip(pieces, marks, marks[1:]))
    ]
    for copy in copies:
        copy.start()
    return copies


def near_kernel(marks, x, *rest):
    n = len(marks) - 1
    l1, r1 = rest[:n], rest[n : 2 * n]
    out, held, sems = rest[2 * n :]
    rows = x.shape[0]
    copies = load_pieces([x], [0, marks[-1]], held.at[rows : 2 * rows], sems.at[0])
    copies += load_pieces(l1, marks, held.at[2 * rows :], sems.at[1])
    copies += load_pieces(r1, marks, held.at[:rows], sems.at[2])
    for copy in copies:
        copy.wait()
    value = dot_rows(held[: 2 * rows], held[2 * rows :]).astype(out.dtype)
    out[2] = value[:rows]
    out[0] = value[rows:]
    value = dot_rows(held[rows:], held[:rows]).astype(out.dtype)
    out[1] = value[:rows]
    out[3] = value[rows:]


def near_blocks(x, l1, r1, marks):
    rows, depth = x.shape
    return pl.pallas_call(
        functools.partial(near_kernel, marks),
        out_shape=jax.ShapeDtypeStruct((4, rows, rows), jnp.bfloat16),
        in_specs=[pl.BlockSpec(memory_space=pl.ANY)] * (1 + len(l1) + len(r1)),
        out_specs=whole(),
        scratch_shapes=[
            pltpu.VMEM((3 * rows, depth), jnp.bfloat16),
            pltpu.SemaphoreType.DMA((3, len(l1))),
        ],
        compiler_params=pltpu.CompilerParams(vmem_limit_bytes=56 * 2**20),
        cost_estimate=pl.CostEstimate(
            flops=8 * rows * rows * depth, bytes_accessed=6 * rows * depth, transcendentals=0
        ),
    )(x, *l1, *r1)


def corner_kernel(marks, place, *rest):
    n = len(marks) - 1
    l1, r1, l2, r2 = (rest[g * n : (g + 1) * n] for g in range(4))
    out, held, sems = rest[4 * n :]
    for plane, one, other in ((1, r1, l2), (2, l1, r2)):

        @pl.when(place[0] == plane)
        def _(one=one, other=other):
            copies = load_pieces(one, marks, held.at[0], sems.at[0])
            copies += load_pieces(other, marks, held.at[1], sems.at[1])
            for copy in copies:
                copy.wait()
            out[0] = dot_rows(held[0], held[1]).astype(out.dtype)

    @pl.when(jnp.logical_or(place[0] == 0, place[0] == 3))
    def _():
        out[...] = jnp.zeros_like(out)


def corner_block(place, l1, r1, l2, r2, marks):
    rows, depth = l1[0].shape[0], marks[-1]
    return pl.pallas_call(
        functools.partial(corner_kernel, marks),
        out_shape=jax.ShapeDtypeStruct((1, rows, rows), jnp.bfloat16),
        in_specs=[scalars()] + [pl.BlockSpec(memory_space=pl.ANY)] * (4 * len(l1)),
        out_specs=whole(),
        scratch_shapes=[
            pltpu.VMEM((2, rows, depth), jnp.bfloat16),
            pltpu.SemaphoreType.DMA((2, len(l1))),
        ],
        compiler_params=pltpu.CompilerParams(vmem_limit_bytes=56 * 2**20),
        cost_estimate=pl.CostEstimate(
            flops=128 * rows * rows * depth, bytes_accessed=8 * rows * depth, transcendentals=0
        ),
    )(place, *l1, *r1, *l2, *r2)


def strips_kernel(place, own, l1, r3, l2, r2, r1, l3, corner, pair, end, out):
    z = place[0]
    _, part, rows = own.shape
    at_end = jnp.logical_or(z == 0, z == 3)
    zero = jnp.zeros_like(end[0])
    near = jnp.where(at_end, end[0], corner[0])
    far = jnp.where(at_end, zero, pair[0])
    low = jnp.where(z < 2, near, far)
    high = jnp.where(z < 2, far, near)
    for e in range(4):
        for block in range(4):
            if e == 0:
                value = own[block]
            else:
                one, other = {1: (l1, r3), 2: (l2, r2), 3: (r1, l3)}[e]
                value = one[block] + other[block]
            if block == 3:
                value = value + jnp.where((z + e) % 4 == 0, low, zero)
            if block == 1:
                value = value + jnp.where((z + e) % 4 == 3, high, zero)
            place_of = (block + e) % 4 * rows
            out[e * part : (e + 1) * part, place_of : place_of + rows] = value


def strips(place, *others):
    _, part, rows = others[0].shape
    return pl.pallas_call(
        strips_kernel,
        out_shape=jax.ShapeDtypeStruct((4 * part, 4 * rows), jnp.bfloat16),
        in_specs=[scalars()] + [whole()] * len(others),
        out_specs=whole(),
        compiler_params=pltpu.CompilerParams(vmem_limit_bytes=24 * 2**20),
        cost_estimate=pl.CostEstimate(
            flops=16 * part * rows, bytes_accessed=2 * 44 * part * rows, transcendentals=0
        ),
    )(place, *others)


def square_kernel(place, panel, right, out, held, strip, sems):
    z = place[0]
    rows, part = panel.shape[1], right.shape[0] // 4
    copies = [pltpu.make_async_copy(right, strip, sems.at[4])]
    for d in range(4):
        columns = held.at[:, d * rows : (d + 1) * rows]
        copies.append(pltpu.make_async_copy(panel.at[d], columns, sems.at[d]))
    for copy in copies:
        copy.start()
    for copy in copies:
        copy.wait()
    for plane, block, e in ((0, 3, 3), (3, 1, 1)):

        @pl.when(z == plane)
        def _(block=block, e=e):
            index = lax.broadcasted_iota(jnp.int32, (part, rows), 0) + place[1] * part
            other = lax.broadcasted_iota(jnp.int32, (part, rows), 1)
            pick = jnp.where(index == other, 1.0, 0.0).astype(jnp.bfloat16)
            far = dot_rows(pick, held[:, block * rows : (block + 1) * rows]).astype(strip.dtype)
            strip[e * part : (e + 1) * part, :rows] += far

    total = dot_rows(held[...], strip[...])
    index = lax.broadcasted_iota(jnp.int32, (rows, rows), 0)
    other = lax.broadcasted_iota(jnp.int32, (rows, rows), 1)
    unit = jnp.where(index == other, 1.0, 0.0).astype(jnp.bfloat16)
    out[...] = (coef_b * dot_rows(unit, strip[:, :rows]) + coef_c * total).astype(out.dtype)


def square(place, panel, right):
    rows, depth = panel.shape[1], right.shape[0]
    outside = pl.BlockSpec(memory_space=pl.ANY)
    return pl.pallas_call(
        square_kernel,
        out_shape=jax.ShapeDtypeStruct((rows, depth), jnp.bfloat16),
        in_specs=[scalars(), outside, outside],
        out_specs=whole(),
        scratch_shapes=[
            pltpu.VMEM((rows, 4 * rows), jnp.bfloat16),
            pltpu.VMEM((depth, 4 * rows), jnp.bfloat16),
            pltpu.SemaphoreType.DMA((5,)),
        ],
        compiler_params=pltpu.CompilerParams(vmem_limit_bytes=56 * 2**20),
        cost_estimate=pl.CostEstimate(
            flops=2 * rows * rows * 4 * depth, bytes_accessed=2 * 5 * rows * rows, transcendentals=0
        ),
    )(place, panel, right)


def product_kernel(marks, ready, place, f, x, *rest):
    l1, r1, across, *rest = rest
    far = rest[: len(marks) - 1]
    rest = rest[len(marks) - 1 + ready :]
    out, whole_f, wide, sems = (rest[0], *rest[-4:-1])
    z = place[0]
    n_col, part, _ = x.shape
    rows, depth = n_col * part, 4 * part
    width = out.shape[1]
    n_tile = (marks[-1] - marks[0]) // width
    step = pl.program_id(0)

    def copy(source, begin, slot, d):
        return pltpu.make_async_copy(
            source.at[:, :, pl.ds(pl.multiple_of(begin, width), width)],
            wide.at[slot, :, pl.ds(d * part, part), :],
            sems.at[slot, d],
        )

    def fetch(tile, slot):
        begin = marks[0] + tile * width
        copy(x, begin, slot, 0).start()
        copy(across, tile * width, slot, 2).start()
        for d, usual, edge in ((1, l1, 3), (3, r1, 0)):

            @pl.when(z != edge)
            def _(d=d, usual=usual):
                copy(usual, tile * width, slot, d).start()

            for piece, low, high in zip(far, marks, marks[1:]):
                inside = jnp.logical_and(begin >= low, begin < high)

                @pl.when(jnp.logical_and(z == edge, inside))
                def _(d=d, piece=piece, low=low):
                    copy(piece, begin - low, slot, d).start()

    slot = lax.rem(step, 2)
    if ready:
        f_sems = rest[-1]
        loads = [pltpu.make_async_copy(f, whole_f, f_sems.at[0])]
    else:
        held_f, f_sems = rest[2], rest[-1]
        loads = [pltpu.make_async_copy(f.at[c], held_f.at[c], f_sems.at[c]) for c in range(n_col)]
        save = pltpu.make_async_copy(whole_f, rest[1], f_sems.at[n_col])

    @pl.when(step == 0)
    def _():
        for one in loads:
            one.start()
        fetch(0, 0)
        if ready:
            loads[0].wait()
        else:
            for c in range(n_col):
                loads[c].wait()
                whole_f[:, c * depth : (c + 1) * depth] = held_f[c]
            save.start()

    @pl.when(step + 1 < n_tile)
    def _():
        fetch(step + 1, 1 - slot)

    for d in range(4):
        copy(x, 0, slot, d).wait()
    total = jnp.dot(
        whole_f[...],
        wide[slot].reshape(n_col * depth, width),
        preferred_element_type=jnp.float32,
    )
    own = wide[slot, :, :part, :].reshape(rows, width).astype(jnp.float32)
    out[...] = (math.sqrt(N) * (coef_a * own + total)).astype(out.dtype)
    if not ready:

        @pl.when(step == n_tile - 1)
        def _():
            save.wait()


def product(place, f, x, near, far, tile, marks, before):
    rows, columns = x.shape
    share = marks[-1] - marks[0]
    ready = before is not None
    n_col = N // columns
    part = rows // n_col
    depth = 4 * part

    def split(value):
        return value.reshape(n_col, part, value.shape[1])

    outside = pl.BlockSpec(memory_space=pl.ANY)
    operands = [place, f, *(split(value) for value in (x, *near, *far))]
    aliases = {}
    out_shape = [jax.ShapeDtypeStruct((rows, columns), jnp.bfloat16)]
    out_specs = [pl.BlockSpec((rows, tile), lambda i: (0, i + marks[0] // tile))]
    scratch = [
        pltpu.VMEM((rows, n_col * depth), jnp.bfloat16),
        pltpu.VMEM((2, n_col, depth, tile), jnp.bfloat16),
        pltpu.SemaphoreType.DMA((2, 4)),
        pltpu.SemaphoreType.DMA((n_col + 1,)),
    ]
    if ready:
        aliases = {len(operands): 0}
        operands.append(before)
    else:
        out_shape.append(jax.ShapeDtypeStruct((rows, n_col * depth), jnp.bfloat16))
        out_specs.append(outside)
        scratch = [pltpu.VMEM(f.shape, jnp.bfloat16), *scratch]
    return pl.pallas_call(
        functools.partial(product_kernel, tuple(marks), ready),
        grid=(share // tile,),
        out_shape=out_shape,
        in_specs=[scalars()] + [outside] * (len(operands) - 1),
        out_specs=out_specs,
        scratch_shapes=scratch,
        input_output_aliases=aliases,
        compiler_params=pltpu.CompilerParams(vmem_limit_bytes=56 * 2**20),
        cost_estimate=pl.CostEstimate(
            flops=2 * rows * n_col * depth * share if ready else 0,
            bytes_accessed=2 * 6 * rows * share if ready else 0,
            transcendentals=0,
        ),
    )(*operands)


def arrived_kernel(value, out):
    pass


def arrived(value):
    outside = pl.BlockSpec(memory_space=pl.ANY)
    return pl.pallas_call(
        arrived_kernel,
        out_shape=jax.ShapeDtypeStruct(value.shape, value.dtype),
        in_specs=[outside],
        out_specs=outside,
        input_output_aliases={0: 0},
        cost_estimate=pl.CostEstimate(flops=2 * 10**11, bytes_accessed=0, transcendentals=0),
    )(value)


def per_device_line(n_col, x):
    z = lax.axis_index("row")
    place = jnp.stack([z, lax.axis_index("col")]).astype(jnp.int32)
    right, left = [(0, 1), (1, 2), (2, 3)], [(3, 2), (2, 1), (1, 0)]

    def send(value, pairs):
        return lax.ppermute(value, "row", pairs)

    def scatter(blocks):
        return lax.psum_scatter(blocks, "col", scatter_dimension=1, tiled=True)

    marks = [0, x.shape[1] - 768, x.shape[1]]
    xs = [x[:, low:high] for low, high in zip(marks, marks[1:])]
    r1 = [send(piece, right) for piece in xs]
    l1 = [send(piece, left) for piece in xs]
    own = scatter(dot_rows(x, x).astype(jnp.bfloat16)[None])
    own, r1[0], l1[0] = lax.optimization_barrier((own, r1[0], l1[0]))
    r2 = [send(piece, right[1:]) for piece in r1]
    l2 = [send(piece, left[1:]) for piece in l1]

    first = scatter(near_blocks(x, l1, r1, marks))
    corner = corner_block(place, l1, r1, l2, r2, marks)
    corner, first = lax.optimization_barrier((corner, first))
    corner = scatter(corner)

    second = send(first[2], left[1:]) + send(first[3], right[1:])
    tile = jnp.stack([own[0], first[0], second, first[1]])
    tr1, tl1 = send(tile, right), send(tile, left)

    across = [a + b for a, b in zip(l2, r2)]
    far_marks = [0, 256, *marks[1:]]

    def send_on(value, *after):
        return send(lax.optimization_barrier((value, *after))[0], [(1, 0), (2, 3)])

    far = [send_on(across[0][:, :256], tile)]
    corner, tr1, tl1, far[0] = lax.optimization_barrier((corner, tr1, tl1, far[0]))
    end = send(corner, [(1, 0), (2, 3)])
    pair = send(corner, [(1, 2), (2, 1)])
    zero = jnp.zeros_like(end)
    added = [zero, jnp.where(z == 3, end, zero), zero, jnp.where(z == 0, end, zero)]
    panel = lax.all_gather(tile + jnp.concatenate(added), "col", axis=1, tiled=True)

    end, tr1, tl1 = lax.optimization_barrier((end, tr1, tl1))
    tr2, tl2 = send(tr1, right[1:]), send(tl1, left[1:])
    tr3, tl3 = send(tr2, right[2:]), send(tl2, left[2:])
    far.append(arrived(send_on(across[0][:, 256:], tr3, tl3, pair)))

    rights = strips(place, tile, tl1, tr3, tl2, tr2, tr1, tl3, corner, pair, end)
    factor = square(place, panel, rights)
    far.append(send_on(across[1], factor))
    factor = lax.all_gather(factor, "col", axis=0, tiled=False)
    near = [l1, r1, across]
    out, factor = product(
        place, factor, x, [group[0] for group in near], far[:2], 256, far_marks[:3], None
    )
    (out,) = product(place, factor, x, [group[1] for group in near], far[2:], 256, marks[1:], out)
    return out


def solution(mesh):
    n_row, n_col = mesh.shape["row"], mesh.shape["col"]

    def body(iterate):
        if (n_row, n_col) == (4, 8) and iterate.shape == (896, 2304):
            return per_device_line(n_col, iterate)
        return per_device(iterate)

    return jax.shard_map(
        body,
        mesh=mesh,
        in_specs=(P("row", "col"),),
        out_specs=P("row", "col"),
        check_vma=False,
    )
```

```python
import functools
import math

import jax
import jax.numpy as jnp
from jax import lax
from jax.experimental import pallas as pl
from jax.experimental.pallas import tpu as pltpu
from jax.sharding import PartitionSpec as P

N = 18432


coef_a = 3.4445
coef_b = -4.775
coef_c = 2.0315


def dot_rows(left, right):
    return lax.dot_general(
        left, right, (((1,), (1,)), ((), ())), preferred_element_type=jnp.float32
    )


def per_device(iterate):
    contract = (((1,), (1,)), ((), ()))
    gathered = lax.all_gather(iterate, "row", axis=0, tiled=True)
    partial_value = lax.dot_general(
        iterate, gathered, contract, preferred_element_type=jnp.float32
    )
    partial_value = partial_value.astype(jnp.bfloat16)
    gram_tile = lax.psum_scatter(partial_value, "col", scatter_dimension=1, tiled=True)
    gram_panel = lax.all_gather(gram_tile, "col", axis=1, tiled=True)
    squared = jnp.dot(
        gram_panel,
        lax.all_gather(gram_tile, "row", axis=0, tiled=True),
        preferred_element_type=jnp.float32,
    )
    factor = (coef_b * gram_tile.astype(jnp.float32) + coef_c * squared).astype(jnp.bfloat16)
    factor_panel = lax.all_gather(factor, "col", axis=1, tiled=True)
    product = jnp.dot(factor_panel, gathered, preferred_element_type=jnp.float32)
    result = coef_a * iterate.astype(jnp.float32) + product
    return (math.sqrt(N) * result).astype(jnp.bfloat16)


def whole():
    return pl.BlockSpec(memory_space=pltpu.VMEM)


def scalars():
    return pl.BlockSpec(memory_space=pltpu.SMEM)


def load_pieces(pieces, marks, target, sem):
    copies = [
        pltpu.make_async_copy(piece, target.at[:, low:high], sem.at[p])
        for p, (piece, low, high) in enumerate(zip(pieces, marks, marks[1:]))
    ]
    for copy in copies:
        copy.start()
    return copies


def near_kernel(marks, x, *rest):
    n = len(marks) - 1
    l1, r1 = rest[:n], rest[n : 2 * n]
    out, held, sems = rest[2 * n :]
    rows = x.shape[0]
    copies = load_pieces([x], [0, marks[-1]], held.at[rows : 2 * rows], sems.at[0])
    copies += load_pieces(l1, marks, held.at[2 * rows :], sems.at[1])
    copies += load_pieces(r1, marks, held.at[:rows], sems.at[2])
    for copy in copies:
        copy.wait()
    value = dot_rows(held[: 2 * rows], held[2 * rows :]).astype(out.dtype)
    out[2] = value[:rows]
    out[0] = value[rows:]
    value = dot_rows(held[rows:], held[:rows]).astype(out.dtype)
    out[1] = value[:rows]
    out[3] = value[rows:]


def near_blocks(x, l1, r1, marks):
    rows, depth = x.shape
    return pl.pallas_call(
        functools.partial(near_kernel, marks),
        out_shape=jax.ShapeDtypeStruct((4, rows, rows), jnp.bfloat16),
        in_specs=[pl.BlockSpec(memory_space=pl.ANY)] * (1 + len(l1) + len(r1)),
        out_specs=whole(),
        scratch_shapes=[
            pltpu.VMEM((3 * rows, depth), jnp.bfloat16),
            pltpu.SemaphoreType.DMA((3, len(l1))),
        ],
        compiler_params=pltpu.CompilerParams(vmem_limit_bytes=56 * 2**20),
        cost_estimate=pl.CostEstimate(
            flops=8 * rows * rows * depth, bytes_accessed=6 * rows * depth, transcendentals=0
        ),
    )(x, *l1, *r1)


def corner_kernel(marks, place, *rest):
    n = len(marks) - 1
    l1, r1, l2, r2 = (rest[g * n : (g + 1) * n] for g in range(4))
    out, held, sems = rest[4 * n :]
    for plane, one, other in ((1, r1, l2), (2, l1, r2)):

        @pl.when(place[0] == plane)
        def _(one=one, other=other):
            copies = load_pieces(one, marks, held.at[0], sems.at[0])
            copies += load_pieces(other, marks, held.at[1], sems.at[1])
            for copy in copies:
                copy.wait()
            out[0] = dot_rows(held[0], held[1]).astype(out.dtype)

    @pl.when(jnp.logical_or(place[0] == 0, place[0] == 3))
    def _():
        out[...] = jnp.zeros_like(out)


def corner_block(place, l1, r1, l2, r2, marks):
    rows, depth = l1[0].shape[0], marks[-1]
    return pl.pallas_call(
        functools.partial(corner_kernel, marks),
        out_shape=jax.ShapeDtypeStruct((1, rows, rows), jnp.bfloat16),
        in_specs=[scalars()] + [pl.BlockSpec(memory_space=pl.ANY)] * (4 * len(l1)),
        out_specs=whole(),
        scratch_shapes=[
            pltpu.VMEM((2, rows, depth), jnp.bfloat16),
            pltpu.SemaphoreType.DMA((2, len(l1))),
        ],
        compiler_params=pltpu.CompilerParams(vmem_limit_bytes=56 * 2**20),
        cost_estimate=pl.CostEstimate(
            flops=128 * rows * rows * depth, bytes_accessed=8 * rows * depth, transcendentals=0
        ),
    )(place, *l1, *r1, *l2, *r2)


def strips_kernel(place, own, l1, r3, l2, r2, r1, l3, corner, pair, end, out, linear):
    z = place[0]
    _, part, rows = own.shape
    at_end = jnp.logical_or(z == 0, z == 3)
    zero = jnp.zeros_like(end[0])
    near = jnp.where(at_end, end[0], corner[0])
    far = jnp.where(at_end, zero, pair[0])
    low = jnp.where(z < 2, near, far)
    high = jnp.where(z < 2, far, near)
    for e in range(4):
        for block in range(4):
            if e == 0:
                value = own[block]
            else:
                one, other = {1: (l1, r3), 2: (l2, r2), 3: (r1, l3)}[e]
                value = one[block] + other[block]
            if block == 3:
                value = value + jnp.where((z + e) % 4 == 0, low, zero)
            if block == 1:
                value = value + jnp.where((z + e) % 4 == 3, high, zero)
            place_of = (block + e) % 4 * rows
            out[e * part : (e + 1) * part, place_of : place_of + rows] = value
    index = lax.broadcasted_iota(jnp.int32, (rows, rows), 0)
    other = lax.broadcasted_iota(jnp.int32, (rows, rows), 1)
    unit = jnp.where(index == other, 1.0, 0.0).astype(jnp.bfloat16)
    linear[...] = dot_rows(unit, out[:, :rows]).astype(linear.dtype)


def strips(place, *others):
    _, part, rows = others[0].shape
    return pl.pallas_call(
        strips_kernel,
        out_shape=[
            jax.ShapeDtypeStruct((4 * part, 4 * rows), jnp.bfloat16),
            jax.ShapeDtypeStruct((rows, 4 * part), jnp.bfloat16),
        ],
        in_specs=[scalars()] + [whole()] * len(others),
        out_specs=[whole(), whole()],
        compiler_params=pltpu.CompilerParams(vmem_limit_bytes=56 * 2**20),
        cost_estimate=pl.CostEstimate(
            flops=16 * part * rows, bytes_accessed=2 * 44 * part * rows, transcendentals=0
        ),
    )(place, *others)


def square_kernel(place, panel, right, linear, out, held, strip, line, sems):
    z = place[0]
    rows, part = panel.shape[1], right.shape[0] // 4
    copies = [
        pltpu.make_async_copy(right, strip, sems.at[4]),
        pltpu.make_async_copy(linear, line, sems.at[5]),
    ]
    for d in range(4):
        columns = held.at[:, d * rows : (d + 1) * rows]
        copies.append(pltpu.make_async_copy(panel.at[d], columns, sems.at[d]))
    for copy in copies:
        copy.start()
    for copy in copies:
        copy.wait()
    for plane, block, e in ((0, 3, 3), (3, 1, 1)):

        @pl.when(z == plane)
        def _(block=block, e=e):
            index = lax.broadcasted_iota(jnp.int32, (part, rows), 0) + place[1] * part
            other = lax.broadcasted_iota(jnp.int32, (part, rows), 1)
            pick = jnp.where(index == other, 1.0, 0.0).astype(jnp.bfloat16)
            corner = held[:, block * rows : (block + 1) * rows]
            here = slice(e * part, (e + 1) * part)
            strip[here, :rows] += dot_rows(pick, corner).astype(strip.dtype)
            line[:, here] += dot_rows(corner, pick).astype(line.dtype)

    total = dot_rows(held[...], strip[...])
    out[...] = (coef_b * line[...].astype(jnp.float32) + coef_c * total).astype(out.dtype)


def square(place, panel, right, linear):
    rows, depth = panel.shape[1], right.shape[0]
    outside = pl.BlockSpec(memory_space=pl.ANY)
    return pl.pallas_call(
        square_kernel,
        out_shape=jax.ShapeDtypeStruct((rows, depth), jnp.bfloat16),
        in_specs=[scalars(), outside, outside, outside],
        out_specs=whole(),
        scratch_shapes=[
            pltpu.VMEM((rows, 4 * rows), jnp.bfloat16),
            pltpu.VMEM((depth, 4 * rows), jnp.bfloat16),
            pltpu.VMEM((rows, depth), jnp.bfloat16),
            pltpu.SemaphoreType.DMA((6,)),
        ],
        compiler_params=pltpu.CompilerParams(vmem_limit_bytes=56 * 2**20),
        cost_estimate=pl.CostEstimate(
            flops=2 * rows * rows * 4 * depth, bytes_accessed=2 * 5 * rows * rows, transcendentals=0
        ),
    )(place, panel, right, linear)


def product_kernel(marks, ready, place, f, x, *rest):
    l1, r1, across, *rest = rest
    far = rest[: len(marks) - 1]
    rest = rest[len(marks) - 1 + ready :]
    out, whole_f, wide, sems = (rest[0], *rest[-4:-1])
    z = place[0]
    n_col, part, _ = x.shape
    rows, depth = n_col * part, 4 * part
    width = out.shape[1]
    n_tile = (marks[-1] - marks[0]) // width
    step = pl.program_id(0)

    def copy(source, begin, slot, d):
        return pltpu.make_async_copy(
            source.at[:, :, pl.ds(pl.multiple_of(begin, width), width)],
            wide.at[slot, :, pl.ds(d * part, part), :],
            sems.at[slot, d],
        )

    def fetch(tile, slot):
        begin = marks[0] + tile * width
        copy(x, begin, slot, 0).start()
        copy(across, tile * width, slot, 2).start()
        for d, usual, edge in ((1, l1, 3), (3, r1, 0)):

            @pl.when(z != edge)
            def _(d=d, usual=usual):
                copy(usual, tile * width, slot, d).start()

            for piece, low, high in zip(far, marks, marks[1:]):
                inside = jnp.logical_and(begin >= low, begin < high)

                @pl.when(jnp.logical_and(z == edge, inside))
                def _(d=d, piece=piece, low=low):
                    copy(piece, begin - low, slot, d).start()

    slot = lax.rem(step, 2)
    if ready:
        f_sems = rest[-1]
        loads = [pltpu.make_async_copy(f, whole_f, f_sems.at[0])]
    else:
        held_f, f_sems = rest[2], rest[-1]
        loads = [pltpu.make_async_copy(f.at[c], held_f.at[c], f_sems.at[c]) for c in range(n_col)]
        save = pltpu.make_async_copy(whole_f, rest[1], f_sems.at[n_col])

    @pl.when(step == 0)
    def _():
        for one in loads:
            one.start()
        fetch(0, 0)
        if ready:
            loads[0].wait()
        else:
            for c in range(n_col):
                loads[c].wait()
                whole_f[:, c * depth : (c + 1) * depth] = held_f[c]
            save.start()

    @pl.when(step + 1 < n_tile)
    def _():
        fetch(step + 1, 1 - slot)

    for d in range(4):
        copy(x, 0, slot, d).wait()
    total = jnp.dot(
        whole_f[...],
        wide[slot].reshape(n_col * depth, width),
        preferred_element_type=jnp.float32,
    )
    own = wide[slot, :, :part, :].reshape(rows, width).astype(jnp.float32)
    out[...] = (math.sqrt(N) * (coef_a * own + total)).astype(out.dtype)
    if not ready:

        @pl.when(step == n_tile - 1)
        def _():
            save.wait()


def product(place, f, x, near, far, tile, marks, before):
    rows, columns = x.shape
    share = marks[-1] - marks[0]
    ready = before is not None
    n_col = N // columns
    part = rows // n_col
    depth = 4 * part

    def split(value):
        return value.reshape(n_col, part, value.shape[1])

    outside = pl.BlockSpec(memory_space=pl.ANY)
    operands = [place, f, *(split(value) for value in (x, *near, *far))]
    aliases = {}
    out_shape = [jax.ShapeDtypeStruct((rows, columns), jnp.bfloat16)]
    out_specs = [pl.BlockSpec((rows, tile), lambda i: (0, i + marks[0] // tile))]
    scratch = [
        pltpu.VMEM((rows, n_col * depth), jnp.bfloat16),
        pltpu.VMEM((2, n_col, depth, tile), jnp.bfloat16),
        pltpu.SemaphoreType.DMA((2, 4)),
        pltpu.SemaphoreType.DMA((n_col + 1,)),
    ]
    if ready:
        aliases = {len(operands): 0}
        operands.append(before)
    else:
        out_shape.append(jax.ShapeDtypeStruct((rows, n_col * depth), jnp.bfloat16))
        out_specs.append(outside)
        scratch = [pltpu.VMEM(f.shape, jnp.bfloat16), *scratch]
    return pl.pallas_call(
        functools.partial(product_kernel, tuple(marks), ready),
        grid=(share // tile,),
        out_shape=out_shape,
        in_specs=[scalars()] + [outside] * (len(operands) - 1),
        out_specs=out_specs,
        scratch_shapes=scratch,
        input_output_aliases=aliases,
        compiler_params=pltpu.CompilerParams(vmem_limit_bytes=56 * 2**20),
        cost_estimate=pl.CostEstimate(
            flops=2 * rows * n_col * depth * share if ready else 0,
            bytes_accessed=2 * 6 * rows * share if ready else 0,
            transcendentals=0,
        ),
    )(*operands)


def arrived_kernel(value, out):
    pass


def arrived(value):
    outside = pl.BlockSpec(memory_space=pl.ANY)
    return pl.pallas_call(
        arrived_kernel,
        out_shape=jax.ShapeDtypeStruct(value.shape, value.dtype),
        in_specs=[outside],
        out_specs=outside,
        input_output_aliases={0: 0},
        cost_estimate=pl.CostEstimate(flops=2 * 10**11, bytes_accessed=0, transcendentals=0),
    )(value)


def per_device_line(n_col, x):
    z = lax.axis_index("row")
    place = jnp.stack([z, lax.axis_index("col")]).astype(jnp.int32)
    right, left = [(0, 1), (1, 2), (2, 3)], [(3, 2), (2, 1), (1, 0)]

    def send(value, pairs):
        return lax.ppermute(value, "row", pairs)

    def scatter(blocks):
        return lax.psum_scatter(blocks, "col", scatter_dimension=1, tiled=True)

    marks = [0, x.shape[1] - 768, x.shape[1]]
    xs = [x[:, low:high] for low, high in zip(marks, marks[1:])]
    r1 = [send(piece, right) for piece in xs]
    l1 = [send(piece, left) for piece in xs]
    own = scatter(dot_rows(x, x).astype(jnp.bfloat16)[None])
    own, r1[0], l1[0] = lax.optimization_barrier((own, r1[0], l1[0]))
    r2 = [send(piece, right[1:]) for piece in r1]
    l2 = [send(piece, left[1:]) for piece in l1]

    first = scatter(near_blocks(x, l1, r1, marks))
    corner = corner_block(place, l1, r1, l2, r2, marks)
    corner, first = lax.optimization_barrier((corner, first))
    shares = lax.all_to_all(corner.reshape(n_col, -1, corner.shape[2]), "col", 0, 0)
    corner = shares.astype(jnp.float32).sum(0, keepdims=True).astype(jnp.bfloat16)

    second = send(first[2], left[1:]) + send(first[3], right[1:])
    tile = jnp.stack([own[0], first[0], second, first[1]])
    tr1, tl1 = send(tile, right), send(tile, left)

    across = [a + b for a, b in zip(l2, r2)]
    far_marks = [0, 256, *marks[1:]]

    def send_on(value, *after):
        return send(lax.optimization_barrier((value, *after))[0], [(1, 0), (2, 3)])

    end = send(corner, [(1, 0), (2, 3)])
    pair = send(corner, [(1, 2), (2, 1)])
    zero = jnp.zeros_like(end)
    added = [zero, jnp.where(z == 3, end, zero), zero, jnp.where(z == 0, end, zero)]
    panel = lax.all_gather(tile + jnp.concatenate(added), "col", axis=1, tiled=True)

    far = [send_on(across[0][:, :256], end)]
    pair, far[0] = lax.optimization_barrier((pair, far[0]))
    end, tr1, tl1 = lax.optimization_barrier((end, tr1, tl1))
    tr2, tl2 = send(tr1, right[1:]), send(tl1, left[1:])
    tr3, tl3 = send(tr2, right[2:]), send(tl2, left[2:])
    far.append(arrived(send_on(across[0][:, 256:], tr3, tl3, pair)))

    strip, linear = strips(place, tile, tl1, tr3, tl2, tr2, tr1, tl3, corner, pair, end)
    factor = square(place, panel, strip, linear)
    far.append(send_on(across[1], factor))
    factor = lax.all_gather(factor, "col", axis=0, tiled=False)
    near = [l1, r1, across]
    out, factor = product(
        place, factor, x, [group[0] for group in near], far[:2], 256, far_marks[:3], None
    )
    (out,) = product(place, factor, x, [group[1] for group in near], far[2:], 256, marks[1:], out)
    return out


def solution(mesh):
    n_row, n_col = mesh.shape["row"], mesh.shape["col"]

    def body(iterate):
        if (n_row, n_col) == (4, 8) and iterate.shape == (896, 2304):
            return per_device_line(n_col, iterate)
        return per_device(iterate)

    return jax.shard_map(
        body,
        mesh=mesh,
        in_specs=(P("row", "col"),),
        out_specs=P("row", "col"),
        check_vma=False,
    )
```

```python
import functools
import math

import jax
import jax.numpy as jnp
from jax import lax
from jax.experimental import pallas as pl
from jax.experimental.pallas import tpu as pltpu
from jax.sharding import PartitionSpec as P

N = 18432


coef_a = 3.4445
coef_b = -4.775
coef_c = 2.0315


def dot_rows(left, right):
    return lax.dot_general(
        left, right, (((1,), (1,)), ((), ())), preferred_element_type=jnp.float32
    )


def per_device(iterate):
    contract = (((1,), (1,)), ((), ()))
    gathered = lax.all_gather(iterate, "row", axis=0, tiled=True)
    partial_value = lax.dot_general(
        iterate, gathered, contract, preferred_element_type=jnp.float32
    )
    partial_value = partial_value.astype(jnp.bfloat16)
    gram_tile = lax.psum_scatter(partial_value, "col", scatter_dimension=1, tiled=True)
    gram_panel = lax.all_gather(gram_tile, "col", axis=1, tiled=True)
    squared = jnp.dot(
        gram_panel,
        lax.all_gather(gram_tile, "row", axis=0, tiled=True),
        preferred_element_type=jnp.float32,
    )
    factor = (coef_b * gram_tile.astype(jnp.float32) + coef_c * squared).astype(jnp.bfloat16)
    factor_panel = lax.all_gather(factor, "col", axis=1, tiled=True)
    product = jnp.dot(factor_panel, gathered, preferred_element_type=jnp.float32)
    result = coef_a * iterate.astype(jnp.float32) + product
    return (math.sqrt(N) * result).astype(jnp.bfloat16)


def whole():
    return pl.BlockSpec(memory_space=pltpu.VMEM)


def scalars():
    return pl.BlockSpec(memory_space=pltpu.SMEM)


def load_pieces(pieces, marks, target, sem):
    copies = [
        pltpu.make_async_copy(piece, target.at[:, low:high], sem.at[p])
        for p, (piece, low, high) in enumerate(zip(pieces, marks, marks[1:]))
    ]
    for copy in copies:
        copy.start()
    return copies


def near_kernel(marks, x, *rest):
    n = len(marks) - 1
    l1, r1 = rest[:n], rest[n : 2 * n]
    out, held, sems = rest[2 * n :]
    rows = x.shape[0]
    copies = load_pieces([x], [0, marks[-1]], held.at[rows : 2 * rows], sems.at[0])
    copies += load_pieces(l1, marks, held.at[2 * rows :], sems.at[1])
    copies += load_pieces(r1, marks, held.at[:rows], sems.at[2])
    for copy in copies:
        copy.wait()
    value = dot_rows(held[: 2 * rows], held[2 * rows :]).astype(out.dtype)
    out[2] = value[:rows]
    out[0] = value[rows:]
    value = dot_rows(held[rows:], held[:rows]).astype(out.dtype)
    out[1] = value[:rows]
    out[3] = value[rows:]


def near_blocks(x, l1, r1, marks):
    rows, depth = x.shape
    return pl.pallas_call(
        functools.partial(near_kernel, marks),
        out_shape=jax.ShapeDtypeStruct((4, rows, rows), jnp.bfloat16),
        in_specs=[pl.BlockSpec(memory_space=pl.ANY)] * (1 + len(l1) + len(r1)),
        out_specs=whole(),
        scratch_shapes=[
            pltpu.VMEM((3 * rows, depth), jnp.bfloat16),
            pltpu.SemaphoreType.DMA((3, len(l1))),
        ],
        compiler_params=pltpu.CompilerParams(vmem_limit_bytes=56 * 2**20),
        cost_estimate=pl.CostEstimate(
            flops=8 * rows * rows * depth, bytes_accessed=6 * rows * depth, transcendentals=0
        ),
    )(x, *l1, *r1)


def corner_kernel(marks, place, *rest):
    n = len(marks) - 1
    l1, r1, l2, r2 = (rest[g * n : (g + 1) * n] for g in range(4))
    out, held, sems = rest[4 * n :]
    for plane, one, other in ((1, r1, l2), (2, l1, r2)):

        @pl.when(place[0] == plane)
        def _(one=one, other=other):
            copies = load_pieces(one, marks, held.at[0], sems.at[0])
            copies += load_pieces(other, marks, held.at[1], sems.at[1])
            for copy in copies:
                copy.wait()
            out[0] = dot_rows(held[0], held[1]).astype(out.dtype)

    @pl.when(jnp.logical_or(place[0] == 0, place[0] == 3))
    def _():
        out[...] = jnp.zeros_like(out)


def corner_block(place, l1, r1, l2, r2, marks):
    rows, depth = l1[0].shape[0], marks[-1]
    return pl.pallas_call(
        functools.partial(corner_kernel, marks),
        out_shape=jax.ShapeDtypeStruct((1, rows, rows), jnp.bfloat16),
        in_specs=[scalars()] + [pl.BlockSpec(memory_space=pl.ANY)] * (4 * len(l1)),
        out_specs=whole(),
        scratch_shapes=[
            pltpu.VMEM((2, rows, depth), jnp.bfloat16),
            pltpu.SemaphoreType.DMA((2, len(l1))),
        ],
        compiler_params=pltpu.CompilerParams(vmem_limit_bytes=56 * 2**20),
        cost_estimate=pl.CostEstimate(
            flops=128 * rows * rows * depth, bytes_accessed=8 * rows * depth, transcendentals=0
        ),
    )(place, *l1, *r1, *l2, *r2)


def strips_kernel(place, own, l1, r3, l2, r2, r1, l3, corner, pair, end, out):
    z = place[0]
    _, part, rows = own.shape
    at_end = jnp.logical_or(z == 0, z == 3)
    zero = jnp.zeros_like(end[0])
    near = jnp.where(at_end, end[0], corner[0])
    far = jnp.where(at_end, zero, pair[0])
    low = jnp.where(z < 2, near, far)
    high = jnp.where(z < 2, far, near)
    for e in range(4):
        for block in range(4):
            if e == 0:
                value = own[block]
            else:
                one, other = {1: (l1, r3), 2: (l2, r2), 3: (r1, l3)}[e]
                value = one[block] + other[block]
            if block == 3:
                value = value + jnp.where((z + e) % 4 == 0, low, zero)
            if block == 1:
                value = value + jnp.where((z + e) % 4 == 3, high, zero)
            place_of = (block + e) % 4 * rows
            out[e * part : (e + 1) * part, place_of : place_of + rows] = value


def strips(place, *others):
    _, part, rows = others[0].shape
    return pl.pallas_call(
        strips_kernel,
        out_shape=jax.ShapeDtypeStruct((4 * part, 4 * rows), jnp.bfloat16),
        in_specs=[scalars()] + [whole()] * len(others),
        out_specs=whole(),
        compiler_params=pltpu.CompilerParams(vmem_limit_bytes=56 * 2**20),
        cost_estimate=pl.CostEstimate(
            flops=16 * part * rows, bytes_accessed=2 * 44 * part * rows, transcendentals=0
        ),
    )(place, *others)


def square_kernel(place, panel, right, out, held, strip, sems):
    z = place[0]
    rows, part = panel.shape[1], right.shape[0] // 4
    copies = [pltpu.make_async_copy(right, strip, sems.at[4])]
    for d in range(4):
        columns = held.at[:, d * rows : (d + 1) * rows]
        copies.append(pltpu.make_async_copy(panel.at[d], columns, sems.at[d]))
    for copy in copies:
        copy.start()
    for copy in copies:
        copy.wait()
    for plane, block, e in ((0, 3, 3), (3, 1, 1)):

        @pl.when(z == plane)
        def _(block=block, e=e):
            index = lax.broadcasted_iota(jnp.int32, (part, rows), 0) + place[1] * part
            other = lax.broadcasted_iota(jnp.int32, (part, rows), 1)
            pick = jnp.where(index == other, 1.0, 0.0).astype(jnp.bfloat16)
            far = dot_rows(pick, held[:, block * rows : (block + 1) * rows]).astype(strip.dtype)
            strip[e * part : (e + 1) * part, :rows] += far

    total = dot_rows(held[...], strip[...])
    index = lax.broadcasted_iota(jnp.int32, (rows, rows), 0)
    other = lax.broadcasted_iota(jnp.int32, (rows, rows), 1)
    unit = jnp.where(index == other, 1.0, 0.0).astype(jnp.bfloat16)
    out[...] = (coef_b * dot_rows(unit, strip[:, :rows]) + coef_c * total).astype(out.dtype)


def square(place, panel, right):
    rows, depth = panel.shape[1], right.shape[0]
    outside = pl.BlockSpec(memory_space=pl.ANY)
    return pl.pallas_call(
        square_kernel,
        out_shape=jax.ShapeDtypeStruct((rows, depth), jnp.bfloat16),
        in_specs=[scalars(), outside, outside],
        out_specs=whole(),
        scratch_shapes=[
            pltpu.VMEM((rows, 4 * rows), jnp.bfloat16),
            pltpu.VMEM((depth, 4 * rows), jnp.bfloat16),
            pltpu.SemaphoreType.DMA((5,)),
        ],
        compiler_params=pltpu.CompilerParams(vmem_limit_bytes=56 * 2**20),
        cost_estimate=pl.CostEstimate(
            flops=2 * rows * rows * 4 * depth, bytes_accessed=2 * 5 * rows * rows, transcendentals=0
        ),
    )(place, panel, right)


def product_kernel(marks, ready, place, f, x, *rest):
    l1, r1, across, *rest = rest
    far = rest[: len(marks) - 1]
    rest = rest[len(marks) - 1 + ready :]
    out, whole_f, wide, sems = (rest[0], *rest[-4:-1])
    z = place[0]
    n_col, part, _ = x.shape
    rows, depth = n_col * part, 4 * part
    width = out.shape[1]
    n_tile = (marks[-1] - marks[0]) // width
    step = pl.program_id(0)

    def copy(source, begin, slot, d):
        return pltpu.make_async_copy(
            source.at[:, :, pl.ds(pl.multiple_of(begin, width), width)],
            wide.at[slot, :, pl.ds(d * part, part), :],
            sems.at[slot, d],
        )

    def fetch(tile, slot):
        begin = marks[0] + tile * width
        copy(x, begin, slot, 0).start()
        copy(across, tile * width, slot, 2).start()
        for d, usual, edge in ((1, l1, 3), (3, r1, 0)):

            @pl.when(z != edge)
            def _(d=d, usual=usual):
                copy(usual, tile * width, slot, d).start()

            for piece, low, high in zip(far, marks, marks[1:]):
                inside = jnp.logical_and(begin >= low, begin < high)

                @pl.when(jnp.logical_and(z == edge, inside))
                def _(d=d, piece=piece, low=low):
                    copy(piece, begin - low, slot, d).start()

    slot = lax.rem(step, 2)
    if ready:
        f_sems = rest[-1]
        loads = [pltpu.make_async_copy(f, whole_f, f_sems.at[0])]
    else:
        held_f, f_sems = rest[2], rest[-1]
        loads = [pltpu.make_async_copy(f.at[c], held_f.at[c], f_sems.at[c]) for c in range(n_col)]
        save = pltpu.make_async_copy(whole_f, rest[1], f_sems.at[n_col])

    @pl.when(step == 0)
    def _():
        for one in loads:
            one.start()
        fetch(0, 0)
        if ready:
            loads[0].wait()
        else:
            for c in range(n_col):
                loads[c].wait()
                whole_f[:, c * depth : (c + 1) * depth] = held_f[c]
            save.start()

    @pl.when(step + 1 < n_tile)
    def _():
        fetch(step + 1, 1 - slot)

    for d in range(4):
        copy(x, 0, slot, d).wait()
    total = jnp.dot(
        whole_f[...],
        wide[slot].reshape(n_col * depth, width),
        preferred_element_type=jnp.float32,
    )
    own = wide[slot, :, :part, :].reshape(rows, width).astype(jnp.float32)
    out[...] = (math.sqrt(N) * (coef_a * own + total)).astype(out.dtype)
    if not ready:

        @pl.when(step == n_tile - 1)
        def _():
            save.wait()


def product(place, f, x, near, far, tile, marks, before):
    rows, columns = x.shape
    share = marks[-1] - marks[0]
    ready = before is not None
    n_col = N // columns
    part = rows // n_col
    depth = 4 * part

    def split(value):
        return value.reshape(n_col, part, value.shape[1])

    outside = pl.BlockSpec(memory_space=pl.ANY)
    operands = [place, f, *(split(value) for value in (x, *near, *far))]
    aliases = {}
    out_shape = [jax.ShapeDtypeStruct((rows, columns), jnp.bfloat16)]
    out_specs = [pl.BlockSpec((rows, tile), lambda i: (0, i + marks[0] // tile))]
    scratch = [
        pltpu.VMEM((rows, n_col * depth), jnp.bfloat16),
        pltpu.VMEM((2, n_col, depth, tile), jnp.bfloat16),
        pltpu.SemaphoreType.DMA((2, 4)),
        pltpu.SemaphoreType.DMA((n_col + 1,)),
    ]
    if ready:
        aliases = {len(operands): 0}
        operands.append(before)
    else:
        out_shape.append(jax.ShapeDtypeStruct((rows, n_col * depth), jnp.bfloat16))
        out_specs.append(outside)
        scratch = [pltpu.VMEM(f.shape, jnp.bfloat16), *scratch]
    return pl.pallas_call(
        functools.partial(product_kernel, tuple(marks), ready),
        grid=(share // tile,),
        out_shape=out_shape,
        in_specs=[scalars()] + [outside] * (len(operands) - 1),
        out_specs=out_specs,
        scratch_shapes=scratch,
        input_output_aliases=aliases,
        compiler_params=pltpu.CompilerParams(vmem_limit_bytes=56 * 2**20),
        cost_estimate=pl.CostEstimate(
            flops=2 * rows * n_col * depth * share if ready else 0,
            bytes_accessed=2 * 6 * rows * share if ready else 0,
            transcendentals=0,
        ),
    )(*operands)


def arrived_kernel(value, out):
    pass


def arrived(value):
    outside = pl.BlockSpec(memory_space=pl.ANY)
    return pl.pallas_call(
        arrived_kernel,
        out_shape=jax.ShapeDtypeStruct(value.shape, value.dtype),
        in_specs=[outside],
        out_specs=outside,
        input_output_aliases={0: 0},
        cost_estimate=pl.CostEstimate(flops=2 * 10**11, bytes_accessed=0, transcendentals=0),
    )(value)


def per_device_line(n_col, x):
    z = lax.axis_index("row")
    place = jnp.stack([z, lax.axis_index("col")]).astype(jnp.int32)
    right, left = [(0, 1), (1, 2), (2, 3)], [(3, 2), (2, 1), (1, 0)]

    def send(value, pairs):
        return lax.ppermute(value, "row", pairs)

    def scatter(blocks):
        return lax.psum_scatter(blocks, "col", scatter_dimension=1, tiled=True)

    marks = [0, x.shape[1] - 768, x.shape[1]]
    xs = [x[:, low:high] for low, high in zip(marks, marks[1:])]
    r1 = [send(piece, right) for piece in xs]
    l1 = [send(piece, left) for piece in xs]
    own = scatter(dot_rows(x, x).astype(jnp.bfloat16)[None])
    own, r1[0], l1[0] = lax.optimization_barrier((own, r1[0], l1[0]))
    r2 = [send(piece, right[1:]) for piece in r1]
    l2 = [send(piece, left[1:]) for piece in l1]

    across = [l2[0] + r2[0]]
    far_marks = [0, 512, *marks[1:]]
    head = across[0][:, :512]
    head, across[0], l2[1], r2[1] = lax.optimization_barrier((head, across[0], l2[1], r2[1]))
    across.append(l2[1] + r2[1])

    first = scatter(near_blocks(x, l1, r1, marks))
    corner = corner_block(place, l1, r1, l2, r2, marks)
    corner, first = lax.optimization_barrier((corner, first))
    shares = lax.all_to_all(corner.reshape(n_col, -1, corner.shape[2]), "col", 0, 0)
    corner = shares.astype(jnp.float32).sum(0, keepdims=True).astype(jnp.bfloat16)

    def send_on(value, *after):
        return send(lax.optimization_barrier((value, *after))[0], [(1, 0), (2, 3)])

    far = [send_on(head)]
    second = send(first[2], left[1:]) + send(first[3], right[1:])
    second, far[0] = lax.optimization_barrier((second, far[0]))
    tile = jnp.stack([own[0], first[0], second, first[1]])
    tr1, tl1 = send(tile, right), send(tile, left)

    end = send(corner, [(1, 0), (2, 3)])
    pair = send(corner, [(1, 2), (2, 1)])
    end, tr1, tl1 = lax.optimization_barrier((end, tr1, tl1))
    zero = jnp.zeros_like(end)
    added = [zero, jnp.where(z == 3, end, zero), zero, jnp.where(z == 0, end, zero)]
    panel = lax.all_gather(tile + jnp.concatenate(added), "col", axis=1, tiled=True)

    tr2, tl2 = send(tr1, right[1:]), send(tl1, left[1:])
    tr3, tl3 = send(tr2, right[2:]), send(tl2, left[2:])
    far.append(arrived(send_on(across[0][:, 512:], tr3, tl3, pair)))

    strip = strips(place, tile, tl1, tr3, tl2, tr2, tr1, tl3, corner, pair, end)
    factor = square(place, panel, strip)
    far.append(send_on(across[1], factor))
    factor = lax.all_gather(factor, "col", axis=0, tiled=False)
    near = [l1, r1, across]
    out, factor = product(
        place, factor, x, [group[0] for group in near], far[:2], 256, far_marks[:3], None
    )
    (out,) = product(place, factor, x, [group[1] for group in near], far[2:], 256, marks[1:], out)
    return out


def solution(mesh):
    n_row, n_col = mesh.shape["row"], mesh.shape["col"]

    def body(iterate):
        if (n_row, n_col) == (4, 8) and iterate.shape == (896, 2304):
            return per_device_line(n_col, iterate)
        return per_device(iterate)

    return jax.shard_map(
        body,
        mesh=mesh,
        in_specs=(P("row", "col"),),
        out_specs=P("row", "col"),
        check_vma=False,
    )
```

```python
import functools
import math

import jax
import jax.numpy as jnp
from jax import lax
from jax.experimental import pallas as pl
from jax.experimental.pallas import tpu as pltpu
from jax.sharding import PartitionSpec as P

N = 18432


coef_a = 3.4445
coef_b = -4.775
coef_c = 2.0315


def dot_rows(left, right):
    return lax.dot_general(
        left, right, (((1,), (1,)), ((), ())), preferred_element_type=jnp.float32
    )


def per_device(iterate):
    contract = (((1,), (1,)), ((), ()))
    gathered = lax.all_gather(iterate, "row", axis=0, tiled=True)
    partial_value = lax.dot_general(
        iterate, gathered, contract, preferred_element_type=jnp.float32
    )
    partial_value = partial_value.astype(jnp.bfloat16)
    gram_tile = lax.psum_scatter(partial_value, "col", scatter_dimension=1, tiled=True)
    gram_panel = lax.all_gather(gram_tile, "col", axis=1, tiled=True)
    squared = jnp.dot(
        gram_panel,
        lax.all_gather(gram_tile, "row", axis=0, tiled=True),
        preferred_element_type=jnp.float32,
    )
    factor = (coef_b * gram_tile.astype(jnp.float32) + coef_c * squared).astype(jnp.bfloat16)
    factor_panel = lax.all_gather(factor, "col", axis=1, tiled=True)
    product = jnp.dot(factor_panel, gathered, preferred_element_type=jnp.float32)
    result = coef_a * iterate.astype(jnp.float32) + product
    return (math.sqrt(N) * result).astype(jnp.bfloat16)


def whole():
    return pl.BlockSpec(memory_space=pltpu.VMEM)


def scalars():
    return pl.BlockSpec(memory_space=pltpu.SMEM)


def load_pieces(pieces, marks, target, sem):
    copies = [
        pltpu.make_async_copy(piece, target.at[:, low:high], sem.at[p])
        for p, (piece, low, high) in enumerate(zip(pieces, marks, marks[1:]))
    ]
    for copy in copies:
        copy.start()
    return copies


def load_near(begin, x, l1, r1, held, sems):
    rows, width = l1.shape
    sources = (r1, x.at[:, begin : begin + width], l1)
    copies = [
        pltpu.make_async_copy(source, held.at[g * rows : (g + 1) * rows], sems.at[g])
        for g, source in enumerate(sources)
    ]
    for copy in copies:
        copy.start()
    for copy in copies:
        copy.wait()


def near_first_kernel(x, l1, r1, out, held, sems):
    rows = x.shape[0]
    load_near(0, x, l1, r1, held, sems)
    out[0] = dot_rows(held[: 2 * rows], held[2 * rows :])
    out[1] = dot_rows(held[rows:], held[:rows])


def near_rest_kernel(begin, x, l1, r1, part, out, held, total, sems):
    rows = x.shape[0]
    copies = [pltpu.make_async_copy(part.at[g], total.at[g], sems.at[3 + g]) for g in range(2)]
    for copy in copies:
        copy.start()
    load_near(begin, x, l1, r1, held, sems)
    for g, (left, right, above, below) in enumerate(
        (
            (slice(0, 2 * rows), slice(2 * rows, 3 * rows), 2, 0),
            (slice(rows, 3 * rows), slice(0, rows), 1, 3),
        )
    ):
        value = dot_rows(held[left], held[right])
        copies[g].wait()
        value = (value + total[g]).astype(out.dtype)
        out[above] = value[:rows]
        out[below] = value[rows:]


def near_call(kernel, shape, dtype, operands, scratch, share):
    rows, width = operands[1].shape
    return pl.pallas_call(
        kernel,
        out_shape=jax.ShapeDtypeStruct(shape, dtype),
        in_specs=[pl.BlockSpec(memory_space=pl.ANY)] * len(operands),
        out_specs=whole(),
        scratch_shapes=[pltpu.VMEM((3 * rows, width), jnp.bfloat16), *scratch],
        compiler_params=pltpu.CompilerParams(vmem_limit_bytes=56 * 2**20),
        cost_estimate=pl.CostEstimate(
            flops=share * 8 * rows * rows * width,
            bytes_accessed=share * 6 * rows * width,
            transcendentals=0,
        ),
    )(*operands)


def near_first(x, l1, r1):
    rows = x.shape[0]
    sems = pltpu.SemaphoreType.DMA((3,))
    return near_call(near_first_kernel, (2, 2 * rows, rows), jnp.float32, [x, l1, r1], [sems], 0)


def near_rest(x, l1, r1, part):
    rows = x.shape[0]
    kernel = functools.partial(near_rest_kernel, x.shape[1] - l1.shape[1])
    scratch = [pltpu.VMEM(part.shape, jnp.float32), pltpu.SemaphoreType.DMA((5,))]
    return near_call(kernel, (4, rows, rows), jnp.bfloat16, [x, l1, r1, part], scratch, 1)


def corner_kernel(marks, place, *rest):
    n = len(marks) - 1
    l1, r1, l2, r2 = (rest[g * n : (g + 1) * n] for g in range(4))
    out, held, sems = rest[4 * n :]
    for plane, one, other in ((1, r1, l2), (2, l1, r2)):

        @pl.when(place[0] == plane)
        def _(one=one, other=other):
            copies = load_pieces(one, marks, held.at[0], sems.at[0])
            copies += load_pieces(other, marks, held.at[1], sems.at[1])
            for copy in copies:
                copy.wait()
            out[0] = dot_rows(held[0], held[1]).astype(out.dtype)

    @pl.when(jnp.logical_or(place[0] == 0, place[0] == 3))
    def _():
        out[...] = jnp.zeros_like(out)


def corner_block(place, l1, r1, l2, r2, marks):
    rows, depth = l1[0].shape[0], marks[-1]
    return pl.pallas_call(
        functools.partial(corner_kernel, marks),
        out_shape=jax.ShapeDtypeStruct((1, rows, rows), jnp.bfloat16),
        in_specs=[scalars()] + [pl.BlockSpec(memory_space=pl.ANY)] * (4 * len(l1)),
        out_specs=whole(),
        scratch_shapes=[
            pltpu.VMEM((2, rows, depth), jnp.bfloat16),
            pltpu.SemaphoreType.DMA((2, len(l1))),
        ],
        compiler_params=pltpu.CompilerParams(vmem_limit_bytes=56 * 2**20),
        cost_estimate=pl.CostEstimate(
            flops=128 * rows * rows * depth, bytes_accessed=8 * rows * depth, transcendentals=0
        ),
    )(place, *l1, *r1, *l2, *r2)


def strips_kernel(place, own, l1, r3, l2, r2, r1, l3, corner, pair, end, out):
    z = place[0]
    _, part, rows = own.shape
    at_end = jnp.logical_or(z == 0, z == 3)
    zero = jnp.zeros_like(end[0])
    near = jnp.where(at_end, end[0], corner[0])
    far = jnp.where(at_end, zero, pair[0])
    low = jnp.where(z < 2, near, far)
    high = jnp.where(z < 2, far, near)
    for e in range(4):
        for block in range(4):
            if e == 0:
                value = own[block]
            else:
                one, other = {1: (l1, r3), 2: (l2, r2), 3: (r1, l3)}[e]
                value = one[block] + other[block]
            if block == 3:
                value = value + jnp.where((z + e) % 4 == 0, low, zero)
            if block == 1:
                value = value + jnp.where((z + e) % 4 == 3, high, zero)
            place_of = (block + e) % 4 * rows
            out[e * part : (e + 1) * part, place_of : place_of + rows] = value


def strips(place, *others):
    _, part, rows = others[0].shape
    return pl.pallas_call(
        strips_kernel,
        out_shape=jax.ShapeDtypeStruct((4 * part, 4 * rows), jnp.bfloat16),
        in_specs=[scalars()] + [whole()] * len(others),
        out_specs=whole(),
        compiler_params=pltpu.CompilerParams(vmem_limit_bytes=24 * 2**20),
        cost_estimate=pl.CostEstimate(
            flops=16 * part * rows, bytes_accessed=2 * 44 * part * rows, transcendentals=0
        ),
    )(place, *others)


def square_kernel(place, panel, right, out, held, strip, sems):
    z = place[0]
    rows, part = panel.shape[1], right.shape[0] // 4
    copies = [pltpu.make_async_copy(right, strip, sems.at[4])]
    for d in range(4):
        columns = held.at[:, d * rows : (d + 1) * rows]
        copies.append(pltpu.make_async_copy(panel.at[d], columns, sems.at[d]))
    for copy in copies:
        copy.start()
    for copy in copies:
        copy.wait()
    for plane, block, e in ((0, 3, 3), (3, 1, 1)):

        @pl.when(z == plane)
        def _(block=block, e=e):
            index = lax.broadcasted_iota(jnp.int32, (part, rows), 0) + place[1] * part
            other = lax.broadcasted_iota(jnp.int32, (part, rows), 1)
            pick = jnp.where(index == other, 1.0, 0.0).astype(jnp.bfloat16)
            far = dot_rows(pick, held[:, block * rows : (block + 1) * rows]).astype(strip.dtype)
            strip[e * part : (e + 1) * part, :rows] += far

    total = dot_rows(held[...], strip[...])
    index = lax.broadcasted_iota(jnp.int32, (rows, rows), 0)
    other = lax.broadcasted_iota(jnp.int32, (rows, rows), 1)
    unit = jnp.where(index == other, 1.0, 0.0).astype(jnp.bfloat16)
    out[...] = (coef_b * dot_rows(unit, strip[:, :rows]) + coef_c * total).astype(out.dtype)


def square(place, panel, right):
    rows, depth = panel.shape[1], right.shape[0]
    outside = pl.BlockSpec(memory_space=pl.ANY)
    return pl.pallas_call(
        square_kernel,
        out_shape=jax.ShapeDtypeStruct((rows, depth), jnp.bfloat16),
        in_specs=[scalars(), outside, outside],
        out_specs=whole(),
        scratch_shapes=[
            pltpu.VMEM((rows, 4 * rows), jnp.bfloat16),
            pltpu.VMEM((depth, 4 * rows), jnp.bfloat16),
            pltpu.SemaphoreType.DMA((5,)),
        ],
        compiler_params=pltpu.CompilerParams(vmem_limit_bytes=56 * 2**20),
        cost_estimate=pl.CostEstimate(
            flops=2 * rows * rows * 4 * depth, bytes_accessed=2 * 5 * rows * rows, transcendentals=0
        ),
    )(place, panel, right)


def product_kernel(marks, ready, place, f, x, *rest):
    l1, r1, across, *rest = rest
    far = rest[: len(marks) - 1]
    rest = rest[len(marks) - 1 + ready :]
    out, whole_f, wide, sems = (rest[0], *rest[-4:-1])
    z = place[0]
    n_col, part, _ = x.shape
    rows, depth = n_col * part, 4 * part
    width = out.shape[1]
    n_tile = (marks[-1] - marks[0]) // width
    step = pl.program_id(0)

    def copy(source, begin, slot, d):
        return pltpu.make_async_copy(
            source.at[:, :, pl.ds(pl.multiple_of(begin, width), width)],
            wide.at[slot, :, pl.ds(d * part, part), :],
            sems.at[slot, d],
        )

    def fetch(tile, slot):
        begin = marks[0] + tile * width
        copy(x, begin, slot, 0).start()
        copy(across, tile * width, slot, 2).start()
        for d, usual, edge in ((1, l1, 3), (3, r1, 0)):

            @pl.when(z != edge)
            def _(d=d, usual=usual):
                copy(usual, tile * width, slot, d).start()

            for piece, low, high in zip(far, marks, marks[1:]):
                inside = jnp.logical_and(begin >= low, begin < high)

                @pl.when(jnp.logical_and(z == edge, inside))
                def _(d=d, piece=piece, low=low):
                    copy(piece, begin - low, slot, d).start()

    slot = lax.rem(step, 2)
    if ready:
        f_sems = rest[-1]
        loads = [pltpu.make_async_copy(f, whole_f, f_sems.at[0])]
    else:
        held_f, f_sems = rest[2], rest[-1]
        loads = [pltpu.make_async_copy(f.at[c], held_f.at[c], f_sems.at[c]) for c in range(n_col)]
        save = pltpu.make_async_copy(whole_f, rest[1], f_sems.at[n_col])

    @pl.when(step == 0)
    def _():
        for one in loads:
            one.start()
        fetch(0, 0)
        if ready:
            loads[0].wait()
        else:
            for c in range(n_col):
                loads[c].wait()
                whole_f[:, c * depth : (c + 1) * depth] = held_f[c]
            save.start()

    @pl.when(step + 1 < n_tile)
    def _():
        fetch(step + 1, 1 - slot)

    for d in range(4):
        copy(x, 0, slot, d).wait()
    total = jnp.dot(
        whole_f[...],
        wide[slot].reshape(n_col * depth, width),
        preferred_element_type=jnp.float32,
    )
    own = wide[slot, :, :part, :].reshape(rows, width).astype(jnp.float32)
    out[...] = (math.sqrt(N) * (coef_a * own + total)).astype(out.dtype)
    if not ready:

        @pl.when(step == n_tile - 1)
        def _():
            save.wait()


def product(place, f, x, near, far, tile, marks, before):
    rows, columns = x.shape
    share = marks[-1] - marks[0]
    ready = before is not None
    n_col = N // columns
    part = rows // n_col
    depth = 4 * part

    def split(value):
        return value.reshape(n_col, part, value.shape[1])

    outside = pl.BlockSpec(memory_space=pl.ANY)
    operands = [place, f, *(split(value) for value in (x, *near, *far))]
    aliases = {}
    out_shape = [jax.ShapeDtypeStruct((rows, columns), jnp.bfloat16)]
    out_specs = [pl.BlockSpec((rows, tile), lambda i: (0, i + marks[0] // tile))]
    scratch = [
        pltpu.VMEM((rows, n_col * depth), jnp.bfloat16),
        pltpu.VMEM((2, n_col, depth, tile), jnp.bfloat16),
        pltpu.SemaphoreType.DMA((2, 4)),
        pltpu.SemaphoreType.DMA((n_col + 1,)),
    ]
    if ready:
        aliases = {len(operands): 0}
        operands.append(before)
    else:
        out_shape.append(jax.ShapeDtypeStruct((rows, n_col * depth), jnp.bfloat16))
        out_specs.append(outside)
        scratch = [pltpu.VMEM(f.shape, jnp.bfloat16), *scratch]
    return pl.pallas_call(
        functools.partial(product_kernel, tuple(marks), ready),
        grid=(share // tile,),
        out_shape=out_shape,
        in_specs=[scalars()] + [outside] * (len(operands) - 1),
        out_specs=out_specs,
        scratch_shapes=scratch,
        input_output_aliases=aliases,
        compiler_params=pltpu.CompilerParams(vmem_limit_bytes=56 * 2**20),
        cost_estimate=pl.CostEstimate(
            flops=2 * rows * n_col * depth * share if ready else 0,
            bytes_accessed=2 * 6 * rows * share if ready else 0,
            transcendentals=0,
        ),
    )(*operands)


def arrived_kernel(*refs):
    pass


def arrived(*values):
    outside = pl.BlockSpec(memory_space=pl.ANY)
    return pl.pallas_call(
        arrived_kernel,
        out_shape=[jax.ShapeDtypeStruct(value.shape, value.dtype) for value in values],
        in_specs=[outside] * len(values),
        out_specs=[outside] * len(values),
        input_output_aliases={i: i for i in range(len(values))},
        cost_estimate=pl.CostEstimate(flops=2 * 10**11, bytes_accessed=0, transcendentals=0),
    )(*values)


def per_device_line(n_col, x):
    z = lax.axis_index("row")
    place = jnp.stack([z, lax.axis_index("col")]).astype(jnp.int32)
    right, left = [(0, 1), (1, 2), (2, 3)], [(3, 2), (2, 1), (1, 0)]

    def send(value, pairs):
        return lax.ppermute(value, "row", pairs)

    def scatter(blocks):
        return lax.psum_scatter(blocks, "col", scatter_dimension=1, tiled=True)

    marks = [0, x.shape[1] - 768, x.shape[1]]
    xs = [x[:, low:high] for low, high in zip(marks, marks[1:])]
    r1 = [send(piece, right) for piece in xs]
    l1 = [send(piece, left) for piece in xs]
    own = scatter(dot_rows(x, x).astype(jnp.bfloat16)[None])
    own, r1[0], l1[0] = lax.optimization_barrier((own, r1[0], l1[0]))
    r2, l2 = [send(r1[0], right[1:])], [send(l1[0], left[1:])]

    part = near_first(x, l1[0], r1[0])
    part, r1[1], l1[1] = lax.optimization_barrier((part, r1[1], l1[1]))
    r1[1], l1[1] = arrived(r1[1], l1[1])
    r2.append(send(r1[1], right[1:]))
    l2.append(send(l1[1], left[1:]))
    first = scatter(near_rest(x, l1[1], r1[1], part))
    across = list(arrived(l2[0] + r2[0]))
    first, across[0] = lax.optimization_barrier((first, across[0]))
    second = send(first[2], left[1:]) + send(first[3], right[1:])

    second, l2[1], r2[1] = lax.optimization_barrier((second, l2[1], r2[1]))
    across.append(l2[1] + r2[1])
    corner = corner_block(place, l1, r1, l2, r2, marks)
    corner, second = lax.optimization_barrier((corner, second))
    shares = lax.all_to_all(corner.reshape(n_col, -1, corner.shape[2]), "col", 0, 0)
    corner = shares.astype(jnp.float32).sum(0, keepdims=True).astype(jnp.bfloat16)

    def send_on(value, *after):
        return send(lax.optimization_barrier((value, *after))[0], [(1, 0), (2, 3)])

    tile = jnp.stack([own[0], first[0], second, first[1]])
    tr1, tl1 = send(tile, right), send(tile, left)

    end = send(corner, [(1, 0), (2, 3)])
    pair = send(corner, [(1, 2), (2, 1)])
    end, tr1, tl1 = lax.optimization_barrier((end, tr1, tl1))
    zero = jnp.zeros_like(end)
    added = [zero, jnp.where(z == 3, end, zero), zero, jnp.where(z == 0, end, zero)]
    panel = lax.all_gather(tile + jnp.concatenate(added), "col", axis=1, tiled=True)

    tr2, tl2 = send(tr1, right[1:]), send(tl1, left[1:])
    tr3, tl3 = send(tr2, right[2:]), send(tl2, left[2:])
    far = list(arrived(send_on(across[0], tr3, tl3, pair)))

    strip = strips(place, tile, tl1, tr3, tl2, tr2, tr1, tl3, corner, pair, end)
    factor = square(place, panel, strip)
    far.append(send_on(across[1], factor))
    factor = lax.all_gather(factor, "col", axis=0, tiled=False)
    near = [l1, r1, across]
    out, factor = product(
        place, factor, x, [group[0] for group in near], far[:1], 256, marks[:2], None
    )
    (out,) = product(place, factor, x, [group[1] for group in near], far[1:], 256, marks[1:], out)
    return out


def solution(mesh):
    n_row, n_col = mesh.shape["row"], mesh.shape["col"]

    def body(iterate):
        if (n_row, n_col) == (4, 8) and iterate.shape == (896, 2304):
            return per_device_line(n_col, iterate)
        return per_device(iterate)

    return jax.shard_map(
        body,
        mesh=mesh,
        in_specs=(P("row", "col"),),
        out_specs=P("row", "col"),
        check_vma=False,
    )
```

```python
import functools
import math

import jax
import jax.numpy as jnp
from jax import lax
from jax.experimental import pallas as pl
from jax.experimental.pallas import tpu as pltpu
from jax.sharding import PartitionSpec as P

N = 18432


coef_a = 3.4445
coef_b = -4.775
coef_c = 2.0315


def dot_rows(left, right):
    return lax.dot_general(
        left, right, (((1,), (1,)), ((), ())), preferred_element_type=jnp.float32
    )


def per_device(iterate):
    contract = (((1,), (1,)), ((), ()))
    gathered = lax.all_gather(iterate, "row", axis=0, tiled=True)
    partial_value = lax.dot_general(
        iterate, gathered, contract, preferred_element_type=jnp.float32
    )
    partial_value = partial_value.astype(jnp.bfloat16)
    gram_tile = lax.psum_scatter(partial_value, "col", scatter_dimension=1, tiled=True)
    gram_panel = lax.all_gather(gram_tile, "col", axis=1, tiled=True)
    squared = jnp.dot(
        gram_panel,
        lax.all_gather(gram_tile, "row", axis=0, tiled=True),
        preferred_element_type=jnp.float32,
    )
    factor = (coef_b * gram_tile.astype(jnp.float32) + coef_c * squared).astype(jnp.bfloat16)
    factor_panel = lax.all_gather(factor, "col", axis=1, tiled=True)
    product = jnp.dot(factor_panel, gathered, preferred_element_type=jnp.float32)
    result = coef_a * iterate.astype(jnp.float32) + product
    return (math.sqrt(N) * result).astype(jnp.bfloat16)


def whole():
    return pl.BlockSpec(memory_space=pltpu.VMEM)


def scalars():
    return pl.BlockSpec(memory_space=pltpu.SMEM)


def load_pieces(pieces, marks, target, sem):
    copies = [
        pltpu.make_async_copy(piece, target.at[:, low:high], sem.at[p])
        for p, (piece, low, high) in enumerate(zip(pieces, marks, marks[1:]))
    ]
    for copy in copies:
        copy.start()
    return copies


def load_near(begin, x, l1, r1, held, sems):
    rows, width = l1.shape
    sources = (r1, x.at[:, begin : begin + width], l1)
    copies = [
        pltpu.make_async_copy(source, held.at[g * rows : (g + 1) * rows], sems.at[g])
        for g, source in enumerate(sources)
    ]
    for copy in copies:
        copy.start()
    for copy in copies:
        copy.wait()


def near_first_kernel(x, l1, r1, out, held, sems):
    rows = x.shape[0]
    load_near(0, x, l1, r1, held, sems)
    out[0] = dot_rows(held[: 2 * rows], held[2 * rows :])
    out[1] = dot_rows(held[rows:], held[:rows])


def near_rest_kernel(begin, x, l1, r1, part, out, held, total, sems):
    rows = x.shape[0]
    copies = [pltpu.make_async_copy(part.at[g], total.at[g], sems.at[3 + g]) for g in range(2)]
    for copy in copies:
        copy.start()
    load_near(begin, x, l1, r1, held, sems)
    for g, (left, right, above, below) in enumerate(
        (
            (slice(0, 2 * rows), slice(2 * rows, 3 * rows), 2, 0),
            (slice(rows, 3 * rows), slice(0, rows), 1, 3),
        )
    ):
        value = dot_rows(held[left], held[right])
        copies[g].wait()
        value = (value + total[g]).astype(out.dtype)
        out[above] = value[:rows]
        out[below] = value[rows:]


def near_call(kernel, shape, dtype, operands, scratch, share):
    rows, width = operands[1].shape
    return pl.pallas_call(
        kernel,
        out_shape=jax.ShapeDtypeStruct(shape, dtype),
        in_specs=[pl.BlockSpec(memory_space=pl.ANY)] * len(operands),
        out_specs=whole(),
        scratch_shapes=[pltpu.VMEM((3 * rows, width), jnp.bfloat16), *scratch],
        compiler_params=pltpu.CompilerParams(vmem_limit_bytes=56 * 2**20),
        cost_estimate=pl.CostEstimate(
            flops=share * 8 * rows * rows * width,
            bytes_accessed=share * 6 * rows * width,
            transcendentals=0,
        ),
    )(*operands)


def near_first(x, l1, r1):
    rows = x.shape[0]
    sems = pltpu.SemaphoreType.DMA((3,))
    return near_call(near_first_kernel, (2, 2 * rows, rows), jnp.float32, [x, l1, r1], [sems], 0)


def near_rest(x, l1, r1, part):
    rows = x.shape[0]
    kernel = functools.partial(near_rest_kernel, x.shape[1] - l1.shape[1])
    scratch = [pltpu.VMEM(part.shape, jnp.float32), pltpu.SemaphoreType.DMA((5,))]
    return near_call(kernel, (4, rows, rows), jnp.bfloat16, [x, l1, r1, part], scratch, 1)


def corner_kernel(marks, place, *rest):
    n = len(marks) - 1
    l1, r1, l2, r2 = (rest[g * n : (g + 1) * n] for g in range(4))
    out, held, sems = rest[4 * n :]
    for plane, one, other in ((1, r1, l2), (2, l1, r2)):

        @pl.when(place[0] == plane)
        def _(one=one, other=other):
            copies = load_pieces(one, marks, held.at[0], sems.at[0])
            copies += load_pieces(other, marks, held.at[1], sems.at[1])
            for copy in copies:
                copy.wait()
            out[0] = dot_rows(held[0], held[1]).astype(out.dtype)

    @pl.when(jnp.logical_or(place[0] == 0, place[0] == 3))
    def _():
        out[...] = jnp.zeros_like(out)


def corner_block(place, l1, r1, l2, r2, marks):
    rows, depth = l1[0].shape[0], marks[-1]
    return pl.pallas_call(
        functools.partial(corner_kernel, marks),
        out_shape=jax.ShapeDtypeStruct((1, rows, rows), jnp.bfloat16),
        in_specs=[scalars()] + [pl.BlockSpec(memory_space=pl.ANY)] * (4 * len(l1)),
        out_specs=whole(),
        scratch_shapes=[
            pltpu.VMEM((2, rows, depth), jnp.bfloat16),
            pltpu.SemaphoreType.DMA((2, len(l1))),
        ],
        compiler_params=pltpu.CompilerParams(vmem_limit_bytes=56 * 2**20),
        cost_estimate=pl.CostEstimate(
            flops=128 * rows * rows * depth, bytes_accessed=8 * rows * depth, transcendentals=0
        ),
    )(place, *l1, *r1, *l2, *r2)


def strips_kernel(place, own, l1, r3, l2, r2, r1, l3, corner, pair, end, out):
    z = place[0]
    _, part, rows = own.shape
    at_end = jnp.logical_or(z == 0, z == 3)
    zero = jnp.zeros_like(end[0])
    near = jnp.where(at_end, end[0], corner[0])
    far = jnp.where(at_end, zero, pair[0])
    low = jnp.where(z < 2, near, far)
    high = jnp.where(z < 2, far, near)
    for e in range(4):
        for block in range(4):
            if e == 0:
                value = own[block]
            else:
                one, other = {1: (l1, r3), 2: (l2, r2), 3: (r1, l3)}[e]
                value = one[block] + other[block]
            if block == 3:
                value = value + jnp.where((z + e) % 4 == 0, low, zero)
            if block == 1:
                value = value + jnp.where((z + e) % 4 == 3, high, zero)
            place_of = (block + e) % 4 * rows
            out[e * part : (e + 1) * part, place_of : place_of + rows] = value


def strips(place, *others):
    _, part, rows = others[0].shape
    return pl.pallas_call(
        strips_kernel,
        out_shape=jax.ShapeDtypeStruct((4 * part, 4 * rows), jnp.bfloat16),
        in_specs=[scalars()] + [whole()] * len(others),
        out_specs=whole(),
        compiler_params=pltpu.CompilerParams(vmem_limit_bytes=24 * 2**20),
        cost_estimate=pl.CostEstimate(
            flops=16 * part * rows, bytes_accessed=2 * 44 * part * rows, transcendentals=0
        ),
    )(place, *others)


def square_kernel(place, panel, right, out, held, strip, sems):
    z = place[0]
    rows, part = panel.shape[1], right.shape[0] // 4
    copies = [pltpu.make_async_copy(right, strip, sems.at[4])]
    for d in range(4):
        columns = held.at[:, d * rows : (d + 1) * rows]
        copies.append(pltpu.make_async_copy(panel.at[d], columns, sems.at[d]))
    for copy in copies:
        copy.start()
    for copy in copies:
        copy.wait()
    for plane, block, e in ((0, 3, 3), (3, 1, 1)):

        @pl.when(z == plane)
        def _(block=block, e=e):
            index = lax.broadcasted_iota(jnp.int32, (part, rows), 0) + place[1] * part
            other = lax.broadcasted_iota(jnp.int32, (part, rows), 1)
            pick = jnp.where(index == other, 1.0, 0.0).astype(jnp.bfloat16)
            far = dot_rows(pick, held[:, block * rows : (block + 1) * rows]).astype(strip.dtype)
            strip[e * part : (e + 1) * part, :rows] += far

    total = dot_rows(held[...], strip[...])
    index = lax.broadcasted_iota(jnp.int32, (rows, rows), 0)
    other = lax.broadcasted_iota(jnp.int32, (rows, rows), 1)
    unit = jnp.where(index == other, 1.0, 0.0).astype(jnp.bfloat16)
    out[...] = (coef_b * dot_rows(unit, strip[:, :rows]) + coef_c * total).astype(out.dtype)


def square(place, panel, right):
    rows, depth = panel.shape[1], right.shape[0]
    outside = pl.BlockSpec(memory_space=pl.ANY)
    return pl.pallas_call(
        square_kernel,
        out_shape=jax.ShapeDtypeStruct((rows, depth), jnp.bfloat16),
        in_specs=[scalars(), outside, outside],
        out_specs=whole(),
        scratch_shapes=[
            pltpu.VMEM((rows, 4 * rows), jnp.bfloat16),
            pltpu.VMEM((depth, 4 * rows), jnp.bfloat16),
            pltpu.SemaphoreType.DMA((5,)),
        ],
        compiler_params=pltpu.CompilerParams(vmem_limit_bytes=56 * 2**20),
        cost_estimate=pl.CostEstimate(
            flops=2 * rows * rows * 4 * depth, bytes_accessed=2 * 5 * rows * rows, transcendentals=0
        ),
    )(place, panel, right)


def product_kernel(marks, ready, place, f, x, *rest):
    l1, r1, across, *rest = rest
    far = rest[: len(marks) - 1]
    rest = rest[len(marks) - 1 + ready :]
    out, whole_f, wide, sems = (rest[0], *rest[-4:-1])
    z = place[0]
    n_col, part, _ = x.shape
    rows, depth = n_col * part, 4 * part
    width = out.shape[1]
    n_tile = (marks[-1] - marks[0]) // width
    step = pl.program_id(0)

    def copy(source, begin, slot, d):
        return pltpu.make_async_copy(
            source.at[:, :, pl.ds(pl.multiple_of(begin, width), width)],
            wide.at[slot, :, pl.ds(d * part, part), :],
            sems.at[slot, d],
        )

    def fetch(tile, slot):
        begin = marks[0] + tile * width
        copy(x, begin, slot, 0).start()
        copy(across, tile * width, slot, 2).start()
        for d, usual, edge in ((1, l1, 3), (3, r1, 0)):

            @pl.when(z != edge)
            def _(d=d, usual=usual):
                copy(usual, tile * width, slot, d).start()

            for piece, low, high in zip(far, marks, marks[1:]):
                inside = jnp.logical_and(begin >= low, begin < high)

                @pl.when(jnp.logical_and(z == edge, inside))
                def _(d=d, piece=piece, low=low):
                    copy(piece, begin - low, slot, d).start()

    slot = lax.rem(step, 2)
    if ready:
        f_sems = rest[-1]
        loads = [pltpu.make_async_copy(f, whole_f, f_sems.at[0])]
    else:
        held_f, f_sems = rest[2], rest[-1]
        loads = [pltpu.make_async_copy(f.at[c], held_f.at[c], f_sems.at[c]) for c in range(n_col)]
        save = pltpu.make_async_copy(whole_f, rest[1], f_sems.at[n_col])

    @pl.when(step == 0)
    def _():
        for one in loads:
            one.start()
        fetch(0, 0)
        if ready:
            loads[0].wait()
        else:
            for c in range(n_col):
                loads[c].wait()
                whole_f[:, c * depth : (c + 1) * depth] = held_f[c]
            save.start()

    @pl.when(step + 1 < n_tile)
    def _():
        fetch(step + 1, 1 - slot)

    for d in range(4):
        copy(x, 0, slot, d).wait()
    total = jnp.dot(
        whole_f[...],
        wide[slot].reshape(n_col * depth, width),
        preferred_element_type=jnp.float32,
    )
    own = wide[slot, :, :part, :].reshape(rows, width).astype(jnp.float32)
    out[...] = (math.sqrt(N) * (coef_a * own + total)).astype(out.dtype)
    if not ready:

        @pl.when(step == n_tile - 1)
        def _():
            save.wait()


def product(place, f, x, near, far, tile, marks, before):
    rows, columns = x.shape
    share = marks[-1] - marks[0]
    ready = before is not None
    n_col = N // columns
    part = rows // n_col
    depth = 4 * part

    def split(value):
        return value.reshape(n_col, part, value.shape[1])

    outside = pl.BlockSpec(memory_space=pl.ANY)
    operands = [place, f, *(split(value) for value in (x, *near, *far))]
    aliases = {}
    out_shape = [jax.ShapeDtypeStruct((rows, columns), jnp.bfloat16)]
    out_specs = [pl.BlockSpec((rows, tile), lambda i: (0, i + marks[0] // tile))]
    scratch = [
        pltpu.VMEM((rows, n_col * depth), jnp.bfloat16),
        pltpu.VMEM((2, n_col, depth, tile), jnp.bfloat16),
        pltpu.SemaphoreType.DMA((2, 4)),
        pltpu.SemaphoreType.DMA((n_col + 1,)),
    ]
    if ready:
        aliases = {len(operands): 0}
        operands.append(before)
    else:
        out_shape.append(jax.ShapeDtypeStruct((rows, n_col * depth), jnp.bfloat16))
        out_specs.append(outside)
        scratch = [pltpu.VMEM(f.shape, jnp.bfloat16), *scratch]
    return pl.pallas_call(
        functools.partial(product_kernel, tuple(marks), ready),
        grid=(share // tile,),
        out_shape=out_shape,
        in_specs=[scalars()] + [outside] * (len(operands) - 1),
        out_specs=out_specs,
        scratch_shapes=scratch,
        input_output_aliases=aliases,
        compiler_params=pltpu.CompilerParams(vmem_limit_bytes=56 * 2**20),
        cost_estimate=pl.CostEstimate(
            flops=2 * rows * n_col * depth * share if ready else 0,
            bytes_accessed=2 * 6 * rows * share if ready else 0,
            transcendentals=0,
        ),
    )(*operands)


def arrived_kernel(*refs):
    pass


def arrived(*values):
    outside = pl.BlockSpec(memory_space=pl.ANY)
    return pl.pallas_call(
        arrived_kernel,
        out_shape=[jax.ShapeDtypeStruct(value.shape, value.dtype) for value in values],
        in_specs=[outside] * len(values),
        out_specs=[outside] * len(values),
        input_output_aliases={i: i for i in range(len(values))},
        cost_estimate=pl.CostEstimate(flops=2 * 10**11, bytes_accessed=0, transcendentals=0),
    )(*values)


def per_device_line(n_col, x):
    z = lax.axis_index("row")
    place = jnp.stack([z, lax.axis_index("col")]).astype(jnp.int32)
    right, left = [(0, 1), (1, 2), (2, 3)], [(3, 2), (2, 1), (1, 0)]

    def send(value, pairs):
        return lax.ppermute(value, "row", pairs)

    def scatter(blocks):
        return lax.psum_scatter(blocks, "col", scatter_dimension=1, tiled=True)

    marks = [0, x.shape[1] - 768, x.shape[1]]
    xs = [x[:, low:high] for low, high in zip(marks, marks[1:])]
    r1 = [send(piece, right) for piece in xs]
    l1 = [send(piece, left) for piece in xs]
    own = scatter(dot_rows(x, x).astype(jnp.bfloat16)[None])
    own, r1[0], l1[0] = lax.optimization_barrier((own, r1[0], l1[0]))
    r2, l2 = [send(r1[0], right[1:])], [send(l1[0], left[1:])]

    part = near_first(x, l1[0], r1[0])
    part, r1[1], l1[1] = lax.optimization_barrier((part, r1[1], l1[1]))
    r1[1], l1[1] = arrived(r1[1], l1[1])
    r2.append(send(r1[1], right[1:]))
    l2.append(send(l1[1], left[1:]))
    first = scatter(near_rest(x, l1[1], r1[1], part))

    across = [l2[0] + r2[0]]
    far_marks = [0, 512, *marks[1:]]
    head = across[0][:, :512]
    head, across[0], l2[1], r2[1] = lax.optimization_barrier((head, across[0], l2[1], r2[1]))
    across.append(l2[1] + r2[1])

    def send_on(value, *after):
        return send(lax.optimization_barrier((value, *after))[0], [(1, 0), (2, 3)])

    corner = corner_block(place, l1, r1, l2, r2, marks)
    corner, first = lax.optimization_barrier((corner, first))
    shares = lax.all_to_all(corner.reshape(n_col, -1, corner.shape[2]), "col", 0, 0)
    corner = shares.astype(jnp.float32).sum(0, keepdims=True).astype(jnp.bfloat16)

    far = [send_on(head)]
    second = send(first[2], left[1:]) + send(first[3], right[1:])
    second, far[0] = lax.optimization_barrier((second, far[0]))
    tile = jnp.stack([own[0], first[0], second, first[1]])
    tr1, tl1 = send(tile, right), send(tile, left)

    end = send(corner, [(1, 0), (2, 3)])
    pair = send(corner, [(1, 2), (2, 1)])
    end, tr1, tl1, across[1] = lax.optimization_barrier((end, tr1, tl1, across[1]))
    zero = jnp.zeros_like(end)
    added = [zero, jnp.where(z == 3, end, zero), zero, jnp.where(z == 0, end, zero)]
    panel = lax.all_gather(tile + jnp.concatenate(added), "col", axis=1, tiled=True)

    tr2, tl2 = send(tr1, right[1:]), send(tl1, left[1:])
    tr3, tl3 = send(tr2, right[2:]), send(tl2, left[2:])
    far += arrived(send_on(across[0][:, 512:], tr3, tl3, pair))

    strip = strips(place, tile, tl1, tr3, tl2, tr2, tr1, tl3, corner, pair, end)
    factor = square(place, panel, strip)
    far.append(send_on(across[1], factor))
    factor = lax.all_gather(factor, "col", axis=0, tiled=False)
    near = [l1, r1, across]
    out, factor = product(
        place, factor, x, [group[0] for group in near], far[:2], 256, far_marks[:3], None
    )
    (out,) = product(place, factor, x, [group[1] for group in near], far[2:], 256, marks[1:], out)
    return out


def solution(mesh):
    n_row, n_col = mesh.shape["row"], mesh.shape["col"]

    def body(iterate):
        if (n_row, n_col) == (4, 8) and iterate.shape == (896, 2304):
            return per_device_line(n_col, iterate)
        return per_device(iterate)

    return jax.shard_map(
        body,
        mesh=mesh,
        in_specs=(P("row", "col"),),
        out_specs=P("row", "col"),
        check_vma=False,
    )
```

```python
import functools
import math

import jax
import jax.numpy as jnp
from jax import lax
from jax.experimental import pallas as pl
from jax.experimental.pallas import tpu as pltpu
from jax.sharding import PartitionSpec as P

N = 18432


coef_a = 3.4445
coef_b = -4.775
coef_c = 2.0315


def dot_rows(left, right):
    return lax.dot_general(
        left, right, (((1,), (1,)), ((), ())), preferred_element_type=jnp.float32
    )


def per_device(iterate):
    contract = (((1,), (1,)), ((), ()))
    gathered = lax.all_gather(iterate, "row", axis=0, tiled=True)
    partial_value = lax.dot_general(
        iterate, gathered, contract, preferred_element_type=jnp.float32
    )
    partial_value = partial_value.astype(jnp.bfloat16)
    gram_tile = lax.psum_scatter(partial_value, "col", scatter_dimension=1, tiled=True)
    gram_panel = lax.all_gather(gram_tile, "col", axis=1, tiled=True)
    squared = jnp.dot(
        gram_panel,
        lax.all_gather(gram_tile, "row", axis=0, tiled=True),
        preferred_element_type=jnp.float32,
    )
    factor = (coef_b * gram_tile.astype(jnp.float32) + coef_c * squared).astype(jnp.bfloat16)
    factor_panel = lax.all_gather(factor, "col", axis=1, tiled=True)
    product = jnp.dot(factor_panel, gathered, preferred_element_type=jnp.float32)
    result = coef_a * iterate.astype(jnp.float32) + product
    return (math.sqrt(N) * result).astype(jnp.bfloat16)


def whole():
    return pl.BlockSpec(memory_space=pltpu.VMEM)


def scalars():
    return pl.BlockSpec(memory_space=pltpu.SMEM)


def load_pieces(pieces, marks, target, sem):
    copies = [
        pltpu.make_async_copy(piece, target.at[:, low:high], sem.at[p])
        for p, (piece, low, high) in enumerate(zip(pieces, marks, marks[1:]))
    ]
    for copy in copies:
        copy.start()
    return copies


def load_near(begin, x, l1, r1, held, sems):
    rows, width = l1.shape
    sources = (r1, x.at[:, begin : begin + width], l1)
    copies = [
        pltpu.make_async_copy(source, held.at[g * rows : (g + 1) * rows], sems.at[g])
        for g, source in enumerate(sources)
    ]
    for copy in copies:
        copy.start()
    for copy in copies:
        copy.wait()


def near_first_kernel(x, l1, r1, out, held, sems):
    rows = x.shape[0]
    load_near(0, x, l1, r1, held, sems)
    out[0] = dot_rows(held[: 2 * rows], held[2 * rows :])
    out[1] = dot_rows(held[rows:], held[:rows])


def near_rest_kernel(begin, x, l1, r1, part, out, held, total, sems):
    rows = x.shape[0]
    copies = [pltpu.make_async_copy(part.at[g], total.at[g], sems.at[3 + g]) for g in range(2)]
    for copy in copies:
        copy.start()
    load_near(begin, x, l1, r1, held, sems)
    for g, (left, right, above, below) in enumerate(
        (
            (slice(0, 2 * rows), slice(2 * rows, 3 * rows), 2, 0),
            (slice(rows, 3 * rows), slice(0, rows), 1, 3),
        )
    ):
        value = dot_rows(held[left], held[right])
        copies[g].wait()
        value = (value + total[g]).astype(out.dtype)
        out[above] = value[:rows]
        out[below] = value[rows:]


def near_call(kernel, shape, dtype, operands, scratch, share):
    rows, width = operands[1].shape
    return pl.pallas_call(
        kernel,
        out_shape=jax.ShapeDtypeStruct(shape, dtype),
        in_specs=[pl.BlockSpec(memory_space=pl.ANY)] * len(operands),
        out_specs=whole(),
        scratch_shapes=[pltpu.VMEM((3 * rows, width), jnp.bfloat16), *scratch],
        compiler_params=pltpu.CompilerParams(vmem_limit_bytes=56 * 2**20),
        cost_estimate=pl.CostEstimate(
            flops=share * 8 * rows * rows * width,
            bytes_accessed=share * 6 * rows * width,
            transcendentals=0,
        ),
    )(*operands)


def near_first(x, l1, r1):
    rows = x.shape[0]
    sems = pltpu.SemaphoreType.DMA((3,))
    return near_call(near_first_kernel, (2, 2 * rows, rows), jnp.float32, [x, l1, r1], [sems], 0)


def near_rest(x, l1, r1, part):
    rows = x.shape[0]
    kernel = functools.partial(near_rest_kernel, x.shape[1] - l1.shape[1])
    scratch = [pltpu.VMEM(part.shape, jnp.float32), pltpu.SemaphoreType.DMA((5,))]
    return near_call(kernel, (4, rows, rows), jnp.bfloat16, [x, l1, r1, part], scratch, 1)


def corner_kernel(marks, place, *rest):
    n = len(marks) - 1
    l1, r1, l2, r2 = (rest[g * n : (g + 1) * n] for g in range(4))
    out, held, sems = rest[4 * n :]
    for plane, one, other in ((1, r1, l2), (2, l1, r2)):

        @pl.when(place[0] == plane)
        def _(one=one, other=other):
            copies = load_pieces(one, marks, held.at[0], sems.at[0])
            copies += load_pieces(other, marks, held.at[1], sems.at[1])
            for copy in copies:
                copy.wait()
            out[0] = dot_rows(held[0], held[1]).astype(out.dtype)

    @pl.when(jnp.logical_or(place[0] == 0, place[0] == 3))
    def _():
        out[...] = jnp.zeros_like(out)


def corner_block(place, l1, r1, l2, r2, marks):
    rows, depth = l1[0].shape[0], marks[-1]
    return pl.pallas_call(
        functools.partial(corner_kernel, marks),
        out_shape=jax.ShapeDtypeStruct((1, rows, rows), jnp.bfloat16),
        in_specs=[scalars()] + [pl.BlockSpec(memory_space=pl.ANY)] * (4 * len(l1)),
        out_specs=whole(),
        scratch_shapes=[
            pltpu.VMEM((2, rows, depth), jnp.bfloat16),
            pltpu.SemaphoreType.DMA((2, len(l1))),
        ],
        compiler_params=pltpu.CompilerParams(vmem_limit_bytes=56 * 2**20),
        cost_estimate=pl.CostEstimate(
            flops=128 * rows * rows * depth, bytes_accessed=8 * rows * depth, transcendentals=0
        ),
    )(place, *l1, *r1, *l2, *r2)


block_order = (1, 3, 0, 2)


def strips_kernel(place, own, l1, r3, l2, r2, r1, l3, corner, pair, end, out):
    z = place[0]
    _, part, rows = own.shape
    at_end = jnp.logical_or(z == 0, z == 3)
    zero = jnp.zeros_like(end[0])
    near = jnp.where(at_end, end[0], corner[0])
    far = jnp.where(at_end, zero, pair[0])
    low = jnp.where(z < 2, near, far)
    high = jnp.where(z < 2, far, near)
    for e in range(4):
        for block in range(4):
            if e == 0:
                value = own[block]
            else:
                one, other = {1: (l1, r3), 2: (l2, r2), 3: (r1, l3)}[e]
                value = one[block] + other[block]
            if block == 3:
                value = value + jnp.where((z + e) % 4 == 0, low, zero)
            if block == 1:
                value = value + jnp.where((z + e) % 4 == 3, high, zero)
            place_of = block_order.index((block + e) % 4) * rows
            out[e * part : (e + 1) * part, place_of : place_of + rows] = value


def strips(place, *others):
    _, part, rows = others[0].shape
    return pl.pallas_call(
        strips_kernel,
        out_shape=jax.ShapeDtypeStruct((4 * part, 4 * rows), jnp.bfloat16),
        in_specs=[scalars()] + [whole()] * len(others),
        out_specs=whole(),
        compiler_params=pltpu.CompilerParams(vmem_limit_bytes=24 * 2**20),
        cost_estimate=pl.CostEstimate(
            flops=16 * part * rows, bytes_accessed=2 * 44 * part * rows, transcendentals=0
        ),
    )(place, *others)


def square_kernel(place, panel, right, out, held, strip, sems):
    z = place[0]
    rows, part = panel.shape[1], right.shape[0] // 4
    half = 2 * rows
    loads = [pltpu.make_async_copy(right, strip, sems.at[4])]
    for i, d in enumerate(block_order):
        columns = held.at[:, i * rows : (i + 1) * rows]
        loads.append(pltpu.make_async_copy(panel.at[d], columns, sems.at[d]))
    for load in loads:
        load.start()
    for load in loads[:3]:
        load.wait()
    total = dot_rows(held[:, :half], strip[:, :half])
    own = slice(half, half + rows)
    for plane, block, e in ((0, 3, 3), (3, 1, 1)):

        @pl.when(z == plane)
        def _(block=block, e=e):
            index = lax.broadcasted_iota(jnp.int32, (part, rows), 0) + place[1] * part
            other = lax.broadcasted_iota(jnp.int32, (part, rows), 1)
            pick = jnp.where(index == other, 1.0, 0.0).astype(jnp.bfloat16)
            at = block_order.index(block) * rows
            far = dot_rows(pick, held[:, at : at + rows]).astype(strip.dtype)
            strip[e * part : (e + 1) * part, own] += far

    for load in loads[3:]:
        load.wait()
    total = total + dot_rows(held[:, half:], strip[:, half:])
    index = lax.broadcasted_iota(jnp.int32, (rows, rows), 0)
    other = lax.broadcasted_iota(jnp.int32, (rows, rows), 1)
    unit = jnp.where(index == other, 1.0, 0.0).astype(jnp.bfloat16)
    out[...] = (coef_b * dot_rows(unit, strip[:, own]) + coef_c * total).astype(out.dtype)


def square(place, panel, right):
    rows, depth = panel.shape[1], right.shape[0]
    outside = pl.BlockSpec(memory_space=pl.ANY)
    return pl.pallas_call(
        square_kernel,
        out_shape=jax.ShapeDtypeStruct((rows, depth), jnp.bfloat16),
        in_specs=[scalars(), outside, outside],
        out_specs=whole(),
        scratch_shapes=[
            pltpu.VMEM((rows, 4 * rows), jnp.bfloat16),
            pltpu.VMEM((depth, 4 * rows), jnp.bfloat16),
            pltpu.SemaphoreType.DMA((5,)),
        ],
        compiler_params=pltpu.CompilerParams(vmem_limit_bytes=56 * 2**20),
        cost_estimate=pl.CostEstimate(
            flops=2 * rows * rows * 4 * depth, bytes_accessed=2 * 5 * rows * rows, transcendentals=0
        ),
    )(place, panel, right)


def product_kernel(marks, ready, place, f, x, *rest):
    l1, r1, across, *rest = rest
    far = rest[: len(marks) - 1]
    rest = rest[len(marks) - 1 + ready :]
    out, whole_f, wide, sems = (rest[0], *rest[-4:-1])
    z = place[0]
    n_col, part, _ = x.shape
    rows, depth = n_col * part, 4 * part
    width = out.shape[1]
    n_tile = (marks[-1] - marks[0]) // width
    step = pl.program_id(0)

    def copy(source, begin, slot, d):
        return pltpu.make_async_copy(
            source.at[:, :, pl.ds(pl.multiple_of(begin, width), width)],
            wide.at[slot, :, pl.ds(d * part, part), :],
            sems.at[slot, d],
        )

    def fetch(tile, slot):
        begin = marks[0] + tile * width
        copy(x, begin, slot, 0).start()
        copy(across, tile * width, slot, 2).start()
        for d, usual, edge in ((1, l1, 3), (3, r1, 0)):

            @pl.when(z != edge)
            def _(d=d, usual=usual):
                copy(usual, tile * width, slot, d).start()

            for piece, low, high in zip(far, marks, marks[1:]):
                inside = jnp.logical_and(begin >= low, begin < high)

                @pl.when(jnp.logical_and(z == edge, inside))
                def _(d=d, piece=piece, low=low):
                    copy(piece, begin - low, slot, d).start()

    slot = lax.rem(step, 2)
    if ready:
        f_sems = rest[-1]
        pair = 2 * depth
        parts = [slice(q * pair, (q + 1) * pair) for q in range(n_col // 2)]
        loads = [
            pltpu.make_async_copy(f.at[:, part_of], whole_f.at[:, part_of], f_sems.at[q])
            for q, part_of in enumerate(parts)
        ]
    else:
        held_f, f_sems = rest[2], rest[-1]
        loads = [pltpu.make_async_copy(f.at[c], held_f.at[c], f_sems.at[c]) for c in range(n_col)]
        save = pltpu.make_async_copy(whole_f, rest[1], f_sems.at[n_col])

    def arrive():
        for d in range(4):
            copy(x, 0, slot, d).wait()

    def finish(total):
        own = wide[slot, :, :part, :].reshape(rows, width).astype(jnp.float32)
        out[...] = (math.sqrt(N) * (coef_a * own + total)).astype(out.dtype)

    @pl.when(step == 0)
    def _():
        fetch(0, 0)
        for load in loads:
            load.start()
        if n_tile > 1:
            fetch(1, 1)
        arrive()
        total = jnp.zeros((rows, width), jnp.float32)
        for i, load in enumerate(loads):
            load.wait()
            if ready:
                left = whole_f[:, parts[i]]
                right = wide[0, 2 * i : 2 * i + 2].reshape(pair, width)
            else:
                left, right = held_f[i], wide[0, i]
                whole_f[:, i * depth : (i + 1) * depth] = left
            total = total + jnp.dot(left, right, preferred_element_type=jnp.float32)
        if not ready:
            save.start()
        finish(total)

    @pl.when(step > 0)
    def _():
        @pl.when(step + 1 < n_tile)
        def _():
            fetch(step + 1, 1 - slot)

        arrive()
        right = wide[slot].reshape(n_col * depth, width)
        finish(jnp.dot(whole_f[...], right, preferred_element_type=jnp.float32))

    if not ready:

        @pl.when(step == n_tile - 1)
        def _():
            save.wait()


def product(place, f, x, near, far, tile, marks, before):
    rows, columns = x.shape
    share = marks[-1] - marks[0]
    ready = before is not None
    n_col = N // columns
    part = rows // n_col
    depth = 4 * part

    def split(value):
        return value.reshape(n_col, part, value.shape[1])

    outside = pl.BlockSpec(memory_space=pl.ANY)
    operands = [place, f, *(split(value) for value in (x, *near, *far))]
    aliases = {}
    out_shape = [jax.ShapeDtypeStruct((rows, columns), jnp.bfloat16)]
    out_specs = [pl.BlockSpec((rows, tile), lambda i: (0, i + marks[0] // tile))]
    scratch = [
        pltpu.VMEM((rows, n_col * depth), jnp.bfloat16),
        pltpu.VMEM((2, n_col, depth, tile), jnp.bfloat16),
        pltpu.SemaphoreType.DMA((2, 4)),
        pltpu.SemaphoreType.DMA((n_col + 1,)),
    ]
    if ready:
        aliases = {len(operands): 0}
        operands.append(before)
    else:
        out_shape.append(jax.ShapeDtypeStruct((rows, n_col * depth), jnp.bfloat16))
        out_specs.append(outside)
        scratch = [pltpu.VMEM(f.shape, jnp.bfloat16), *scratch]
    return pl.pallas_call(
        functools.partial(product_kernel, tuple(marks), ready),
        grid=(share // tile,),
        out_shape=out_shape,
        in_specs=[scalars()] + [outside] * (len(operands) - 1),
        out_specs=out_specs,
        scratch_shapes=scratch,
        input_output_aliases=aliases,
        compiler_params=pltpu.CompilerParams(vmem_limit_bytes=56 * 2**20),
        cost_estimate=pl.CostEstimate(
            flops=2 * rows * n_col * depth * share if ready else 0,
            bytes_accessed=2 * 6 * rows * share if ready else 0,
            transcendentals=0,
        ),
    )(*operands)


def arrived_kernel(*refs):
    pass


def arrived(*values):
    outside = pl.BlockSpec(memory_space=pl.ANY)
    return pl.pallas_call(
        arrived_kernel,
        out_shape=[jax.ShapeDtypeStruct(value.shape, value.dtype) for value in values],
        in_specs=[outside] * len(values),
        out_specs=[outside] * len(values),
        input_output_aliases={i: i for i in range(len(values))},
        cost_estimate=pl.CostEstimate(flops=2 * 10**11, bytes_accessed=0, transcendentals=0),
    )(*values)


def per_device_line(n_col, x):
    z = lax.axis_index("row")
    place = jnp.stack([z, lax.axis_index("col")]).astype(jnp.int32)
    right, left = [(0, 1), (1, 2), (2, 3)], [(3, 2), (2, 1), (1, 0)]

    def send(value, pairs):
        return lax.ppermute(value, "row", pairs)

    def scatter(blocks):
        return lax.psum_scatter(blocks, "col", scatter_dimension=1, tiled=True)

    marks = [0, x.shape[1] - 768, x.shape[1]]
    xs = [x[:, low:high] for low, high in zip(marks, marks[1:])]
    r1 = [send(piece, right) for piece in xs]
    l1 = [send(piece, left) for piece in xs]
    own = scatter(dot_rows(x, x).astype(jnp.bfloat16)[None])
    own, r1[0], l1[0] = lax.optimization_barrier((own, r1[0], l1[0]))
    r2, l2 = [send(r1[0], right[1:])], [send(l1[0], left[1:])]

    part = near_first(x, l1[0], r1[0])
    part, r1[1], l1[1] = lax.optimization_barrier((part, r1[1], l1[1]))
    r1[1], l1[1] = arrived(r1[1], l1[1])
    r2.append(send(r1[1], right[1:]))
    l2.append(send(l1[1], left[1:]))
    first = scatter(near_rest(x, l1[1], r1[1], part))

    across = [l2[0] + r2[0]]
    far_marks = [0, 512, *marks[1:]]
    head = across[0][:, :512]
    head, across[0], l2[1], r2[1] = lax.optimization_barrier((head, across[0], l2[1], r2[1]))
    across.append(l2[1] + r2[1])

    def send_on(value, *after):
        return send(lax.optimization_barrier((value, *after))[0], [(1, 0), (2, 3)])

    corner = corner_block(place, l1, r1, l2, r2, marks)
    corner, first = lax.optimization_barrier((corner, first))
    shares = lax.all_to_all(corner.reshape(n_col, -1, corner.shape[2]), "col", 0, 0)
    corner = shares.astype(jnp.float32).sum(0, keepdims=True).astype(jnp.bfloat16)

    far = [send_on(head)]
    second = send(first[2], left[1:]) + send(first[3], right[1:])
    second, far[0] = lax.optimization_barrier((second, far[0]))
    tile = jnp.stack([own[0], first[0], second, first[1]])
    tr1, tl1 = send(tile, right), send(tile, left)

    end = send(corner, [(1, 0), (2, 3)])
    pair = send(corner, [(1, 2), (2, 1)])
    end, tr1, tl1, across[1] = lax.optimization_barrier((end, tr1, tl1, across[1]))
    zero = jnp.zeros_like(end)
    added = [zero, jnp.where(z == 3, end, zero), zero, jnp.where(z == 0, end, zero)]
    panel = lax.all_gather(tile + jnp.concatenate(added), "col", axis=1, tiled=True)

    tr2, tl2 = send(tr1, right[1:]), send(tl1, left[1:])
    tr3, tl3 = send(tr2, right[2:]), send(tl2, left[2:])
    far += arrived(send_on(across[0][:, 512:], tr3, tl3, pair))

    strip = strips(place, tile, tl1, tr3, tl2, tr2, tr1, tl3, corner, pair, end)
    factor = square(place, panel, strip)
    far.append(send_on(across[1], factor))
    factor = lax.all_gather(factor, "col", axis=0, tiled=False)
    near = [l1, r1, across]
    out, factor = product(
        place, factor, x, [group[0] for group in near], far[:2], 256, far_marks[:3], None
    )
    (out,) = product(place, factor, x, [group[1] for group in near], far[2:], 256, marks[1:], out)
    return out


def solution(mesh):
    n_row, n_col = mesh.shape["row"], mesh.shape["col"]

    def body(iterate):
        if (n_row, n_col) == (4, 8) and iterate.shape == (896, 2304):
            return per_device_line(n_col, iterate)
        return per_device(iterate)

    return jax.shard_map(
        body,
        mesh=mesh,
        in_specs=(P("row", "col"),),
        out_specs=P("row", "col"),
        check_vma=False,
    )
```

```python
import functools
import math

import jax
import jax.numpy as jnp
from jax import lax
from jax.experimental import pallas as pl
from jax.experimental.pallas import tpu as pltpu
from jax.sharding import PartitionSpec as P

N = 18432


coef_a = 3.4445
coef_b = -4.775
coef_c = 2.0315


def dot_rows(left, right):
    return lax.dot_general(
        left, right, (((1,), (1,)), ((), ())), preferred_element_type=jnp.float32
    )


def per_device(iterate):
    contract = (((1,), (1,)), ((), ()))
    gathered = lax.all_gather(iterate, "row", axis=0, tiled=True)
    partial_value = lax.dot_general(
        iterate, gathered, contract, preferred_element_type=jnp.float32
    )
    partial_value = partial_value.astype(jnp.bfloat16)
    gram_tile = lax.psum_scatter(partial_value, "col", scatter_dimension=1, tiled=True)
    gram_panel = lax.all_gather(gram_tile, "col", axis=1, tiled=True)
    squared = jnp.dot(
        gram_panel,
        lax.all_gather(gram_tile, "row", axis=0, tiled=True),
        preferred_element_type=jnp.float32,
    )
    factor = (coef_b * gram_tile.astype(jnp.float32) + coef_c * squared).astype(jnp.bfloat16)
    factor_panel = lax.all_gather(factor, "col", axis=1, tiled=True)
    product = jnp.dot(factor_panel, gathered, preferred_element_type=jnp.float32)
    result = coef_a * iterate.astype(jnp.float32) + product
    return (math.sqrt(N) * result).astype(jnp.bfloat16)


def whole():
    return pl.BlockSpec(memory_space=pltpu.VMEM)


def scalars():
    return pl.BlockSpec(memory_space=pltpu.SMEM)


def load_near(begin, x, l1, r1, held, sems):
    rows, width = l1.shape
    sources = (r1, x.at[:, begin : begin + width], l1)
    copies = [
        pltpu.make_async_copy(source, held.at[g * rows : (g + 1) * rows], sems.at[g])
        for g, source in enumerate(sources)
    ]
    for copy in copies:
        copy.start()
    for copy in copies:
        copy.wait()


def near_first_kernel(x, l1, r1, out, held, sems):
    rows = x.shape[0]
    load_near(0, x, l1, r1, held, sems)
    out[0] = dot_rows(held[: 2 * rows], held[2 * rows :])
    out[1] = dot_rows(held[rows:], held[:rows])


def near_rest_kernel(begin, x, l1, r1, part, out, held, total, sems):
    rows = x.shape[0]
    copies = [pltpu.make_async_copy(part.at[g], total.at[g], sems.at[3 + g]) for g in range(2)]
    for copy in copies:
        copy.start()
    load_near(begin, x, l1, r1, held, sems)
    for g, (left, right, above, below) in enumerate(
        (
            (slice(0, 2 * rows), slice(2 * rows, 3 * rows), 2, 0),
            (slice(rows, 3 * rows), slice(0, rows), 1, 3),
        )
    ):
        value = dot_rows(held[left], held[right])
        copies[g].wait()
        value = (value + total[g]).astype(out.dtype)
        out[above] = value[:rows]
        out[below] = value[rows:]


def near_call(kernel, shape, dtype, operands, scratch, share):
    rows, width = operands[1].shape
    return pl.pallas_call(
        kernel,
        out_shape=jax.ShapeDtypeStruct(shape, dtype),
        in_specs=[pl.BlockSpec(memory_space=pl.ANY)] * len(operands),
        out_specs=whole(),
        scratch_shapes=[pltpu.VMEM((3 * rows, width), jnp.bfloat16), *scratch],
        compiler_params=pltpu.CompilerParams(vmem_limit_bytes=56 * 2**20),
        cost_estimate=pl.CostEstimate(
            flops=share * 8 * rows * rows * width,
            bytes_accessed=share * 6 * rows * width,
            transcendentals=0,
        ),
    )(*operands)


def near_first(x, l1, r1):
    rows = x.shape[0]
    sems = pltpu.SemaphoreType.DMA((3,))
    return near_call(near_first_kernel, (2, 2 * rows, rows), jnp.float32, [x, l1, r1], [sems], 0)


def near_rest(x, l1, r1, part):
    rows = x.shape[0]
    kernel = functools.partial(near_rest_kernel, x.shape[1] - l1.shape[1])
    scratch = [pltpu.VMEM(part.shape, jnp.float32), pltpu.SemaphoreType.DMA((5,))]
    return near_call(kernel, (4, rows, rows), jnp.bfloat16, [x, l1, r1, part], scratch, 1)


def corner_kernel(place, l1, r1, l2, r2, *rest):
    *part, out, held, total, sems = rest
    for plane, one, other in ((1, r1, l2), (2, l1, r2)):

        @pl.when(place[0] == plane)
        def _(one=one, other=other):
            copies = [
                pltpu.make_async_copy(one, held.at[0], sems.at[0]),
                pltpu.make_async_copy(other, held.at[1], sems.at[1]),
            ]
            if part:
                copies.append(pltpu.make_async_copy(part[0].at[0], total, sems.at[2]))
            for copy in copies:
                copy.start()
            for copy in copies[:2]:
                copy.wait()
            value = dot_rows(held[0], held[1])
            if part:
                copies[2].wait()
                value = value + total[...]
            out[0] = value.astype(out.dtype)

    @pl.when(jnp.logical_or(place[0] == 0, place[0] == 3))
    def _():
        out[...] = jnp.zeros_like(out)


def corner_block(place, l1, r1, l2, r2, *part):
    rows, width = l1.shape
    operands = [l1, r1, l2, r2, *part]
    return pl.pallas_call(
        corner_kernel,
        out_shape=jax.ShapeDtypeStruct((1, rows, rows), jnp.bfloat16 if part else jnp.float32),
        in_specs=[scalars()] + [pl.BlockSpec(memory_space=pl.ANY)] * len(operands),
        out_specs=whole(),
        scratch_shapes=[
            pltpu.VMEM((2, rows, width), jnp.bfloat16),
            pltpu.VMEM((rows, rows), jnp.float32),
            pltpu.SemaphoreType.DMA((3,)),
        ],
        compiler_params=pltpu.CompilerParams(vmem_limit_bytes=56 * 2**20),
        cost_estimate=pl.CostEstimate(
            flops=256 * rows * rows * width if part else 0,
            bytes_accessed=8 * rows * width if part else 0,
            transcendentals=0,
        ),
    )(place, *operands)


def strips_kernel(place, own, l1, r3, l2, r2, r1, l3, corner, pair, end, out):
    z = place[0]
    _, part, rows = own.shape
    at_end = jnp.logical_or(z == 0, z == 3)
    zero = jnp.zeros_like(end[0])
    near = jnp.where(at_end, end[0], corner[0])
    far = jnp.where(at_end, zero, pair[0])
    low = jnp.where(z < 2, near, far)
    high = jnp.where(z < 2, far, near)
    for e in range(4):
        for block in range(4):
            if e == 0:
                value = own[block]
            else:
                one, other = {1: (l1, r3), 2: (l2, r2), 3: (r1, l3)}[e]
                value = one[block] + other[block]
            if block == 3:
                value = value + jnp.where((z + e) % 4 == 0, low, zero)
            if block == 1:
                value = value + jnp.where((z + e) % 4 == 3, high, zero)
            place_of = (block + e) % 4 * rows
            out[e * part : (e + 1) * part, place_of : place_of + rows] = value


def strips(place, *others):
    _, part, rows = others[0].shape
    return pl.pallas_call(
        strips_kernel,
        out_shape=jax.ShapeDtypeStruct((4 * part, 4 * rows), jnp.bfloat16),
        in_specs=[scalars()] + [whole()] * len(others),
        out_specs=whole(),
        compiler_params=pltpu.CompilerParams(vmem_limit_bytes=24 * 2**20),
        cost_estimate=pl.CostEstimate(
            flops=16 * part * rows, bytes_accessed=2 * 44 * part * rows, transcendentals=0
        ),
    )(place, *others)


def square_kernel(place, panel, right, out, held, strip, sems):
    z = place[0]
    rows, part = panel.shape[1], right.shape[0] // 4
    copies = [pltpu.make_async_copy(right, strip, sems.at[4])]
    for d in range(4):
        columns = held.at[:, d * rows : (d + 1) * rows]
        copies.append(pltpu.make_async_copy(panel.at[d], columns, sems.at[d]))
    for copy in copies:
        copy.start()
    for copy in copies:
        copy.wait()
    for plane, block, e in ((0, 3, 3), (3, 1, 1)):

        @pl.when(z == plane)
        def _(block=block, e=e):
            index = lax.broadcasted_iota(jnp.int32, (part, rows), 0) + place[1] * part
            other = lax.broadcasted_iota(jnp.int32, (part, rows), 1)
            pick = jnp.where(index == other, 1.0, 0.0).astype(jnp.bfloat16)
            far = dot_rows(pick, held[:, block * rows : (block + 1) * rows]).astype(strip.dtype)
            strip[e * part : (e + 1) * part, :rows] += far

    total = dot_rows(held[...], strip[...])
    index = lax.broadcasted_iota(jnp.int32, (rows, rows), 0)
    other = lax.broadcasted_iota(jnp.int32, (rows, rows), 1)
    unit = jnp.where(index == other, 1.0, 0.0).astype(jnp.bfloat16)
    out[...] = (coef_b * dot_rows(unit, strip[:, :rows]) + coef_c * total).astype(out.dtype)


def square(place, panel, right):
    rows, depth = panel.shape[1], right.shape[0]
    outside = pl.BlockSpec(memory_space=pl.ANY)
    return pl.pallas_call(
        square_kernel,
        out_shape=jax.ShapeDtypeStruct((rows, depth), jnp.bfloat16),
        in_specs=[scalars(), outside, outside],
        out_specs=whole(),
        scratch_shapes=[
            pltpu.VMEM((rows, 4 * rows), jnp.bfloat16),
            pltpu.VMEM((depth, 4 * rows), jnp.bfloat16),
            pltpu.SemaphoreType.DMA((5,)),
        ],
        compiler_params=pltpu.CompilerParams(vmem_limit_bytes=56 * 2**20),
        cost_estimate=pl.CostEstimate(
            flops=2 * rows * rows * 4 * depth, bytes_accessed=2 * 5 * rows * rows, transcendentals=0
        ),
    )(place, panel, right)


def product_kernel(marks, ready, place, f, x, *rest):
    l1, r1, across, *rest = rest
    far = rest[: len(marks) - 1]
    rest = rest[len(marks) - 1 + ready :]
    out, whole_f, wide, sems = (rest[0], *rest[-4:-1])
    z = place[0]
    n_col, part, _ = x.shape
    rows, depth = n_col * part, 4 * part
    width = out.shape[1]
    n_tile = (marks[-1] - marks[0]) // width
    step = pl.program_id(0)

    def copy(source, begin, slot, d):
        return pltpu.make_async_copy(
            source.at[:, :, pl.ds(pl.multiple_of(begin, width), width)],
            wide.at[slot, :, pl.ds(d * part, part), :],
            sems.at[slot, d],
        )

    def fetch(tile, slot):
        begin = marks[0] + tile * width
        copy(x, begin, slot, 0).start()
        copy(across, tile * width, slot, 2).start()
        for d, usual, edge in ((1, l1, 3), (3, r1, 0)):

            @pl.when(z != edge)
            def _(d=d, usual=usual):
                copy(usual, tile * width, slot, d).start()

            for piece, low, high in zip(far, marks, marks[1:]):
                inside = jnp.logical_and(begin >= low, begin < high)

                @pl.when(jnp.logical_and(z == edge, inside))
                def _(d=d, piece=piece, low=low):
                    copy(piece, begin - low, slot, d).start()

    slot = lax.rem(step, 2)
    if ready:
        f_sems = rest[-1]
        loads = [pltpu.make_async_copy(f, whole_f, f_sems.at[0])]
    else:
        held_f, f_sems = rest[2], rest[-1]
        loads = [pltpu.make_async_copy(f.at[c], held_f.at[c], f_sems.at[c]) for c in range(n_col)]
        save = pltpu.make_async_copy(whole_f, rest[1], f_sems.at[n_col])

    @pl.when(step == 0)
    def _():
        for one in loads:
            one.start()
        fetch(0, 0)
        if ready:
            loads[0].wait()
        else:
            for c in range(n_col):
                loads[c].wait()
                whole_f[:, c * depth : (c + 1) * depth] = held_f[c]
            save.start()

    @pl.when(step + 1 < n_tile)
    def _():
        fetch(step + 1, 1 - slot)

    for d in range(4):
        copy(x, 0, slot, d).wait()
    total = jnp.dot(
        whole_f[...],
        wide[slot].reshape(n_col * depth, width),
        preferred_element_type=jnp.float32,
    )
    own = wide[slot, :, :part, :].reshape(rows, width).astype(jnp.float32)
    out[...] = (math.sqrt(N) * (coef_a * own + total)).astype(out.dtype)
    if not ready:

        @pl.when(step == n_tile - 1)
        def _():
            save.wait()


def product(place, f, x, near, far, tile, marks, before):
    rows, columns = x.shape
    share = marks[-1] - marks[0]
    ready = before is not None
    n_col = N // columns
    part = rows // n_col
    depth = 4 * part

    def split(value):
        return value.reshape(n_col, part, value.shape[1])

    outside = pl.BlockSpec(memory_space=pl.ANY)
    operands = [place, f, *(split(value) for value in (x, *near, *far))]
    aliases = {}
    out_shape = [jax.ShapeDtypeStruct((rows, columns), jnp.bfloat16)]
    out_specs = [pl.BlockSpec((rows, tile), lambda i: (0, i + marks[0] // tile))]
    scratch = [
        pltpu.VMEM((rows, n_col * depth), jnp.bfloat16),
        pltpu.VMEM((2, n_col, depth, tile), jnp.bfloat16),
        pltpu.SemaphoreType.DMA((2, 4)),
        pltpu.SemaphoreType.DMA((n_col + 1,)),
    ]
    if ready:
        aliases = {len(operands): 0}
        operands.append(before)
    else:
        out_shape.append(jax.ShapeDtypeStruct((rows, n_col * depth), jnp.bfloat16))
        out_specs.append(outside)
        scratch = [pltpu.VMEM(f.shape, jnp.bfloat16), *scratch]
    return pl.pallas_call(
        functools.partial(product_kernel, tuple(marks), ready),
        grid=(share // tile,),
        out_shape=out_shape,
        in_specs=[scalars()] + [outside] * (len(operands) - 1),
        out_specs=out_specs,
        scratch_shapes=scratch,
        input_output_aliases=aliases,
        compiler_params=pltpu.CompilerParams(vmem_limit_bytes=56 * 2**20),
        cost_estimate=pl.CostEstimate(
            flops=2 * rows * n_col * depth * share if ready else 0,
            bytes_accessed=2 * 6 * rows * share if ready else 0,
            transcendentals=0,
        ),
    )(*operands)


def arrived_kernel(*refs):
    pass


def arrived(*values):
    outside = pl.BlockSpec(memory_space=pl.ANY)
    return pl.pallas_call(
        arrived_kernel,
        out_shape=[jax.ShapeDtypeStruct(value.shape, value.dtype) for value in values],
        in_specs=[outside] * len(values),
        out_specs=[outside] * len(values),
        input_output_aliases={i: i for i in range(len(values))},
        cost_estimate=pl.CostEstimate(flops=2 * 10**11, bytes_accessed=0, transcendentals=0),
    )(*values)


def per_device_line(n_col, x):
    z = lax.axis_index("row")
    place = jnp.stack([z, lax.axis_index("col")]).astype(jnp.int32)
    right, left = [(0, 1), (1, 2), (2, 3)], [(3, 2), (2, 1), (1, 0)]

    def send(value, pairs):
        return lax.ppermute(value, "row", pairs)

    def scatter(blocks):
        return lax.psum_scatter(blocks, "col", scatter_dimension=1, tiled=True)

    marks = [0, x.shape[1] - 768, x.shape[1]]
    xs = [x[:, low:high] for low, high in zip(marks, marks[1:])]
    r1 = [send(piece, right) for piece in xs]
    l1 = [send(piece, left) for piece in xs]
    own = scatter(dot_rows(x, x).astype(jnp.bfloat16)[None])
    own, r1[0], l1[0] = lax.optimization_barrier((own, r1[0], l1[0]))
    r2, l2 = [send(r1[0], right[1:])], [send(l1[0], left[1:])]

    part = near_first(x, l1[0], r1[0])
    part, r1[1], l1[1] = lax.optimization_barrier((part, r1[1], l1[1]))
    r1[1], l1[1] = arrived(r1[1], l1[1])
    r2.append(send(r1[1], right[1:]))
    l2.append(send(l1[1], left[1:]))
    first = scatter(near_rest(x, l1[1], r1[1], part))

    across = [l2[0] + r2[0]]
    far_marks = [0, 512, *marks[1:]]
    head = across[0][:, :512]
    part = corner_block(place, l1[0], r1[0], l2[0], r2[0])
    part, head, across[0], l2[1], r2[1] = lax.optimization_barrier(
        (part, head, across[0], l2[1], r2[1])
    )
    across.append(l2[1] + r2[1])

    def send_on(value, *after):
        return send(lax.optimization_barrier((value, *after))[0], [(1, 0), (2, 3)])

    corner = corner_block(place, l1[1], r1[1], l2[1], r2[1], part)
    corner, first = lax.optimization_barrier((corner, first))
    shares = lax.all_to_all(corner.reshape(n_col, -1, corner.shape[2]), "col", 0, 0)
    corner = shares.astype(jnp.float32).sum(0, keepdims=True).astype(jnp.bfloat16)

    far = [send_on(head)]
    second = send(first[2], left[1:]) + send(first[3], right[1:])
    second, far[0] = lax.optimization_barrier((second, far[0]))
    tile = jnp.stack([own[0], first[0], second, first[1]])
    tr1, tl1 = send(tile, right), send(tile, left)

    end = send(corner, [(1, 0), (2, 3)])
    pair = send(corner, [(1, 2), (2, 1)])
    end, tr1, tl1, across[1] = lax.optimization_barrier((end, tr1, tl1, across[1]))
    zero = jnp.zeros_like(end)
    added = [zero, jnp.where(z == 3, end, zero), zero, jnp.where(z == 0, end, zero)]
    panel = lax.all_gather(tile + jnp.concatenate(added), "col", axis=1, tiled=True)

    tr2, tl2 = send(tr1, right[1:]), send(tl1, left[1:])
    tr3, tl3 = send(tr2, right[2:]), send(tl2, left[2:])
    far += arrived(send_on(across[0][:, 512:], tr3, tl3, pair))

    strip = strips(place, tile, tl1, tr3, tl2, tr2, tr1, tl3, corner, pair, end)
    factor = square(place, panel, strip)
    far.append(send_on(across[1], factor))
    factor = lax.all_gather(factor, "col", axis=0, tiled=False)
    near = [l1, r1, across]
    out, factor = product(
        place, factor, x, [group[0] for group in near], far[:2], 256, far_marks[:3], None
    )
    (out,) = product(place, factor, x, [group[1] for group in near], far[2:], 256, marks[1:], out)
    return out


def solution(mesh):
    n_row, n_col = mesh.shape["row"], mesh.shape["col"]

    def body(iterate):
        if (n_row, n_col) == (4, 8) and iterate.shape == (896, 2304):
            return per_device_line(n_col, iterate)
        return per_device(iterate)

    return jax.shard_map(
        body,
        mesh=mesh,
        in_specs=(P("row", "col"),),
        out_specs=P("row", "col"),
        check_vma=False,
    )
```

```python
import functools
import math

import jax
import jax.numpy as jnp
from jax import lax
from jax.experimental import pallas as pl
from jax.experimental.pallas import tpu as pltpu
from jax.sharding import PartitionSpec as P

N = 18432


coef_a = 3.4445
coef_b = -4.775
coef_c = 2.0315


def dot_rows(left, right):
    return lax.dot_general(
        left, right, (((1,), (1,)), ((), ())), preferred_element_type=jnp.float32
    )


def per_device(iterate):
    contract = (((1,), (1,)), ((), ()))
    gathered = lax.all_gather(iterate, "row", axis=0, tiled=True)
    partial_value = lax.dot_general(
        iterate, gathered, contract, preferred_element_type=jnp.float32
    )
    partial_value = partial_value.astype(jnp.bfloat16)
    gram_tile = lax.psum_scatter(partial_value, "col", scatter_dimension=1, tiled=True)
    gram_panel = lax.all_gather(gram_tile, "col", axis=1, tiled=True)
    squared = jnp.dot(
        gram_panel,
        lax.all_gather(gram_tile, "row", axis=0, tiled=True),
        preferred_element_type=jnp.float32,
    )
    factor = (coef_b * gram_tile.astype(jnp.float32) + coef_c * squared).astype(jnp.bfloat16)
    factor_panel = lax.all_gather(factor, "col", axis=1, tiled=True)
    product = jnp.dot(factor_panel, gathered, preferred_element_type=jnp.float32)
    result = coef_a * iterate.astype(jnp.float32) + product
    return (math.sqrt(N) * result).astype(jnp.bfloat16)


def whole():
    return pl.BlockSpec(memory_space=pltpu.VMEM)


def scalars():
    return pl.BlockSpec(memory_space=pltpu.SMEM)


def load_near(begin, x, l1, r1, held, sems):
    rows, width = l1.shape
    sources = (r1, x.at[:, begin : begin + width], l1)
    copies = [
        pltpu.make_async_copy(source, held.at[g * rows : (g + 1) * rows], sems.at[g])
        for g, source in enumerate(sources)
    ]
    for copy in copies:
        copy.start()
    for copy in copies:
        copy.wait()


def near_first_kernel(x, l1, r1, out, held, sems):
    rows = x.shape[0]
    load_near(0, x, l1, r1, held, sems)
    out[0] = dot_rows(held[: 2 * rows], held[2 * rows :])
    out[1] = dot_rows(held[rows:], held[:rows])


def near_rest_kernel(begin, x, l1, r1, part, out, held, total, sems):
    rows = x.shape[0]
    copies = [pltpu.make_async_copy(part.at[g], total.at[g], sems.at[3 + g]) for g in range(2)]
    for copy in copies:
        copy.start()
    load_near(begin, x, l1, r1, held, sems)
    for g, (left, right, above, below) in enumerate(
        (
            (slice(0, 2 * rows), slice(2 * rows, 3 * rows), 2, 0),
            (slice(rows, 3 * rows), slice(0, rows), 1, 3),
        )
    ):
        value = dot_rows(held[left], held[right])
        copies[g].wait()
        value = (value + total[g]).astype(out.dtype)
        out[above] = value[:rows]
        out[below] = value[rows:]


def near_call(kernel, shape, dtype, operands, scratch, share):
    rows, width = operands[1].shape
    return pl.pallas_call(
        kernel,
        out_shape=jax.ShapeDtypeStruct(shape, dtype),
        in_specs=[pl.BlockSpec(memory_space=pl.ANY)] * len(operands),
        out_specs=whole(),
        scratch_shapes=[pltpu.VMEM((3 * rows, width), jnp.bfloat16), *scratch],
        compiler_params=pltpu.CompilerParams(vmem_limit_bytes=56 * 2**20),
        cost_estimate=pl.CostEstimate(
            flops=share * 8 * rows * rows * width,
            bytes_accessed=share * 6 * rows * width,
            transcendentals=0,
        ),
    )(*operands)


def near_first(x, l1, r1):
    rows = x.shape[0]
    sems = pltpu.SemaphoreType.DMA((3,))
    return near_call(near_first_kernel, (2, 2 * rows, rows), jnp.float32, [x, l1, r1], [sems], 0)


def near_rest(x, l1, r1, part):
    rows = x.shape[0]
    kernel = functools.partial(near_rest_kernel, x.shape[1] - l1.shape[1])
    scratch = [pltpu.VMEM(part.shape, jnp.float32), pltpu.SemaphoreType.DMA((5,))]
    return near_call(kernel, (4, rows, rows), jnp.bfloat16, [x, l1, r1, part], scratch, 1)


def corner_kernel(place, l1, r1, l2, r2, *rest):
    *part, out, held, total, sems = rest
    for plane, one, other in ((1, r1, l2), (2, l1, r2)):

        @pl.when(place[0] == plane)
        def _(one=one, other=other):
            copies = [
                pltpu.make_async_copy(one, held.at[0], sems.at[0]),
                pltpu.make_async_copy(other, held.at[1], sems.at[1]),
            ]
            if part:
                copies.append(pltpu.make_async_copy(part[0].at[0], total, sems.at[2]))
            for copy in copies:
                copy.start()
            for copy in copies[:2]:
                copy.wait()
            value = dot_rows(held[0], held[1])
            if part:
                copies[2].wait()
                value = value + total[...]
            out[0] = value.astype(out.dtype)

    @pl.when(jnp.logical_or(place[0] == 0, place[0] == 3))
    def _():
        out[...] = jnp.zeros_like(out)


def corner_block(place, l1, r1, l2, r2, *part):
    rows, width = l1.shape
    operands = [l1, r1, l2, r2, *part]
    return pl.pallas_call(
        corner_kernel,
        out_shape=jax.ShapeDtypeStruct((1, rows, rows), jnp.bfloat16 if part else jnp.float32),
        in_specs=[scalars()] + [pl.BlockSpec(memory_space=pl.ANY)] * len(operands),
        out_specs=whole(),
        scratch_shapes=[
            pltpu.VMEM((2, rows, width), jnp.bfloat16),
            pltpu.VMEM((rows, rows), jnp.float32),
            pltpu.SemaphoreType.DMA((3,)),
        ],
        compiler_params=pltpu.CompilerParams(vmem_limit_bytes=56 * 2**20),
        cost_estimate=pl.CostEstimate(
            flops=256 * rows * rows * width if part else 0,
            bytes_accessed=8 * rows * width if part else 0,
            transcendentals=0,
        ),
    )(place, *operands)


def strips_kernel(place, own, l1, r3, l2, r2, r1, l3, corner, pair, end, out):
    z = place[0]
    _, part, rows = own.shape
    at_end = jnp.logical_or(z == 0, z == 3)
    zero = jnp.zeros_like(end[0])
    near = jnp.where(at_end, end[0], corner[0])
    far = jnp.where(at_end, zero, pair[0])
    low = jnp.where(z < 2, near, far)
    high = jnp.where(z < 2, far, near)
    for e in range(4):
        for block in range(4):
            if e == 0:
                value = own[block]
            else:
                one, other = {1: (l1, r3), 2: (l2, r2), 3: (r1, l3)}[e]
                value = one[block] + other[block]
            if block == 3:
                value = value + jnp.where((z + e) % 4 == 0, low, zero)
            if block == 1:
                value = value + jnp.where((z + e) % 4 == 3, high, zero)
            place_of = (block + e) % 4 * rows
            out[e * part : (e + 1) * part, place_of : place_of + rows] = value


def strips(place, *others):
    _, part, rows = others[0].shape
    return pl.pallas_call(
        strips_kernel,
        out_shape=jax.ShapeDtypeStruct((4 * part, 4 * rows), jnp.bfloat16),
        in_specs=[scalars()] + [whole()] * len(others),
        out_specs=whole(),
        compiler_params=pltpu.CompilerParams(vmem_limit_bytes=24 * 2**20),
        cost_estimate=pl.CostEstimate(
            flops=16 * part * rows, bytes_accessed=2 * 44 * part * rows, transcendentals=0
        ),
    )(place, *others)


def square_kernel(place, panel, right, out, held, strip, sems):
    z = place[0]
    rows, part = panel.shape[1], right.shape[0] // 4
    copies = [pltpu.make_async_copy(right, strip, sems.at[4])]
    for d in range(4):
        columns = held.at[:, d * rows : (d + 1) * rows]
        copies.append(pltpu.make_async_copy(panel.at[d], columns, sems.at[d]))
    for copy in copies:
        copy.start()
    for copy in copies:
        copy.wait()
    for plane, block, e in ((0, 3, 3), (3, 1, 1)):

        @pl.when(z == plane)
        def _(block=block, e=e):
            index = lax.broadcasted_iota(jnp.int32, (part, rows), 0) + place[1] * part
            other = lax.broadcasted_iota(jnp.int32, (part, rows), 1)
            pick = jnp.where(index == other, 1.0, 0.0).astype(jnp.bfloat16)
            far = dot_rows(pick, held[:, block * rows : (block + 1) * rows]).astype(strip.dtype)
            strip[e * part : (e + 1) * part, :rows] += far

    total = dot_rows(held[...], strip[...])
    index = lax.broadcasted_iota(jnp.int32, (rows, rows), 0)
    other = lax.broadcasted_iota(jnp.int32, (rows, rows), 1)
    unit = jnp.where(index == other, 1.0, 0.0).astype(jnp.bfloat16)
    out[...] = (coef_b * dot_rows(unit, strip[:, :rows]) + coef_c * total).astype(out.dtype)


def square(place, panel, right):
    rows, depth = panel.shape[1], right.shape[0]
    outside = pl.BlockSpec(memory_space=pl.ANY)
    return pl.pallas_call(
        square_kernel,
        out_shape=jax.ShapeDtypeStruct((rows, depth), jnp.bfloat16),
        in_specs=[scalars(), outside, outside],
        out_specs=whole(),
        scratch_shapes=[
            pltpu.VMEM((rows, 4 * rows), jnp.bfloat16),
            pltpu.VMEM((depth, 4 * rows), jnp.bfloat16),
            pltpu.SemaphoreType.DMA((5,)),
        ],
        compiler_params=pltpu.CompilerParams(vmem_limit_bytes=56 * 2**20),
        cost_estimate=pl.CostEstimate(
            flops=2 * rows * rows * 4 * depth, bytes_accessed=2 * 5 * rows * rows, transcendentals=0
        ),
    )(place, panel, right)


def product_kernel(marks, ready, place, f, x, *rest):
    l1, r1, across, *rest = rest
    far = rest[: len(marks) - 1]
    rest = rest[len(marks) - 1 + ready :]
    out, whole_f, wide, sems = (rest[0], *rest[-4:-1])
    z = place[0]
    n_col, part, _ = x.shape
    rows, depth = n_col * part, 4 * part
    width = out.shape[1]
    n_tile = (marks[-1] - marks[0]) // width
    step = pl.program_id(0)

    def copy(source, begin, slot, d):
        return pltpu.make_async_copy(
            source.at[:, :, pl.ds(pl.multiple_of(begin, width), width)],
            wide.at[slot, :, pl.ds(d * part, part), :],
            sems.at[slot, d],
        )

    def fetch(tile, slot):
        begin = marks[0] + tile * width
        copy(x, begin, slot, 0).start()
        copy(across, tile * width, slot, 2).start()
        for d, usual, edge in ((1, l1, 3), (3, r1, 0)):

            @pl.when(z != edge)
            def _(d=d, usual=usual):
                copy(usual, tile * width, slot, d).start()

            for piece, low, high in zip(far, marks, marks[1:]):
                inside = jnp.logical_and(begin >= low, begin < high)

                @pl.when(jnp.logical_and(z == edge, inside))
                def _(d=d, piece=piece, low=low):
                    copy(piece, begin - low, slot, d).start()

    slot = lax.rem(step, 2)
    if ready:
        f_sems = rest[-1]
        loads = [pltpu.make_async_copy(f, whole_f, f_sems.at[0])]
    else:
        held_f, f_sems = rest[2], rest[-1]
        loads = [pltpu.make_async_copy(f.at[c], held_f.at[c], f_sems.at[c]) for c in range(n_col)]
        save = pltpu.make_async_copy(whole_f, rest[1], f_sems.at[n_col])

    @pl.when(step == 0)
    def _():
        for one in loads:
            one.start()
        fetch(0, 0)
        if ready:
            loads[0].wait()
        else:
            for c in range(n_col):
                loads[c].wait()
                whole_f[:, c * depth : (c + 1) * depth] = held_f[c]
            save.start()

    @pl.when(step + 1 < n_tile)
    def _():
        fetch(step + 1, 1 - slot)

    for d in range(4):
        copy(x, 0, slot, d).wait()
    total = jnp.dot(
        whole_f[...],
        wide[slot].reshape(n_col * depth, width),
        preferred_element_type=jnp.float32,
    )
    own = wide[slot, :, :part, :].reshape(rows, width).astype(jnp.float32)
    out[...] = (math.sqrt(N) * (coef_a * own + total)).astype(out.dtype)
    if not ready:

        @pl.when(step == n_tile - 1)
        def _():
            save.wait()


def product(place, f, x, near, far, tile, marks, before):
    rows, columns = x.shape
    share = marks[-1] - marks[0]
    ready = before is not None
    n_col = N // columns
    part = rows // n_col
    depth = 4 * part

    def split(value):
        return value.reshape(n_col, part, value.shape[1])

    outside = pl.BlockSpec(memory_space=pl.ANY)
    operands = [place, f, *(split(value) for value in (x, *near, *far))]
    aliases = {}
    out_shape = [jax.ShapeDtypeStruct((rows, columns), jnp.bfloat16)]
    out_specs = [pl.BlockSpec((rows, tile), lambda i: (0, i + marks[0] // tile))]
    scratch = [
        pltpu.VMEM((rows, n_col * depth), jnp.bfloat16),
        pltpu.VMEM((2, n_col, depth, tile), jnp.bfloat16),
        pltpu.SemaphoreType.DMA((2, 4)),
        pltpu.SemaphoreType.DMA((n_col + 1,)),
    ]
    if ready:
        aliases = {len(operands): 0}
        operands.append(before)
    else:
        out_shape.append(jax.ShapeDtypeStruct((rows, n_col * depth), jnp.bfloat16))
        out_specs.append(outside)
        scratch = [pltpu.VMEM(f.shape, jnp.bfloat16), *scratch]
    return pl.pallas_call(
        functools.partial(product_kernel, tuple(marks), ready),
        grid=(share // tile,),
        out_shape=out_shape,
        in_specs=[scalars()] + [outside] * (len(operands) - 1),
        out_specs=out_specs,
        scratch_shapes=scratch,
        input_output_aliases=aliases,
        compiler_params=pltpu.CompilerParams(vmem_limit_bytes=56 * 2**20),
        cost_estimate=pl.CostEstimate(
            flops=2 * rows * n_col * depth * share if ready else 0,
            bytes_accessed=2 * 6 * rows * share if ready else 0,
            transcendentals=0,
        ),
    )(*operands)


def arrived_kernel(*refs):
    pass


def arrived(*values):
    outside = pl.BlockSpec(memory_space=pl.ANY)
    return pl.pallas_call(
        arrived_kernel,
        out_shape=[jax.ShapeDtypeStruct(value.shape, value.dtype) for value in values],
        in_specs=[outside] * len(values),
        out_specs=[outside] * len(values),
        input_output_aliases={i: i for i in range(len(values))},
        cost_estimate=pl.CostEstimate(flops=2 * 10**11, bytes_accessed=0, transcendentals=0),
    )(*values)


def per_device_line(n_col, x):
    z = lax.axis_index("row")
    place = jnp.stack([z, lax.axis_index("col")]).astype(jnp.int32)
    right, left = [(0, 1), (1, 2), (2, 3)], [(3, 2), (2, 1), (1, 0)]

    def send(value, pairs):
        return lax.ppermute(value, "row", pairs)

    def scatter(blocks):
        return lax.psum_scatter(blocks, "col", scatter_dimension=1, tiled=True)

    marks = [0, x.shape[1] - 768, x.shape[1]]
    xs = [x[:, low:high] for low, high in zip(marks, marks[1:])]
    r1 = [send(piece, right) for piece in xs]
    l1 = [send(piece, left) for piece in xs]
    own = scatter(dot_rows(x, x).astype(jnp.bfloat16)[None])
    own, r1[0], l1[0] = lax.optimization_barrier((own, r1[0], l1[0]))
    r2, l2 = [send(r1[0], right[1:])], [send(l1[0], left[1:])]

    part = near_first(x, l1[0], r1[0])
    part, r1[1], l1[1] = lax.optimization_barrier((part, r1[1], l1[1]))
    r1[1], l1[1] = arrived(r1[1], l1[1])
    r2.append(send(r1[1], right[1:]))
    l2.append(send(l1[1], left[1:]))
    first = scatter(near_rest(x, l1[1], r1[1], part))

    across = [l2[0] + r2[0]]
    far_marks = [0, 256, *marks[1:]]
    head = across[0][:, :256]
    part = corner_block(place, l1[0], r1[0], l2[0], r2[0])
    part, head, across[0], l2[1], r2[1] = lax.optimization_barrier(
        (part, head, across[0], l2[1], r2[1])
    )
    across.append(l2[1] + r2[1])

    def send_on(value, *after):
        return send(lax.optimization_barrier((value, *after))[0], [(1, 0), (2, 3)])

    corner = corner_block(place, l1[1], r1[1], l2[1], r2[1], part)
    corner, first = lax.optimization_barrier((corner, first))
    shares = lax.all_to_all(corner.reshape(n_col, -1, corner.shape[2]), "col", 0, 0)
    corner = shares.astype(jnp.float32).sum(0, keepdims=True).astype(jnp.bfloat16)

    far = [send_on(head)]
    second = send(first[2], left[1:]) + send(first[3], right[1:])
    second, far[0] = lax.optimization_barrier((second, far[0]))
    tile = jnp.stack([own[0], first[0], second, first[1]])
    tr1, tl1 = send(tile, right), send(tile, left)

    end = send(corner, [(1, 0), (2, 3)])
    pair = send(corner, [(1, 2), (2, 1)])
    end, tr1, tl1, across[1] = lax.optimization_barrier((end, tr1, tl1, across[1]))
    zero = jnp.zeros_like(end)
    added = [zero, jnp.where(z == 3, end, zero), zero, jnp.where(z == 0, end, zero)]
    panel = lax.all_gather(tile + jnp.concatenate(added), "col", axis=1, tiled=True)

    tr2, tl2 = send(tr1, right[1:]), send(tl1, left[1:])
    tr3, tl3 = send(tr2, right[2:]), send(tl2, left[2:])
    far += arrived(send_on(across[0][:, 256:], tr3, tl3, pair))

    strip = strips(place, tile, tl1, tr3, tl2, tr2, tr1, tl3, corner, pair, end)
    factor = square(place, panel, strip)
    far.append(send_on(across[1], factor))
    factor = lax.all_gather(factor, "col", axis=0, tiled=False)
    near = [l1, r1, across]
    out, factor = product(
        place, factor, x, [group[0] for group in near], far[:2], 256, far_marks[:3], None
    )
    (out,) = product(place, factor, x, [group[1] for group in near], far[2:], 256, marks[1:], out)
    return out


def solution(mesh):
    n_row, n_col = mesh.shape["row"], mesh.shape["col"]

    def body(iterate):
        if (n_row, n_col) == (4, 8) and iterate.shape == (896, 2304):
            return per_device_line(n_col, iterate)
        return per_device(iterate)

    return jax.shard_map(
        body,
        mesh=mesh,
        in_specs=(P("row", "col"),),
        out_specs=P("row", "col"),
        check_vma=False,
    )
```
